32 devices in a mesh: dp: 8 (over z, y), zero: 4 (over x, core).
Axes of the slice: x: 2, y: 2, z: 4, core: 2. Of those that a mesh axis runs over, the one named last changes fastest.
Arguments:
- nodes: float32 [65536, 128], P(('dp', 'zero')), may hold values from -6 to 6
- cotangent: float32 [65536, 128], P(('dp', 'zero')), may hold values from -6 to 6
- lengths: int32 [128], P(('dp', 'zero')), may hold values from 256 to 512, as said below
- w_query: float32 [2, 128, 128], P(None, 'zero'), may hold values from -0.5 to 0.5
- w_key: float32 [2, 128, 128], P(None, 'zero'), may hold values from -0.5 to 0.5
- w_value: float32 [2, 128, 128], P(None, 'zero'), may hold values from -0.5 to 0.5
- w_out: float32 [2, 128, 128], P(None, 'zero'), may hold values from -1 to 1
- b_query: float32 [2, 128], P(None, 'zero'), may hold values from -2 to 2
- b_key: float32 [2, 128], P(None, 'zero'), may hold values from -2 to 2
- b_value: float32 [2, 128], P(None, 'zero'), may hold values from -2 to 2
- b_out: float32 [2, 128], P(None, 'zero'), may hold values from -2 to 2
- gain_key: float32 [2, 128], P(None, 'zero'), may hold values from 0.5 to 1.5
- shift_key: float32 [2, 128], P(None, 'zero'), may hold values from -2 to 2
- gain_value: float32 [2, 128], P(None, 'zero'), may hold values from 0.5 to 1.5
- shift_value: float32 [2, 128], P(None, 'zero'), may hold values from -2 to 2
- w_up: float32 [2, 128, 256], P(None, 'zero'), may hold values from -0.5 to 0.5
- b_up: float32 [2, 256], P(None, 'zero'), may hold values from -2 to 2
- w_down: float32 [2, 256, 128], P(None, 'zero'), may hold values from -0.375 to 0.375
- b_down: float32 [2, 128], P(None, 'zero'), may hold values from -2 to 2
Outputs:
- output: float32 [65536, 128], P(('dp', 'zero'))
- grad_nodes: float32 [65536, 128], P(('dp', 'zero'))
- grad_w_query: float32 [2, 128, 128], P(None, 'zero')
- grad_w_key: float32 [2, 128, 128], P(None, 'zero')
- grad_w_value: float32 [2, 128, 128], P(None, 'zero')
- grad_w_out: float32 [2, 128, 128], P(None, 'zero')
- grad_b_query: float32 [2, 128], P(None, 'zero')
- grad_b_key: float32 [2, 128], P(None, 'zero')
- grad_b_value: float32 [2, 128], P(None, 'zero')
- grad_b_out: float32 [2, 128], P(None, 'zero')
- grad_gain_key: float32 [2, 128], P(None, 'zero')
- grad_shift_key: float32 [2, 128], P(None, 'zero')
- grad_gain_value: float32 [2, 128], P(None, 'zero')
- grad_shift_value: float32 [2, 128], P(None, 'zero')
- grad_w_up: float32 [2, 128, 256], P(None, 'zero')
- grad_b_up: float32 [2, 256], P(None, 'zero')
- grad_w_down: float32 [2, 256, 128], P(None, 'zero')
- grad_b_down: float32 [2, 128], P(None, 'zero')
The draws below stay inside these ranges and needn't reach their ends.
Inputs may be any that keep to these rules, and one draw needn't show every extreme that they name: Each device's 4 lengths sum to at most 2048, and one of them is exactly 512.
All inputs are finite; a program needn't handle non-finite values.
Results may differ from the reference program's by a relative error of at most 0.0003.
Values sent between devices are 32-bit elements; how exact they have to be, the bound alone decides.
A program may use at most 128 MiB of HBM per device.

```python
import jax
import jax.numpy as jnp
from jax import lax

D = 128
HEADS = 4
HDIM = 32
FF = 256
LAYERS = 2
TOK_DEV = 2048
SEGS = 4
MAXLEN = 512
MINLEN = 256
TOKENS = 65536
MESHES = 128


def draw_lengths(key, part):
    key = jax.random.fold_in(key, 7)
    groups = MESHES // SEGS
    base = jax.random.randint(key, (groups, SEGS), MINLEN, MAXLEN + 1)
    picked = jax.random.randint(jax.random.fold_in(key, 1), (groups, 1), 0, SEGS)
    column = jnp.arange(SEGS, dtype=jnp.int32)[None, :]
    return jnp.where(column == picked, MAXLEN, base).reshape(-1).astype(jnp.int32)


def steps_of(own_key, shape, pieces, smallest, largest):
    loudness, own = 1.0, jax.random.fold_in(own_key, 6)
    for dim, shards_of in pieces:
        heights = jnp.exp(jax.random.uniform(jax.random.fold_in(own, dim), (shards_of,), jnp.float32, smallest / len(pieces), largest / len(pieces)))
        loudness = loudness * jnp.repeat(heights, shape[dim] // shards_of).reshape([-1 if axis == dim else 1 for axis in range(len(shape))])
    return loudness


def gaussian(key, dims, width, limit, shards=(), kind=jnp.bfloat16):
    array = jax.random.normal(key, dims, jnp.float32) * width
    if len(shards) > 0:
        array = steps_of(key, dims, shards, -0.22, 0.18) * array
    return jnp.clip(array, min=-limit, max=limit).astype(kind)


def setup_inputs(seed: int = 0) -> dict:
    key_list = jax.random.split(jax.random.key(seed), 20)
    return {
        "nodes": gaussian(key_list[0], (TOKENS, D), 1.0, 6.0, ((0, 32),), jnp.float32),
        "cotangent": gaussian(key_list[1], (TOKENS, D), 1.0, 6.0, ((0, 32),), jnp.float32),
        "lengths": draw_lengths(jax.random.fold_in(key_list[19], 71), 0),
        "w_query": gaussian(key_list[3], (LAYERS, D, D), D ** -0.5, 0.5, ((1, 4),), jnp.float32),
        "w_key": gaussian(key_list[4], (LAYERS, D, D), D ** -0.5, 0.5, ((1, 4),), jnp.float32),
        "w_value": gaussian(key_list[5], (LAYERS, D, D), D ** -0.5, 0.5, ((1, 4),), jnp.float32),
        "w_out": gaussian(key_list[6], (LAYERS, D, D), HDIM ** -0.5, 1.0, ((1, 4),), jnp.float32),
        "b_query": gaussian(key_list[7], (LAYERS, D), 0.3, 2.0, ((1, 4),), jnp.float32),
        "b_key": gaussian(key_list[8], (LAYERS, D), 0.3, 2.0, ((1, 4),), jnp.float32),
        "b_value": gaussian(key_list[9], (LAYERS, D), 0.3, 2.0, ((1, 4),), jnp.float32),
        "b_out": gaussian(key_list[10], (LAYERS, D), 0.3, 2.0, ((1, 4),), jnp.float32),
        "gain_key": jnp.clip(1.0 + 0.1 * jax.random.normal(key_list[11], (LAYERS, D), jnp.float32), 0.5, 1.5),
        "shift_key": gaussian(key_list[12], (LAYERS, D), 0.3, 2.0, ((1, 4),), jnp.float32),
        "gain_value": jnp.clip(1.0 + 0.1 * jax.random.normal(key_list[13], (LAYERS, D), jnp.float32), 0.5, 1.5),
        "shift_value": gaussian(key_list[14], (LAYERS, D), 0.3, 2.0, ((1, 4),), jnp.float32),
        "w_up": gaussian(key_list[15], (LAYERS, D, FF), D ** -0.5, 0.5, ((1, 4),), jnp.float32),
        "b_up": gaussian(key_list[16], (LAYERS, FF), 0.3, 2.0, ((1, 4),), jnp.float32),
        "w_down": gaussian(key_list[17], (LAYERS, FF, D), FF ** -0.5, 0.375, ((1, 4),), jnp.float32),
        "b_down": gaussian(key_list[18], (LAYERS, D), 0.3, 2.0, ((1, 4),), jnp.float32),
    }


@jax.custom_vjp
def low(v):
    return lax.optimization_barrier(v.astype(jnp.bfloat16)).astype(jnp.float32)

@jax.custom_vjp
def low_back(v):
    return v

def low_keep(v):
    return (low(v), None)

def low_pass(kept, grad):
    return (grad,)

def back_keep(v):
    return (v, None)

def back_low(kept, grad):
    return (low(grad),)
low.defvjp(low_keep, low_pass)
low_back.defvjp(back_keep, back_low)

def product(left, right):
    return jnp.dot(left, right, precision=lax.Precision.HIGHEST)

def segment_tables(lengths, rows):
    ends = jnp.cumsum(lengths).astype(jnp.int32)
    starts = (ends - lengths).astype(jnp.int32)
    places = jnp.arange(rows, dtype=jnp.int32)[:, None]
    member = jnp.logical_and(places >= starts[None, :], places < ends[None, :]).astype(jnp.float32)
    live_rows = lax.optimization_barrier(jnp.sum(member, axis=1, keepdims=True))
    scaled = member / lengths.astype(jnp.float32)[None, :]
    return (member, scaled, live_rows)

def head_norm(values, gain, shift):
    rows = values.shape[0]
    split = values.reshape(rows, HEADS, -1)
    centred = split - lax.optimization_barrier(jnp.mean(split, axis=2, keepdims=True))
    spread = lax.optimization_barrier(jnp.mean(centred * centred, axis=2, keepdims=True))
    return (centred * lax.rsqrt(spread + 1e-05)).reshape(rows, -1) * gain + shift

def apply_layer(inputs, params, member, scaled, live_rows):
    w_query, w_key, w_value, w_out, b_query, b_key, b_value, b_out, gain_key, shift_key, gain_value, shift_value, w_up, b_up, w_down, b_down = params
    rows = inputs.shape[0]
    query = (product(inputs, w_query) + b_query).reshape(rows, HEADS, -1)
    keys = head_norm(product(inputs, w_key) + b_key, gain_key, shift_key).reshape(rows, HEADS, -1)
    values = head_norm(product(inputs, w_value) + b_value, gain_value, shift_value).reshape(rows, HEADS, -1)
    summary = jnp.einsum('ts,thk,thv->shkv', scaled, keys, values, precision=lax.Precision.HIGHEST)
    mixed = jnp.einsum('ts,thk,shkv->thv', member, query, summary, precision=lax.Precision.HIGHEST).reshape(rows, -1)
    middle = inputs + live_rows * (product(mixed, w_out) + b_out)
    hidden = jax.nn.gelu(product(middle, w_up) + b_up)
    return middle + live_rows * (product(hidden, w_down) + b_down)

def reference(nodes, cotangent, lengths, w_query, w_key, w_value, w_out, b_query, b_key, b_value, b_out, gain_key, shift_key, gain_value, shift_value, w_up, b_up, w_down, b_down):
    params = (w_query, w_key, w_value, w_out, b_query, b_key, b_value, b_out, gain_key, shift_key, gain_value, shift_value, w_up, b_up, w_down, b_down)
    blocks = nodes.shape[0] // TOK_DEV
    node_blocks = nodes.reshape(blocks, TOK_DEV, D)
    grad_blocks = cotangent.reshape(blocks, TOK_DEV, D)
    length_blocks = lengths.reshape(blocks, SEGS)

    def forward(inputs, weights, block_lengths):
        member, scaled, live_rows = segment_tables(block_lengths, inputs.shape[0])
        state = inputs
        for level in range(LAYERS):
            state = apply_layer(state, tuple((p[level] for p in weights)), member, scaled, live_rows)
        return state

    def visit(totals, item):
        inputs, incoming, block_lengths = item
        result, pull = jax.vjp(lambda a, w: forward(a, w, block_lengths), inputs, params)
        grad_in, grad_params = pull(incoming)
        return (jax.tree.map(jnp.add, totals, grad_params), (result, grad_in))
    zeros = tuple((jnp.zeros_like(p) for p in params))
    grads, (results, grad_ins) = lax.scan(visit, zeros, (node_blocks, grad_blocks, length_blocks))
    return (results.reshape(-1, D), grad_ins.reshape(-1, D), grads[0], grads[1], grads[2], grads[3], grads[4], grads[5], grads[6], grads[7], grads[8], grads[9], grads[10], grads[11], grads[12], grads[13], grads[14], grads[15])
```

```python
import jax
import jax.numpy as jnp
from jax import lax
from jax.experimental import pallas as pl
from jax.experimental.pallas import tpu as pltpu
from jax.sharding import PartitionSpec as P

D=128; FF=256; SEGS=4; BLK=512; TOK=2048; HD=32
F32=jnp.float32; BF=jnp.bfloat16
VM=pltpu.VMEM

def split(x):
    hi=x.astype(BF); lo=(x-hi.astype(F32)).astype(BF)
    return hi,lo
def pack(x):
    return jnp.concatenate(split(x),axis=1)
def quad(x):
    p=pack(x)
    return jnp.concatenate([p,p],axis=0)
def mm(a,b):
    return jnp.dot(a,b,preferred_element_type=F32)
def tn(a,b):
    return lax.dot_general(a,b,(((0,),(0,)),((),())),preferred_element_type=F32)
def halves(r):
    n=r.shape[1]//2
    return r[:,:n]+r[:,n:]
def quads(r):
    m=r.shape[0]//2
    return halves(r[:m]+r[m:])
def prod(a,b):
    return halves(mm(pack(a),quad(b)))
def part(x):
    return jnp.sum(x.reshape(x.shape[0]//8,8,x.shape[1]),axis=0)

def group_mask():
    r=lax.broadcasted_iota(jnp.int32,(D,D),0)//HD
    c=lax.broadcasted_iota(jnp.int32,(D,D),1)//HD
    return r==c

BQ,BK,BV,BO,GK,SK,GV,SV,BD,BU0,BU1=range(11)

LAYER_SCRATCH=dict(
    X=((TOK,2*D),BF), H=((TOK,D),F32), NK=((TOK,D),F32), NV=((TOK,D),F32), RK=((TOK,D),F32), RV=((TOK,D),F32),
    KN=((TOK,2*D),BF), VN=((TOK,2*D),BF), MD=((TOK,2*D),BF), ACT=((TOK,2*FF),BF), DG=((TOK,FF),F32),
    WKV=((2*D,4*D),BF), WUP=((2*D,2*FF),BF), WDN=((2*FF,2*D),BF), WDNT=((2*D,2*FF),BF), WUPT=((2*FF,2*D),BF),
    WKVT=((4*D,2*D),BF), WO2=((2*D,2*D),BF), WOT2=((2*D,2*D),BF), WQL=((D,2*D),BF), WQTL=((D,2*D),BF),
    S=((SEGS,D,D),F32), T=((SEGS,D,D),F32), UT2=((SEGS,2*D,2*D),BF), U2=((SEGS,2*D,2*D),BF), UB=((SEGS,8,D),F32),
    CB=((8,D),F32),
)
TMP_SCRATCH=dict(
    E=((TOK,D),F32), ED=((TOK,2*D),BF), EP=((TOK,2*FF),BF), EM=((TOK,D),F32), EO=((TOK,2*D),BF), FKV=((TOK,4*D),BF),
    A2=((2*D,D),BF),
)

def prep_kv(L,w,vec,A2):
    a1=A2[0:D,:]
    b=vec[BK:BV+1,:]
    b8=jnp.concatenate([b,jnp.zeros((6,D),F32)],axis=0)
    L['CB'][...]=center(b8,a1)
    wk=center(w['k'][...],a1); wv=center(w['v'][...],a1)
    kh,kl=split(wk); vh,vl=split(wv)
    kv=jnp.concatenate([kh,vh,kl,vl],axis=1)
    L['WKV'][0:D,:]=kv; L['WKV'][D:,:]=kv
    L['WKVT'][0:2*D,:]=quad(wk.T); L['WKVT'][2*D:,:]=quad(wv.T)

def prep_qo(L,w):
    wo=w['o'][...]
    L['WO2'][...]=quad(wo); L['WOT2'][...]=quad(wo.T)
    wq=w['q'][...]
    L['WQL'][...]=pack(wq); L['WQTL'][...]=pack(wq.T)

def prep_ff(L,w):
    L['WUP'][...]=quad(w['up'][...])
    L['WDN'][...]=quad(w['dn'][...])

def prep_back(L,w):
    L['WUPT'][...]=quad(w['up'][...].T)
    L['WDNT'][...]=quad(w['dn'][...].T)

def fwd_a(L,vec,A2,live,r0,n):
    rows=pl.ds(r0,n)
    x=pack(L['H'][rows,:])
    L['X'][rows,:]=x
    r=mm(x,L['WKV'][...])
    a2=A2[...]
    lv=live(r0,n)
    for i,(N,R,O,g,s) in enumerate((('NK','RK','KN',GK,SK),('NV','RV','VN',GV,SV))):
        c=r[:,i*D:(i+1)*D]+r[:,(i+2)*D:(i+3)*D]+L['CB'][i:i+1,:]
        rs=lax.rsqrt(mm(pack(c*c),a2)+1e-5)
        nn=c*rs
        L[R][rows,:]=rs; L[N][rows,:]=nn
        y=jnp.where(lv,nn*vec[g:g+1,:]+vec[s:s+1,:],0.0)
        L[O][rows,:]=pack(y)

def fwd_s(L,vec,gm,s,inv):
    rows=pl.ds(s*BLK,BLK)
    S=jnp.where(gm,quads(tn(L['KN'][rows,:],L['VN'][rows,:]))*inv,0.0)
    L['S'][s]=S
    t=halves(mm(pack(S),L['WO2'][...]))
    L['T'][s]=t
    t2=quad(t)
    u=halves(mm(L['WQL'][...],t2))
    bq=jnp.broadcast_to(vec[BQ:BQ+1,:],(8,D))
    L['UB'][s]=halves(mm(pack(bq),t2))+vec[BO:BO+1,:]
    L['U2'][s]=quad(u)
    L['UT2'][s]=quad(u.T)

def fwd_c(L,vec,OUT,s,r0,n):
    rows=pl.ds(r0,n)
    mid=L['H'][rows,:]+halves(mm(L['X'][rows,:],L['U2'][s]))+L['UB'][s,0:1,:]
    md=pack(mid); L['MD'][rows,:]=md
    bu=jnp.concatenate([vec[BU0:BU0+1,:],vec[BU1:BU1+1,:]],axis=1)
    z=halves(mm(md,L['WUP'][...]))+bu
    z2=z*z
    c0=0.7978845608028654
    t=jnp.tanh(z*(c0+(c0*0.044715)*z2))
    p=0.5*t+0.5
    act=z*p
    L['DG'][rows,:]=p+act*(1.0-p)*((2*c0)+(6*c0*0.044715)*z2)
    act2=pack(act)
    L['ACT'][rows,:]=act2
    OUT[rows,:]=mid+halves(mm(act2,L['WDN'][...]))+vec[BD:BD+1,:]

def bwd_a(L,Tm,r0,n):
    rows=pl.ds(r0,n)
    e=Tm['E'][rows,:]
    ed=pack(e); Tm['ED'][rows,:]=ed
    ep=halves(mm(ed,L['WDNT'][...]))*L['DG'][rows,:]
    ep2=pack(ep); Tm['EP'][rows,:]=ep2
    em=e+halves(mm(ep2,L['WUPT'][...]))
    Tm['EM'][rows,:]=em
    Tm['EO'][rows,:]=pack(em)
    return part(e),part(ep),part(em)

def bwd_s(L,vec,Tm,gm,s,inv,c):
    rows=pl.ds(s*BLK,BLK)
    H=quads(tn(L['X'][rows,:],Tm['EO'][rows,:]))
    c1=jnp.sum(c,axis=0,keepdims=True)
    H2=quad(H)
    P=halves(mm(L['WQTL'][...],H2))+vec[BQ:BQ+1,:].T*c1
    es=jnp.where(gm,halves(mm(pack(P),L['WOT2'][...]))*inv,0.0)
    t2=quad(L['T'][s].T)
    gq=halves(mm(pack(H),t2))
    gbq=halves(mm(pack(c),t2))
    go=halves(mm(pack(L['S'][s].T),quad(P)))
    return quad(es.T),quad(es),gq,gbq,go

def bwd_b(L,vec,Tm,A2,esT2,es2,r0,n):
    rows=pl.ds(r0,n)
    a2=A2[...]
    out=[]
    for i,(N,R,O,g,w) in enumerate((('NK','RK','VN',GK,esT2),('NV','RV','KN',GV,es2))):
        en=halves(mm(L[O][rows,:],w))
        nn=L[N][rows,:]
        m=en*vec[g:g+1,:]
        mn=m*nn
        av=mm(pack(mn),a2)
        f=L[R][rows,:]*(m-nn*av)
        Tm['FKV'][rows,i*2*D:(i+1)*2*D]=pack(f)
        out+= [part(en),part(en*nn),part(f)]
    return out

def bwd_x(L,Tm,DX,s,r0,n):
    rows=pl.ds(r0,n)
    DX[rows,:]=Tm['EM'][rows,:]+halves(mm(Tm['FKV'][rows,:],L['WKVT'][...])+mm(Tm['EO'][rows,:],L['UT2'][s]))


MESH = pl.DeviceIdType.MESH
NAMES = ("k", "v", "q", "o", "up", "dn")
ARG = dict(q=0, k=1, v=2, o=3, up=12, dn=14)
VECS = ((4, BQ), (5, BK), (6, BV), (7, BO), (8, GK), (9, SK), (10, GV), (11, SV), (15, BD), (13, BU0))
SMALL = 16
GROUPS = (
    ((1, "up"), (1, "dn"), (1, "q"), (1, "o"), (1, "k"), (1, "v"), (1, "small")),
    ((0, "up"), (0, "dn"), (0, "q"), (0, "o")),
    ((0, "k"), (0, "v"), (0, "small")),
)


def shard(name, n_zero):
    if name == "dn":
        return FF // n_zero, D
    return D // n_zero, FF if name == "up" else D


def group_layout(n_dp, n_zero):
    places, sizes, pieces = {}, [], []
    for g, members in enumerate(GROUPS):
        at = 0
        for item in members:
            places[item] = (g, at)
            if item[1] == "small":
                at += SMALL
            else:
                rows, cols = shard(item[1], n_zero)
                at += rows * cols // D
        sizes.append(at)
        pieces.append(-(-at // (8 * n_dp)) * 8)
    return places, sizes, pieces


def center(x, a1):
    h = x.astype(BF)
    r = x - h.astype(F32)
    m = r.astype(BF)
    lo = (r - m.astype(F32)).astype(BF)
    return x - (mm(h, a1) + mm(m, a1) + mm(lo, a1))


def one(x):
    return jnp.sum(x, axis=0, keepdims=True)


class Names:
    pass


def fused_kernel(n_dp, n_zero, order, *refs):
    R = Names()
    for name, ref in zip(order, refs):
        setattr(R, name, ref)
    places, sizes, pieces = group_layout(n_dp, n_zero)
    dp, zero = lax.axis_index("dp"), lax.axis_index("zero")
    zpeer = [None] + [lax.rem(zero + k, n_zero) for k in range(1, n_zero)]
    zfrom = [None] + [lax.rem(zero + n_zero - k, n_zero) for k in range(1, n_zero)]
    dpeer = [None] + [lax.rem(dp + k, n_dp) for k in range(1, n_dp)]
    dfrom = [None] + [lax.rem(dp + n_dp - k, n_dp) for k in range(1, n_dp)]

    barrier = pltpu.get_barrier_semaphore()
    for k in range(1, n_zero):
        pl.semaphore_signal(barrier, inc=1, device_id=(dp, zpeer[k]), device_id_type=MESH)
    for k in range(1, n_dp):
        pl.semaphore_signal(barrier, inc=1, device_id=(dpeer[k], zero), device_id_type=MESH)

    small_in = []
    for i, (arg, _) in enumerate(VECS):
        c = pltpu.make_async_copy(R.params[arg], R.stage[i], R.stage_sem.at[i])
        c.start()
        small_in.append(c)
    nodes_in = pltpu.make_async_copy(R.nodes, R.nodes_v, R.io_sem.at[0])
    nodes_in.start()

    def rows_of(name, who):
        n = shard(name, n_zero)[0]
        return pl.ds(pl.multiple_of(who * n, n), n)

    own = {}
    for level in range(2):
        for i, name in enumerate(NAMES):
            own[level, name] = pltpu.make_async_copy(
                R.params[ARG[name]].at[level],
                R.weights[name].at[level, rows_of(name, zero), :],
                R.own_sem.at[level, i],
            )
    for level in range(2):
        for name in NAMES:
            own[level, name].start()
    cot_in = pltpu.make_async_copy(R.cotangent, R.cot_v, R.io_sem.at[1])
    cot_in.start()

    pl.semaphore_wait(barrier, n_zero - 1 + n_dp - 1)

    def weight_copy(level, name, k, who):
        i = NAMES.index(name)
        return pltpu.make_async_remote_copy(
            src_ref=R.params[ARG[name]].at[level],
            dst_ref=R.weights[name].at[level, rows_of(name, who), :],
            send_sem=R.w_send.at[level, i, k - 1],
            recv_sem=R.w_recv.at[level, i, k - 1],
            device_id=(dp, zpeer[k]),
            device_id_type=MESH,
        )

    def send_weights(level, names):
        for name in names:
            for k in range(1, n_zero):
                weight_copy(level, name, k, zero).start()

    def take_weights(level, names):
        for name in names:
            own[level, name].wait()
            for k in range(1, n_zero):
                weight_copy(level, name, k, zfrom[k]).wait_recv()

    send_weights(0, ("k", "v"))

    for c in small_in:
        c.wait()
    lane = lax.broadcasted_iota(jnp.int32, (2, D), 1)
    R.vec_own[...] = jnp.zeros((2, SMALL, D), F32)
    for i, (arg, row) in enumerate(VECS):
        x = R.stage[i][...]
        n = x.shape[1]
        x = jnp.concatenate([x, jnp.zeros((2, D - n), F32)], axis=1)
        x = pltpu.roll(x, lax.rem(zero * n, D), axis=1)
        if row != BU0:
            R.vec_own[:, row, :] = x
        else:
            first = zero * n < D
            R.vec_own[:, row, :] = jnp.where(first, x, 0.0)
            R.vec_own[:, row + 1, :] = jnp.where(first, 0.0, x)

    def vec_copy(k):
        return pltpu.make_async_remote_copy(
            src_ref=R.vec_own,
            dst_ref=R.vec_in.at[k - 1],
            send_sem=R.vec_send.at[k - 1],
            recv_sem=R.vec_recv.at[k - 1],
            device_id=(dp, zpeer[k]),
            device_id_type=MESH,
        )

    for k in range(1, n_zero):
        vec_copy(k).start()
    send_weights(0, ("q", "o", "up", "dn"))
    send_weights(1, NAMES)

    gm = group_mask()
    a = jnp.where(gm, 1.0 / HD, 0.0).astype(BF)
    R.A2[0:D, :] = a
    R.A2[D:, :] = a
    ln = [R.lengths[i] for i in range(SEGS)]
    st = [0]
    for i in range(SEGS):
        st.append(st[-1] + ln[i])
    inv = [1.0 / (jnp.full((1, D), ln[s], jnp.int32).astype(F32)) for s in range(SEGS)]

    def live(r0, n):
        s = r0 // BLK
        return lax.broadcasted_iota(jnp.int32, (n, D), 0) + (r0 - s * BLK) < ln[s]

    Ls, Tm = R.layers, R.temps
    Tm["A2"] = R.A2
    nodes_in.wait()
    for s in range(SEGS):
        Ls[0]["H"][s * BLK : (s + 1) * BLK, :] = R.nodes_v[pl.ds(st[s], BLK), :]

    for k in range(1, n_zero):
        vec_copy(k).wait_recv()
    vecs = []
    for level in range(2):
        x = R.vec_own[level]
        for k in range(1, n_zero):
            x = x + R.vec_in[k - 1, level]
        R.vec[level] = x
        vecs.append(R.vec.at[level])

    for level in range(2):
        L = Ls[level]
        dst = Ls[1]["H"] if level == 0 else R.Y
        w = {n: R.weights[n].at[level] for n in NAMES}
        take_weights(level, ("k", "v"))
        prep_kv(L, w, vecs[level], R.A2)
        for s in range(SEGS):
            fwd_a(L, vecs[level], R.A2, live, s * BLK, BLK)
        take_weights(level, ("q", "o"))
        prep_qo(L, w)
        for s in range(SEGS):
            fwd_s(L, vecs[level], gm, s, inv[s])
        take_weights(level, ("up", "dn"))
        prep_ff(L, w)
        for s in range(SEGS):
            fwd_c(L, vecs[level], dst, s, s * BLK, BLK)

    cot_in.wait()
    for s in range(SEGS):
        x = R.cot_v[pl.ds(st[s], BLK), :]
        Tm["E"][s * BLK : (s + 1) * BLK, :] = jnp.where(live(s * BLK, BLK), x, 0.0)

    def put(level, name, g):
        grp, at = places[level, name]
        n = shard(name, n_zero)[0]
        for p in range(n_zero):
            part_p = g[p * n : (p + 1) * n]
            if name == "up":
                R.gsend[grp][p, at : at + n, :] = part_p[:, :D]
                R.gsend[grp][p, at + n : at + 2 * n, :] = part_p[:, D:]
            else:
                R.gsend[grp][p, at : at + n, :] = part_p

    def zero_copy(grp, k):
        return pltpu.make_async_remote_copy(
            src_ref=R.gsend[grp].at[zpeer[k]],
            dst_ref=R.gzero[grp].at[k - 1],
            send_sem=R.z_send.at[grp, k - 1],
            recv_sem=R.z_recv.at[grp, k - 1],
            device_id=(dp, zpeer[k]),
            device_id_type=MESH,
        )

    def start_zero(grp):
        for k in range(1, n_zero):
            zero_copy(grp, k).start()

    def piece_copy(grp, k):
        return pltpu.make_async_remote_copy(
            src_ref=R.gred[grp].at[dpeer[k]],
            dst_ref=R.gdp[grp].at[k - 1],
            send_sem=R.d_send.at[grp, k - 1],
            recv_sem=R.d_recv.at[grp, k - 1],
            device_id=(dpeer[k], zero),
            device_id_type=MESH,
        )

    def final_copy(grp, k, who):
        return pltpu.make_async_remote_copy(
            src_ref=R.gfin[grp].at[dp],
            dst_ref=R.gfin[grp].at[who],
            send_sem=R.f_send.at[grp, k - 1],
            recv_sem=R.f_recv.at[grp, k - 1],
            device_id=(dpeer[k], zero),
            device_id_type=MESH,
        )

    def start_dp(grp):
        for k in range(1, n_zero):
            zero_copy(grp, k).wait_recv()
        total, piece = sizes[grp], pieces[grp]
        for j in range(n_dp):
            lo, hi = j * piece, min((j + 1) * piece, total)
            if lo < hi:
                x = R.gsend[grp][zero, lo:hi, :]
                for k in range(1, n_zero):
                    x = x + R.gzero[grp][k - 1, lo:hi, :]
                R.gred[grp][j, 0 : hi - lo, :] = x
            if hi - lo < piece:
                lo = max(hi - lo, 0)
                R.gred[grp][j, lo:piece, :] = jnp.zeros((piece - lo, D), F32)
        for k in range(1, n_dp):
            piece_copy(grp, k).start()

    def start_final(grp):
        x = R.gred[grp][dp]
        for k in range(1, n_dp):
            piece_copy(grp, k).wait_recv()
            x = x + R.gdp[grp][k - 1]
        R.gfin[grp][dp] = x
        for k in range(1, n_dp):
            final_copy(grp, k, dp).start()

    def end_final(grp):
        for k in range(1, n_dp):
            final_copy(grp, k, dfrom[k]).wait_recv()
        c = pltpu.make_async_copy(R.gfin[grp], R.fin_out[grp], R.io_sem.at[4 + grp])
        c.start()
        return c

    shift = [jnp.minimum(BLK * s - st[s], (BLK - 256) * s) for s in range(SEGS)]

    def unpack(o, base):
        lo, hi = (0, 256, 512, 768), (512, 1024, 1536, 2048)
        step = 256
        for t0 in range(0, TOK, step):
            it = lax.broadcasted_iota(jnp.int32, (step, D), 0) + t0
            x = base[t0 : t0 + step, :]
            for s in range(SEGS):
                if t0 < hi[s] and t0 + step > lo[s]:
                    y = R.Y[pl.ds(t0 + shift[s], step), :]
                    x = jnp.where((it >= st[s]) & (it < st[s + 1]), y, x)
            o[t0 : t0 + step, :] = x

    R.Y[TOK:, :] = jnp.zeros((R.Y.shape[0] - TOK, D), F32)
    unpack(R.nodes_v, R.nodes_v)
    store_out = pltpu.make_async_copy(R.nodes_v, R.out, R.io_sem.at[2])
    store_out.start()

    zero8 = jnp.zeros((8, D), F32)
    for level in (1, 0):
        L = Ls[level]
        w = {n: R.weights[n].at[level] for n in NAMES}
        prep_back(L, w)
        sb, su, sc = zero8, jnp.zeros((8, FF), F32), []
        for s in range(SEGS):
            b, u, o = bwd_a(L, Tm, s * BLK, BLK)
            sb, su = sb + b, su + u
            sc.append(o)
        if level == 0:
            start_dp(0)
        put(level, "dn", quads(tn(L["ACT"][...], Tm["ED"][...])))
        put(level, "up", quads(tn(L["MD"][...], Tm["EP"][...])))
        gq = go = jnp.zeros((D, D), F32)
        gbq = zero8
        es = []
        for s in range(SEGS):
            eT, e2, q1, b1, o1 = bwd_s(L, vecs[level], Tm, gm, s, inv[s], sc[s])
            gq, go, gbq = gq + q1, go + o1, gbq + b1
            es.append((eT, e2))
        put(level, "q", gq)
        put(level, "o", go)
        if level == 0:
            start_zero(1)
        ss = [zero8] * 6
        for s in range(SEGS):
            o = bwd_b(L, vecs[level], Tm, R.A2, *es[s], s * BLK, BLK)
            ss = [x + y for x, y in zip(ss, o)]
        a1 = R.A2[0:D, :]
        gkv = tn(L["X"][...], Tm["FKV"][...])
        gkv = gkv[0:D] + gkv[D:]
        put(level, "k", center(halves(gkv[:, : 2 * D]), a1))
        put(level, "v", center(halves(gkv[:, 2 * D :]), a1))
        rows = [None] * SMALL
        rows[BQ], rows[BK], rows[BV] = one(gbq), one(center(ss[2], a1)), one(center(ss[5], a1))
        rows[BO] = one(sc[0] + sc[1] + sc[2] + sc[3])
        rows[SK], rows[GK], rows[SV], rows[GV] = one(ss[0]), one(ss[1]), one(ss[3]), one(ss[4])
        rows[BD] = one(sb)
        u = one(su)
        rows[BU0], rows[BU1] = u[:, :D], u[:, D:]
        rows = [jnp.zeros((1, D), F32) if r is None else r for r in rows]
        small = jnp.concatenate(rows, axis=0)
        grp, at = places[level, "small"]
        for p in range(n_zero):
            R.gsend[grp][p, at : at + SMALL, :] = small
        start_zero(0 if level == 1 else 2)
        if level == 0:
            start_final(0)
        dst = Tm["E"] if level == 1 else R.Y
        for s in range(SEGS):
            bwd_x(L, Tm, dst, s, s * BLK, BLK)

    start_dp(1)
    start_dp(2)
    unpack(R.cot_v, R.cot_v)
    store_gx = pltpu.make_async_copy(R.cot_v, R.gx, R.io_sem.at[3])
    store_gx.start()
    start_final(1)
    start_final(2)
    last = [store_out, store_gx] + [end_final(g) for g in range(3)]

    for level in range(2):
        for name in NAMES:
            for k in range(1, n_zero):
                weight_copy(level, name, k, zero).wait_send()
    for k in range(1, n_zero):
        vec_copy(k).wait_send()
    for g in range(3):
        for k in range(1, n_zero):
            zero_copy(g, k).wait_send()
        for k in range(1, n_dp):
            piece_copy(g, k).wait_send()
            final_copy(g, k, dp).wait_send()
    for c in last:
        c.wait()


def finish_kernel(n_dp, n_zero, order, *refs):
    R = Names()
    for name, ref in zip(order, refs):
        setattr(R, name, ref)
    places, sizes, pieces = group_layout(n_dp, n_zero)
    copies = []

    def copy(src, dst):
        c = pltpu.make_async_copy(src, dst, R.sem.at[len(copies)])
        c.start()
        copies.append(c)

    fins = []
    for g in range(3):
        c = pltpu.make_async_copy(R.fin[g], R.fin_v[g], R.fin_sem.at[g])
        c.start()
        fins.append(c)
    half = TOK // 2
    for i in range(2):
        copy(R.out.at[pl.ds(i * half, half), :], R.outs[0].at[pl.ds(i * half, half), :])
        copy(R.gx.at[pl.ds(i * half, half), :], R.outs[1].at[pl.ds(i * half, half), :])
    for c in fins:
        c.wait()
    for name, arg in ARG.items():
        for level in range(2):
            g, at = places[level, name]
            n = shard(name, n_zero)[0]
            if name == "up":
                for h in range(2):
                    copy(
                        R.fin_v[g].at[pl.ds(at + h * n, n), :],
                        R.outs[2 + arg].at[level, :, pl.ds(h * D, D)],
                    )
            else:
                copy(R.fin_v[g].at[pl.ds(at, n), :], R.outs[2 + arg].at[level])
    zero = lax.axis_index("zero")
    small = []
    for level in range(2):
        g, at = places[level, "small"]
        small.append(R.fin_v[g][at : at + SMALL, :])
    for arg, row in VECS:
        n = R.outs[2 + arg].shape[1]
        x = jnp.concatenate([s[row : row + 1, :] for s in small], axis=0)
        if row == BU0:
            x1 = jnp.concatenate([s[row + 1 : row + 2, :] for s in small], axis=0)
            x = jnp.where(zero * n < D, x, x1)
        x = pltpu.roll(x, lax.rem(D - lax.rem(zero * n, D), D), axis=1)
        R.outs[2 + arg][...] = x[:, :n]
    for c in copies:
        c.wait()


def make_fused(n_dp, n_zero, params):
    places, sizes, pieces = group_layout(n_dp, n_zero)
    dma = pltpu.SemaphoreType.DMA
    any_ = pl.BlockSpec(memory_space=pl.ANY)
    order, scratch = [], []

    def add(name, shape):
        order.append(name)
        scratch.append(shape)

    def sds(*shape):
        return jax.ShapeDtypeStruct(shape, F32)

    n_params = len(params)
    out_shape = [sds(TOK, D), sds(TOK, D)] + [sds(n_dp, p, D) for p in pieces]
    ls, ts = list(LAYER_SCRATCH), [n for n in TMP_SCRATCH if n != "A2"]
    for level in range(2):
        for n in ls:
            add(("layer", level, n), VM(*LAYER_SCRATCH[n]))
    for n in ts:
        add(("temp", n), VM(*TMP_SCRATCH[n]))
    add("A2", VM(*TMP_SCRATCH["A2"]))
    add("Y", VM((TOK + 768, D), F32))
    add("nodes_v", VM((TOK, D), F32))
    add("cot_v", VM((TOK, D), F32))
    for i, (arg, _) in enumerate(VECS):
        add(("stage", i), VM(params[arg].shape, F32))
    for n in NAMES:
        rows, cols = shard(n, n_zero)
        add(("weights", n), VM((2, rows * n_zero, cols), F32))
    add("vec_own", VM((2, SMALL, D), F32))
    add("vec_in", VM((n_zero - 1, 2, SMALL, D), F32))
    add("vec", VM((2, SMALL, D), F32))
    for g in range(3):
        add(("gsend", g), VM((n_zero, sizes[g], D), F32))
        add(("gzero", g), VM((n_zero - 1, sizes[g], D), F32))
        add(("gred", g), VM((n_dp, pieces[g], D), F32))
        add(("gdp", g), VM((n_dp - 1, pieces[g], D), F32))
        add(("gfin", g), VM((n_dp, pieces[g], D), F32))
    add("stage_sem", dma((len(VECS),)))
    add("io_sem", dma((8,)))
    add("own_sem", dma((2, 6)))
    add("w_send", dma((2, 6, n_zero - 1)))
    add("w_recv", dma((2, 6, n_zero - 1)))
    add("vec_send", dma((n_zero - 1,)))
    add("vec_recv", dma((n_zero - 1,)))
    for n, m in (("z", n_zero), ("d", n_dp), ("f", n_dp)):
        add(n + "_send", dma((3, m - 1)))
        add(n + "_recv", dma((3, m - 1)))

    def body(*refs):
        lengths, nodes, cot = refs[:3]
        pr = refs[3 : 3 + n_params]
        outs = refs[3 + n_params : 8 + n_params]
        rest = refs[8 + n_params :]
        simple = dict(lengths=lengths, nodes=nodes, cotangent=cot, params=pr, out=outs[0], gx=outs[1], fin_out=outs[2:5])
        layers, temps = [{}, {}], {}
        simple.update(layers=layers, temps=temps, stage=[None] * len(VECS), weights={})
        for n in ("gsend", "gzero", "gred", "gdp", "gfin"):
            simple[n] = [None] * 3
        for key, ref in zip(order, rest):
            if isinstance(key, str):
                simple[key] = ref
            elif key[0] == "layer":
                layers[key[1]][key[2]] = ref
            elif key[0] == "temp":
                temps[key[1]] = ref
            else:
                simple[key[0]][key[1]] = ref
        fused_kernel(n_dp, n_zero, list(simple), *simple.values())

    call = pl.pallas_call(
        body,
        out_shape=out_shape,
        in_specs=[pl.BlockSpec(memory_space=pltpu.SMEM)] + [any_] * (2 + n_params),
        out_specs=[any_] * 5,
        scratch_shapes=scratch,
        compiler_params=pltpu.CompilerParams(
            collective_id=0, has_side_effects=True, vmem_limit_bytes=60 * 1024 * 1024
        ),
    )
    return call


def make_finish(n_dp, n_zero, params):
    places, sizes, pieces = group_layout(n_dp, n_zero)
    any_ = pl.BlockSpec(memory_space=pltpu.HBM)
    vmem = pl.BlockSpec(memory_space=pltpu.VMEM)
    out_shape = [jax.ShapeDtypeStruct((TOK, D), F32)] * 2
    out_shape += [jax.ShapeDtypeStruct(p.shape, F32) for p in params]
    weights = set(ARG.values())
    out_specs = [any_] * 2 + [any_ if i in weights else vmem for i in range(len(params))]

    def body(*refs):
        out, gx = refs[:2]
        fin = refs[2:5]
        outs = refs[5 : 7 + len(params)]
        rest = refs[7 + len(params) :]
        simple = dict(out=out, gx=gx, fin=fin, outs=outs, fin_v=rest[:3], sem=rest[3], fin_sem=rest[4])
        finish_kernel(n_dp, n_zero, list(simple), *simple.values())

    return pl.pallas_call(
        body,
        out_shape=out_shape,
        in_specs=[any_] * 5,
        out_specs=out_specs,
        scratch_shapes=[VM((n_dp * p, D), F32) for p in pieces]
        + [pltpu.SemaphoreType.DMA((18,)), pltpu.SemaphoreType.DMA((3,))],
        compiler_params=pltpu.CompilerParams(vmem_limit_bytes=32 * 1024 * 1024),
    )


def solution(mesh):
    n_dp, n_zero = mesh.shape["dp"], mesh.shape["zero"]
    wide, flat = P(None, "zero", None), P(None, "zero")
    params = (wide,) * 4 + (flat,) * 8 + (wide, flat, wide, flat)
    rows = P(("dp", "zero"), None)

    def local(nodes, cotangent, lengths, *params):
        out, gx, *fins = make_fused(n_dp, n_zero, params)(lengths, nodes, cotangent, *params)
        fins = [f.reshape(-1, D) for f in fins]
        return tuple(make_finish(n_dp, n_zero, params)(out, gx, *fins))

    return jax.shard_map(
        local,
        mesh=mesh,
        in_specs=(rows, rows, P(("dp", "zero"))) + params,
        out_specs=(rows, rows) + params,
        check_vma=False,
    )
```

```python
import jax
import jax.numpy as jnp
from jax import lax
from jax.experimental import pallas as pl
from jax.experimental.pallas import tpu as pltpu
from jax.sharding import PartitionSpec as P

D=128; FF=256; SEGS=4; BLK=512; TOK=2048; HD=32
F32=jnp.float32; BF=jnp.bfloat16
VM=pltpu.VMEM

def split(x):
    hi=x.astype(BF); lo=(x-hi.astype(F32)).astype(BF)
    return hi,lo
def cat0(*x): return jnp.concatenate(x,axis=0)
def cat1(*x): return jnp.concatenate(x,axis=1)
def pack(x):
    return cat1(*split(x))
def quad(x):
    p=pack(x)
    return cat0(p,p)
def quad_t(x):
    h,l=split(x)
    return cat0(cat1(h,h),cat1(l,l))
def mm(a,b):
    return jnp.dot(a,b,preferred_element_type=F32)
def tn(a,b):
    return lax.dot_general(a,b,(((0,),(0,)),((),())),preferred_element_type=F32)
def nt(a,b):
    return lax.dot_general(a,b,(((1,),(1,)),((),())),preferred_element_type=F32)
def halves(r):
    n=r.shape[1]//2
    return r[:,:n]+r[:,n:]
def quads(r):
    m=r.shape[0]//2
    return halves(r[:m]+r[m:])
def part(x):
    return jnp.sum(x.reshape(x.shape[0]//8,8,x.shape[1]),axis=0)
def one(x):
    return jnp.sum(x,axis=0,keepdims=True)
def group_mask():
    r=lax.broadcasted_iota(jnp.int32,(D,D),0)//HD
    c=lax.broadcasted_iota(jnp.int32,(D,D),1)//HD
    return r==c
def center(x,a1):
    h=x.astype(BF); r=x-h.astype(F32); m=r.astype(BF); lo=(r-m.astype(F32)).astype(BF)
    return x-(mm(h,a1)+mm(m,a1)+mm(lo,a1))

BQ,BK,BV,BO,GK,SK,GV,SV,BD,BU0,BU1=range(11)
AUG=D+16

LAYER_SCRATCH=dict(
    X=((TOK,2*D),BF), H=((TOK,D),F32), NK=((TOK,D),F32), NV=((TOK,D),F32), RK=((TOK,D),F32), RV=((TOK,D),F32),
    KN=((TOK,2*D),BF), VN=((TOK,2*D),BF), MD=((TOK,2*D),BF), ACT=((TOK,2*FF),BF), DG=((TOK,FF),F32),
    WKV=((2*D,4*D),BF), WUP=((2*D,2*FF),BF), WDN=((2*FF,2*D),BF), WDNT=((2*FF,2*D),BF), WUPT=((2*D,2*FF),BF),
    WKVT=((2*D,4*D),BF), WO2=((2*D,2*D),BF), WOT2=((2*D,2*D),BF), WQA=((AUG,2*D),BF),
    SP=((SEGS*D,2*D),BF), TP=((2*D,SEGS*D),BF), UT2=((SEGS,2*D,2*D),BF), U2=((SEGS,2*D,2*D),BF), UB=((SEGS,8,D),F32),
    CB=((8,D),F32),
)
TMP_SCRATCH=dict(
    E=((TOK,D),F32), ED=((TOK,2*D),BF), EP=((TOK,2*FF),BF), EM=((TOK,D),F32), EO=((TOK,2*D),BF), FKV=((TOK,4*D),BF),
    A2=((2*D,D),BF),
)

def prep_kv(L,w,vec,A2):
    a1=A2[0:D,:]
    b8=cat0(vec[BK:BV+1,:],jnp.zeros((6,D),F32))
    L['CB'][...]=center(b8,a1)
    wk=center(w['k'][...],a1); wv=center(w['v'][...],a1)
    kh,kl=split(wk); vh,vl=split(wv)
    kv=cat1(kh,vh,kl,vl)
    L['WKV'][0:D,:]=kv; L['WKV'][D:,:]=kv
    L['WKVT'][0:D,:]=cat1(kh,kh,vh,vh); L['WKVT'][D:,:]=cat1(kl,kl,vl,vl)

def prep_qo(L,w,vec):
    wo=w['o'][...]
    L['WO2'][...]=quad(wo); L['WOT2'][...]=quad_t(wo)
    L['WQA'][0:D,:]=pack(w['q'][...])
    L['WQA'][D:,:]=pack(cat0(vec[BQ:BQ+1,:],jnp.zeros((15,D),F32)))

def prep_ff(L,w):
    up=w['up'][...]
    L['WUP'][...]=quad(up)
    dn=w['dn'][...]
    L['WDN'][...]=quad(dn)

def prep_back(L,w):
    L['WUPT'][...]=quad_t(w['up'][...])
    L['WDNT'][...]=quad_t(w['dn'][...])

def fwd_a(L,vec,A2,live,r0,n,fresh):
    rows=pl.ds(r0,n)
    if fresh:
        x=pack(L['H'][rows,:])
        L['X'][rows,:]=x
    else:
        x=L['X'][rows,:]
    r=mm(x,L['WKV'][...])
    a2=A2[...]
    lv=live(r0,n)
    for i,(N,R,O,g,s) in enumerate((('NK','RK','KN',GK,SK),('NV','RV','VN',GV,SV))):
        c=r[:,i*D:(i+1)*D]+r[:,(i+2)*D:(i+3)*D]+L['CB'][i:i+1,:]
        rs=lax.rsqrt(mm(pack(c*c),a2)+1e-5)
        nn=c*rs
        L[R][rows,:]=rs; L[N][rows,:]=nn
        y=jnp.where(lv,nn*vec[g:g+1,:]+vec[s:s+1,:],0.0)
        L[O][rows,:]=pack(y)

def fwd_s(L,vec,gm,inv):
    for s in range(SEGS):
        rows=pl.ds(s*BLK,BLK)
        S=jnp.where(gm,quads(tn(L['KN'][rows,:],L['VN'][rows,:]))*inv[s],0.0)
        L['SP'][s*D:(s+1)*D,:]=pack(S)
    T=halves(mm(L['SP'][...],L['WO2'][...]))
    ts=[T[s*D:(s+1)*D] for s in range(SEGS)]
    sp=[split(t) for t in ts]
    for s in range(SEGS):
        L['TP'][0:D,s*D:(s+1)*D]=sp[s][0]; L['TP'][D:,s*D:(s+1)*D]=sp[s][1]
    row=cat1(*[x for hl in sp for x in hl])
    u=mm(L['WQA'][...],cat0(row,row))
    for s in range(SEGS):
        us=halves(u[:,s*2*D:(s+1)*2*D])
        L['UB'][s]=us[D:D+8]+vec[BO:BO+1,:]
        h,l=split(us[:D])
        p=cat1(h,l)
        L['U2'][s,0:D,:]=p; L['U2'][s,D:,:]=p
        L['UT2'][s,0:D,:]=cat1(h,h); L['UT2'][s,D:,:]=cat1(l,l)

def fwd_c1(L,s,r0,n):
    rows=pl.ds(r0,n)
    mid=L['H'][rows,:]+halves(mm(L['X'][rows,:],L['U2'][s]))+L['UB'][s,0:1,:]
    L['MD'][rows,:]=pack(mid)
    return mid

def fwd_c2(L,vec,r0,n):
    rows=pl.ds(r0,n)
    bu=cat1(vec[BU0:BU0+1,:],vec[BU1:BU1+1,:])
    z=halves(mm(L['MD'][rows,:],L['WUP'][...]))+bu
    z2=z*z
    c0=0.7978845608028654
    t=jnp.tanh(z*(c0+(c0*0.044715)*z2))
    p=0.5*t+0.5
    act=z*p
    L['DG'][rows,:]=p+act*(1.0-p)*((2*c0)+(6*c0*0.044715)*z2)
    L['ACT'][rows,:]=pack(act)

def fwd_c3(L,vec,OUT,mid,r0,n):
    rows=pl.ds(r0,n)
    OUT[rows,:]=mid+halves(mm(L['ACT'][rows,:],L['WDN'][...]))+vec[BD:BD+1,:]

def bwd_a1(L,Tm,r0,n,fresh):
    rows=pl.ds(r0,n)
    if fresh:
        e=Tm['E'][rows,:]
        ed=pack(e); Tm['ED'][rows,:]=ed
        se=part(e)
    else:
        ed=Tm['ED'][rows,:]; se=None
    ep=halves(nt(ed,L['WDNT'][...]))*L['DG'][rows,:]
    Tm['EP'][rows,:]=pack(ep)
    return se,part(ep)

def bwd_a2(L,Tm,r0,n):
    rows=pl.ds(r0,n)
    em=Tm['E'][rows,:]+halves(nt(Tm['EP'][rows,:],L['WUPT'][...]))
    Tm['EM'][rows,:]=em
    Tm['EO'][rows,:]=pack(em)
    return part(em)

def bwd_s1(L,Tm,c):
    hs=[]
    for s in range(SEGS):
        rows=pl.ds(s*BLK,BLK)
        H=quads(tn(L['X'][rows,:],Tm['EO'][rows,:]))
        hs.append(split(cat0(H,one(c[s]),jnp.zeros((15,D),F32))))
    return hs

def bwd_s2(L,hs):
    P=tn(L['WQA'][...],cat1(*[x for hl in hs for x in hl]))
    P=P[:D]+P[D:]
    pp=cat0(*[pack(halves(P[:,s*2*D:(s+1)*2*D])) for s in range(SEGS)])
    return pp

def bwd_s3(L,gm,inv,pp):
    es=halves(nt(pp,L['WOT2'][...]))
    out=[]
    for s in range(SEGS):
        e=jnp.where(gm,es[s*D:(s+1)*D]*inv[s],0.0)
        h,l=split(e); p=cat1(h,l)
        out.append((cat0(cat1(h,h),cat1(l,l)),cat0(p,p)))
    return out

def bwd_s4(L,hs,pp):
    go=quads(tn(L['SP'][...],pp))
    gq=halves(nt(cat0(cat1(*[h for h,l in hs]),cat1(*[l for h,l in hs])),L['TP'][...]))
    gq=gq[:AUG]+gq[AUG:]
    return gq[:D],gq[D:D+1],go

def bwd_b(L,vec,Tm,A2,esT2,es2,r0,n):
    rows=pl.ds(r0,n)
    a2=A2[...]
    out=[]
    for i,(N,R,O,g,f,w) in enumerate((('NK','RK','VN',GK,nt,esT2),('NV','RV','KN',GV,mm,es2))):
        en=halves(f(L[O][rows,:],w))
        nn=L[N][rows,:]
        m=en*vec[g:g+1,:]
        mn=m*nn
        av=mm(pack(mn),a2)
        f=L[R][rows,:]*(m-nn*av)
        Tm['FKV'][rows,i*2*D:(i+1)*2*D]=pack(f)
        out+= [part(en),part(en*nn),part(f)]
    return out

def bwd_x(L,Tm,DX,s,r0,n):
    rows=pl.ds(r0,n)
    DX[rows,:]=Tm['EM'][rows,:]+halves(nt(Tm['FKV'][rows,:],L['WKVT'][...])+nt(Tm['EO'][rows,:],L['UT2'][s]))


MESH = pl.DeviceIdType.MESH
NAMES = ("k", "v", "q", "o", "up", "dn")
ARG = dict(q=0, k=1, v=2, o=3, up=12, dn=14)
VECS = ((4, BQ), (5, BK), (6, BV), (7, BO), (8, GK), (9, SK), (10, GV), (11, SV), (15, BD), (13, BU0))
SMALL = 16
GROUPS = (
    ((1, "up"), (1, "dn"), (1, "q"), (1, "o")),
    ((1, "k"), (1, "v"), (1, "small")),
    ((0, "up"), (0, "dn")),
    ((0, "q"), (0, "o")),
    ((0, "k"), (0, "v"), (0, "small")),
)
NG = len(GROUPS)


def shard(name, n_zero):
    if name == "dn":
        return FF // n_zero, D
    return D // n_zero, FF if name == "up" else D


def group_layout(n_dp, n_zero):
    places, sizes, pieces = {}, [], []
    for g, members in enumerate(GROUPS):
        at = 0
        for item in members:
            places[item] = (g, at)
            if item[1] == "small":
                at += SMALL
            else:
                rows, cols = shard(item[1], n_zero)
                at += rows * cols // D
        sizes.append(at)
        pieces.append(-(-at // (8 * n_dp)) * 8)
    return places, sizes, pieces


class Names:
    pass


def fused_kernel(n_dp, n_zero, order, *refs):
    R = Names()
    for name, ref in zip(order, refs):
        setattr(R, name, ref)
    places, sizes, pieces = group_layout(n_dp, n_zero)
    dp, zero = lax.axis_index("dp"), lax.axis_index("zero")
    zpeer = [None] + [lax.rem(zero + k, n_zero) for k in range(1, n_zero)]
    zfrom = [None] + [lax.rem(zero + n_zero - k, n_zero) for k in range(1, n_zero)]
    dpeer = [None] + [lax.rem(dp + k, n_dp) for k in range(1, n_dp)]
    dfrom = [None] + [lax.rem(dp + n_dp - k, n_dp) for k in range(1, n_dp)]

    barrier = pltpu.get_barrier_semaphore()
    for k in range(1, n_zero):
        pl.semaphore_signal(barrier, inc=1, device_id=(dp, zpeer[k]), device_id_type=MESH)
    for k in range(1, n_dp):
        pl.semaphore_signal(barrier, inc=1, device_id=(dpeer[k], zero), device_id_type=MESH)

    len_in = pltpu.make_async_copy(R.lengths_in, R.lengths, R.io_sem.at[2])
    len_in.start()
    small_in = []
    for i, (arg, _) in enumerate(VECS):
        c = pltpu.make_async_copy(R.params[arg], R.stage[i], R.stage_sem.at[i])
        c.start()
        small_in.append(c)
    nodes_in = pltpu.make_async_copy(R.nodes, R.nodes_v, R.io_sem.at[0])
    nodes_in.start()

    def rows_of(name, who):
        n = shard(name, n_zero)[0]
        return pl.ds(pl.multiple_of(who * n, n), n)

    own = {}
    for level in range(2):
        for i, name in enumerate(NAMES):
            own[level, name] = pltpu.make_async_copy(
                R.params[ARG[name]].at[level],
                R.weights[name].at[level, rows_of(name, zero), :],
                R.own_sem.at[level, i],
            )
    for level in range(2):
        for name in NAMES:
            own[level, name].start()
    cot_in = pltpu.make_async_copy(R.cotangent, R.cot_v, R.io_sem.at[1])
    cot_in.start()

    pl.semaphore_wait(barrier, n_zero - 1 + n_dp - 1)

    def weight_copy(level, name, k, who):
        i = NAMES.index(name)
        return pltpu.make_async_remote_copy(
            src_ref=R.params[ARG[name]].at[level],
            dst_ref=R.weights[name].at[level, rows_of(name, who), :],
            send_sem=R.w_send.at[level, i, k - 1],
            recv_sem=R.w_recv.at[level, i, k - 1],
            device_id=(dp, zpeer[k]),
            device_id_type=MESH,
        )

    def send_weights(level, names):
        for name in names:
            for k in range(1, n_zero):
                weight_copy(level, name, k, zero).start()

    def take_weights(level, names):
        for name in names:
            own[level, name].wait()
            for k in range(1, n_zero):
                weight_copy(level, name, k, zfrom[k]).wait_recv()

    send_weights(0, ("k", "v"))

    for c in small_in:
        c.wait()
    lane = lax.broadcasted_iota(jnp.int32, (2, D), 1)
    R.vec_own[...] = jnp.zeros((2, SMALL, D), F32)
    for i, (arg, row) in enumerate(VECS):
        x = R.stage[i][...]
        n = x.shape[1]
        x = jnp.concatenate([x, jnp.zeros((2, D - n), F32)], axis=1)
        x = pltpu.roll(x, lax.rem(zero * n, D), axis=1)
        if row != BU0:
            R.vec_own[:, row, :] = x
        else:
            first = zero * n < D
            R.vec_own[:, row, :] = jnp.where(first, x, 0.0)
            R.vec_own[:, row + 1, :] = jnp.where(first, 0.0, x)

    def vec_copy(k):
        return pltpu.make_async_remote_copy(
            src_ref=R.vec_own,
            dst_ref=R.vec_in.at[k - 1],
            send_sem=R.vec_send.at[k - 1],
            recv_sem=R.vec_recv.at[k - 1],
            device_id=(dp, zpeer[k]),
            device_id_type=MESH,
        )

    for k in range(1, n_zero):
        vec_copy(k).start()
    len_in.wait()
    gm = group_mask()
    a = jnp.where(gm, 1.0 / HD, 0.0).astype(BF)
    R.A2[0:D, :] = a
    R.A2[D:, :] = a
    ln = [R.lengths[i] for i in range(SEGS)]
    st = [0]
    for i in range(SEGS):
        st.append(st[-1] + ln[i])
    inv = [1.0 / (jnp.full((1, D), ln[s], jnp.int32).astype(F32)) for s in range(SEGS)]

    def live(r0, n):
        s = r0 // BLK
        return lax.broadcasted_iota(jnp.int32, (n, D), 0) + (r0 - s * BLK) < ln[s]

    Ls, Tm = R.layers, R.temps
    Tm["A2"] = R.A2
    R.Y[TOK:, :] = jnp.zeros((R.Y.shape[0] - TOK, D), F32)
    nodes_in.wait()
    for s in range(SEGS):
        x = R.nodes_v[pl.ds(st[s], BLK), :]
        Ls[0]["H"][s * BLK : (s + 1) * BLK, :] = x
        Ls[0]["X"][s * BLK : (s + 1) * BLK, :] = pack(x)
    send_weights(0, ("q", "o"))
    cot_in.wait()
    sum_e = zero8 = jnp.zeros((8, D), F32)
    for s in range(SEGS):
        x = jnp.where(live(s * BLK, BLK), R.cot_v[pl.ds(st[s], BLK), :], 0.0)
        Tm["E"][s * BLK : (s + 1) * BLK, :] = x
        Tm["ED"][s * BLK : (s + 1) * BLK, :] = pack(x)
        sum_e = sum_e + part(x)

    for k in range(1, n_zero):
        vec_copy(k).wait_recv()
    vecs = []
    for level in range(2):
        x = R.vec_own[level]
        for k in range(1, n_zero):
            x = x + R.vec_in[k - 1, level]
        R.vec[level] = x
        vecs.append(R.vec.at[level])

    tiles = [(s, s * BLK) for s in range(SEGS)]

    def pipe(stages):
        kept = [None] * len(tiles)
        for t in range(len(tiles) + len(stages) - 1):
            for j, stage in enumerate(stages):
                if 0 <= t - j < len(tiles):
                    kept[t - j] = stage(tiles[t - j], kept[t - j])
        return kept

    for level in range(2):
        L, vec = Ls[level], vecs[level]
        dst = Ls[1]["H"] if level == 0 else R.Y
        w = {n: R.weights[n].at[level] for n in NAMES}
        take_weights(level, ("k", "v"))
        if level == 0:
            send_weights(0, ("up", "dn"))
        prep_kv(L, w, vec, R.A2)
        for s, r in tiles:
            fwd_a(L, vec, R.A2, live, r, BLK, level == 1)
        take_weights(level, ("q", "o"))
        if level == 0:
            send_weights(1, NAMES)
        prep_qo(L, w, vec)
        fwd_s(L, vec, gm, inv)
        take_weights(level, ("up", "dn"))
        prep_ff(L, w)

        def middle(tile, _):
            return fwd_c1(L, *tile, BLK)

        def hidden(tile, mid):
            fwd_c2(L, vec, tile[1], BLK)
            return mid

        def close(tile, mid):
            fwd_c3(L, vec, dst, mid, tile[1], BLK)

        pipe([middle, hidden, close])

    def put(level, name, g):
        grp, at = places[level, name]
        n = shard(name, n_zero)[0]
        for p in range(n_zero):
            part_p = g[p * n : (p + 1) * n]
            if name == "up":
                R.gsend[grp][p, at : at + n, :] = part_p[:, :D]
                R.gsend[grp][p, at + n : at + 2 * n, :] = part_p[:, D:]
            else:
                R.gsend[grp][p, at : at + n, :] = part_p

    def zero_copy(grp, k):
        return pltpu.make_async_remote_copy(
            src_ref=R.gsend[grp].at[zpeer[k]],
            dst_ref=R.gzero[grp].at[k - 1],
            send_sem=R.z_send.at[grp, k - 1],
            recv_sem=R.z_recv.at[grp, k - 1],
            device_id=(dp, zpeer[k]),
            device_id_type=MESH,
        )

    def start_zero(grp):
        for k in range(1, n_zero):
            zero_copy(grp, k).start()

    def piece_copy(grp, k):
        return pltpu.make_async_remote_copy(
            src_ref=R.gred[grp].at[dpeer[k]],
            dst_ref=R.gdp[grp].at[k - 1],
            send_sem=R.d_send.at[grp, k - 1],
            recv_sem=R.d_recv.at[grp, k - 1],
            device_id=(dpeer[k], zero),
            device_id_type=MESH,
        )

    def final_copy(grp, k, who):
        return pltpu.make_async_remote_copy(
            src_ref=R.gfin[grp].at[dp],
            dst_ref=R.gfin[grp].at[who],
            send_sem=R.f_send.at[grp, k - 1],
            recv_sem=R.f_recv.at[grp, k - 1],
            device_id=(dpeer[k], zero),
            device_id_type=MESH,
        )

    def start_dp(grp):
        for k in range(1, n_zero):
            zero_copy(grp, k).wait_recv()
        total, piece = sizes[grp], pieces[grp]
        for j in range(n_dp):
            lo, hi = j * piece, min((j + 1) * piece, total)
            if lo < hi:
                x = R.gsend[grp][zero, lo:hi, :]
                for k in range(1, n_zero):
                    x = x + R.gzero[grp][k - 1, lo:hi, :]
                R.gred[grp][j, 0 : hi - lo, :] = x
            if hi - lo < piece:
                lo = max(hi - lo, 0)
                R.gred[grp][j, lo:piece, :] = jnp.zeros((piece - lo, D), F32)
        for k in range(1, n_dp):
            piece_copy(grp, k).start()

    def start_final(grp):
        x = R.gred[grp][dp]
        for k in range(1, n_dp):
            piece_copy(grp, k).wait_recv()
            x = x + R.gdp[grp][k - 1]
        R.gfin[grp][dp] = x
        for k in range(1, n_dp):
            final_copy(grp, k, dp).start()

    def end_final(grp):
        for k in range(1, n_dp):
            final_copy(grp, k, dfrom[k]).wait_recv()
        c = pltpu.make_async_copy(R.gfin[grp], R.fin_out[grp], R.io_sem.at[5 + grp])
        c.start()
        return c

    shift = [jnp.minimum(BLK * s - st[s], (BLK - 256) * s) for s in range(SEGS)]

    def unpack(o, base):
        lo, hi = (0, 256, 512, 768), (512, 1024, 1536, 2048)
        step = 256
        for t0 in range(0, TOK, step):
            it = lax.broadcasted_iota(jnp.int32, (step, D), 0) + t0
            x = base[t0 : t0 + step, :]
            for s in range(SEGS):
                if t0 < hi[s] and t0 + step > lo[s]:
                    y = R.Y[pl.ds(t0 + shift[s], step), :]
                    x = jnp.where((it >= st[s]) & (it < st[s + 1]), y, x)
            o[t0 : t0 + step, :] = x

    unpack(R.nodes_v, R.nodes_v)
    store_out = pltpu.make_async_copy(R.nodes_v, R.out, R.io_sem.at[3])
    store_out.start()

    for level in (1, 0):
        L, vec = Ls[level], vecs[level]
        w = {n: R.weights[n].at[level] for n in NAMES}
        prep_back(L, w)

        def feed(tile, _):
            return bwd_a1(L, Tm, tile[1], BLK, level == 0)

        def after(tile, sums):
            return (*sums, bwd_a2(L, Tm, tile[1], BLK))

        sums = pipe([feed, after])
        sb = sum_e if level == 1 else sum((x[0] for x in sums), zero8)
        su = sum((x[1] for x in sums), jnp.zeros((8, FF), F32))
        sc = [x[2] for x in sums]
        put(level, "dn", quads(tn(L["ACT"][...], Tm["ED"][...])))
        put(level, "up", quads(tn(L["MD"][...], Tm["EP"][...])))
        if level == 0:
            start_zero(2)
        hs = bwd_s1(L, Tm, sc)
        pp = bwd_s2(L, hs)
        es = bwd_s3(L, gm, inv, pp)
        gq, gbq, go = bwd_s4(L, hs, pp)
        put(level, "q", gq)
        put(level, "o", go)
        if level == 0:
            start_zero(3)
            start_dp(0)
        else:
            start_zero(0)
        ss = [zero8] * 6
        for s, r in tiles:
            o = bwd_b(L, vec, Tm, R.A2, *es[s], r, BLK)
            ss = [x + y for x, y in zip(ss, o)]
        a1 = R.A2[0:D, :]
        gkv = tn(L["X"][...], Tm["FKV"][...])
        gkv = gkv[0:D] + gkv[D:]
        put(level, "k", center(halves(gkv[:, : 2 * D]), a1))
        put(level, "v", center(halves(gkv[:, 2 * D :]), a1))
        rows = [jnp.zeros((1, D), F32)] * SMALL
        rows[BQ], rows[BK], rows[BV] = gbq, one(center(ss[2], a1)), one(center(ss[5], a1))
        rows[BO] = one(sc[0] + sc[1] + sc[2] + sc[3])
        rows[SK], rows[GK], rows[SV], rows[GV] = one(ss[0]), one(ss[1]), one(ss[3]), one(ss[4])
        rows[BD] = one(sb)
        u = one(su)
        rows[BU0], rows[BU1] = u[:, :D], u[:, D:]
        small = jnp.concatenate(rows, axis=0)
        grp, at = places[level, "small"]
        for p in range(n_zero):
            R.gsend[grp][p, at : at + SMALL, :] = small
        if level == 1:
            start_zero(1)
        else:
            start_zero(4)
            start_dp(1)
            start_final(0)
        dst = Tm["E"] if level == 1 else R.Y
        for s, r in tiles:
            bwd_x(L, Tm, dst, s, r, BLK)

    start_dp(2)
    start_dp(3)
    unpack(R.cot_v, R.cot_v)
    store_gx = pltpu.make_async_copy(R.cot_v, R.gx, R.io_sem.at[4])
    store_gx.start()
    start_dp(4)
    start_final(1)
    start_final(2)
    start_final(3)
    start_final(4)
    last = [store_out, store_gx] + [end_final(g) for g in range(NG)]

    for level in range(2):
        for name in NAMES:
            for k in range(1, n_zero):
                weight_copy(level, name, k, zero).wait_send()
    for k in range(1, n_zero):
        vec_copy(k).wait_send()
    for g in range(NG):
        for k in range(1, n_zero):
            zero_copy(g, k).wait_send()
        for k in range(1, n_dp):
            piece_copy(g, k).wait_send()
            final_copy(g, k, dp).wait_send()
    for c in last:
        c.wait()


def finish_kernel(n_dp, n_zero, order, *refs):
    R = Names()
    for name, ref in zip(order, refs):
        setattr(R, name, ref)
    places, sizes, pieces = group_layout(n_dp, n_zero)
    copies = []

    def copy(src, dst):
        c = pltpu.make_async_copy(src, dst, R.sem.at[len(copies)])
        c.start()
        copies.append(c)

    smalls = []
    for level in range(2):
        g, at = places[level, "small"]
        c = pltpu.make_async_copy(R.fin[g].at[pl.ds(at, SMALL), :], R.small.at[level], R.small_sem.at[level])
        c.start()
        smalls.append(c)
    half = TOK // 2
    for i in range(2):
        copy(R.out.at[pl.ds(i * half, half), :], R.outs[0].at[pl.ds(i * half, half), :])
        copy(R.gx.at[pl.ds(i * half, half), :], R.outs[1].at[pl.ds(i * half, half), :])
    for name, arg in ARG.items():
        for level in range(2):
            g, at = places[level, name]
            n = shard(name, n_zero)[0]
            if name == "up":
                for h in range(2):
                    copy(
                        R.fin[g].at[pl.ds(at + h * n, n), :],
                        R.outs[2 + arg].at[level, :, pl.ds(h * D, D)],
                    )
            else:
                copy(R.fin[g].at[pl.ds(at, n), :], R.outs[2 + arg].at[level])
    zero = lax.axis_index("zero")
    for c in smalls:
        c.wait()
    small = [R.small[level] for level in range(2)]
    for arg, row in VECS:
        n = R.outs[2 + arg].shape[1]
        x = jnp.concatenate([s[row : row + 1, :] for s in small], axis=0)
        if row == BU0:
            x1 = jnp.concatenate([s[row + 1 : row + 2, :] for s in small], axis=0)
            x = jnp.where(zero * n < D, x, x1)
        x = pltpu.roll(x, lax.rem(D - lax.rem(zero * n, D), D), axis=1)
        R.outs[2 + arg][...] = x[:, :n]
    for c in copies:
        c.wait()


def make_fused(n_dp, n_zero, params):
    places, sizes, pieces = group_layout(n_dp, n_zero)
    dma = pltpu.SemaphoreType.DMA
    any_ = pl.BlockSpec(memory_space=pl.ANY)
    order, scratch = [], []

    def add(name, shape):
        order.append(name)
        scratch.append(shape)

    n_params = len(params)
    out_shape = [VM((TOK, D), F32)] * 2 + [VM((n_dp, p, D), F32) for p in pieces]
    ls, ts = list(LAYER_SCRATCH), [n for n in TMP_SCRATCH if n != "A2"]
    for level in range(2):
        for n in ls:
            add(("layer", level, n), VM(*LAYER_SCRATCH[n]))
    for n in ts:
        add(("temp", n), VM(*TMP_SCRATCH[n]))
    add("lengths", pltpu.SMEM((SEGS,), jnp.int32))
    add("A2", VM(*TMP_SCRATCH["A2"]))
    add("Y", VM((TOK + 768, D), F32))
    add("nodes_v", VM((TOK, D), F32))
    add("cot_v", VM((TOK, D), F32))
    for i, (arg, _) in enumerate(VECS):
        add(("stage", i), VM(params[arg].shape, F32))
    for n in NAMES:
        rows, cols = shard(n, n_zero)
        add(("weights", n), VM((2, rows * n_zero, cols), F32))
    add("vec_own", VM((2, SMALL, D), F32))
    add("vec_in", VM((n_zero - 1, 2, SMALL, D), F32))
    add("vec", VM((2, SMALL, D), F32))
    for g in range(NG):
        add(("gsend", g), VM((n_zero, sizes[g], D), F32))
        add(("gzero", g), VM((n_zero - 1, sizes[g], D), F32))
        add(("gred", g), VM((n_dp, pieces[g], D), F32))
        add(("gdp", g), VM((n_dp - 1, pieces[g], D), F32))
        add(("gfin", g), VM((n_dp, pieces[g], D), F32))
    add("stage_sem", dma((len(VECS),)))
    add("io_sem", dma((5 + NG,)))
    add("own_sem", dma((2, 6)))
    add("w_send", dma((2, 6, n_zero - 1)))
    add("w_recv", dma((2, 6, n_zero - 1)))
    add("vec_send", dma((n_zero - 1,)))
    add("vec_recv", dma((n_zero - 1,)))
    for n, m in (("z", n_zero), ("d", n_dp), ("f", n_dp)):
        add(n + "_send", dma((NG, m - 1)))
        add(n + "_recv", dma((NG, m - 1)))

    def body(*refs):
        lengths_in, nodes, cot = refs[:3]
        pr = refs[3 : 3 + n_params]
        outs = refs[3 + n_params : 5 + NG + n_params]
        rest = refs[5 + NG + n_params :]
        simple = dict(lengths_in=lengths_in, nodes=nodes, cotangent=cot, params=pr, out=outs[0], gx=outs[1], fin_out=outs[2:])
        layers, temps = [{}, {}], {}
        simple.update(layers=layers, temps=temps, stage=[None] * len(VECS), weights={})
        for n in ("gsend", "gzero", "gred", "gdp", "gfin"):
            simple[n] = [None] * NG
        for key, ref in zip(order, rest):
            if isinstance(key, str):
                simple[key] = ref
            elif key[0] == "layer":
                layers[key[1]][key[2]] = ref
            elif key[0] == "temp":
                temps[key[1]] = ref
            else:
                simple[key[0]][key[1]] = ref
        fused_kernel(n_dp, n_zero, list(simple), *simple.values())

    call = pl.pallas_call(
        body,
        out_shape=out_shape,
        in_specs=[any_] * (3 + n_params),
        out_specs=[any_] * (2 + NG),
        scratch_shapes=scratch,
        compiler_params=pltpu.CompilerParams(
            collective_id=0, has_side_effects=True, vmem_limit_bytes=56 * 1024 * 1024
        ),
    )
    return call


def make_finish(n_dp, n_zero, params):
    places, sizes, pieces = group_layout(n_dp, n_zero)
    any_ = pl.BlockSpec(memory_space=pl.ANY)
    vmem = pl.BlockSpec(memory_space=pltpu.VMEM)
    out_shape = [jax.ShapeDtypeStruct((TOK, D), F32)] * 2
    out_shape += [jax.ShapeDtypeStruct(p.shape, F32) for p in params]
    weights = set(ARG.values())
    out_specs = [any_] * 2 + [any_ if i in weights else vmem for i in range(len(params))]

    def body(*refs):
        out, gx = refs[:2]
        fin = refs[2 : 2 + NG]
        outs = refs[2 + NG : 4 + NG + len(params)]
        rest = refs[4 + NG + len(params) :]
        simple = dict(out=out, gx=gx, fin=fin, outs=outs, small=rest[0], sem=rest[1], small_sem=rest[2])
        finish_kernel(n_dp, n_zero, list(simple), *simple.values())

    call = pl.pallas_call(
        body,
        out_shape=out_shape,
        in_specs=[any_] * (2 + NG),
        out_specs=out_specs,
        scratch_shapes=[
            VM((2, SMALL, D), F32),
            pltpu.SemaphoreType.DMA((18,)),
            pltpu.SemaphoreType.DMA((2,)),
        ],
        compiler_params=pltpu.CompilerParams(vmem_limit_bytes=16 * 1024 * 1024),
    )
    return lambda *xs: call(*[pltpu.with_memory_space_constraint(x, pltpu.VMEM) for x in xs])


def solution(mesh):
    n_dp, n_zero = mesh.shape["dp"], mesh.shape["zero"]
    wide, flat = P(None, "zero", None), P(None, "zero")
    params = (wide,) * 4 + (flat,) * 8 + (wide, flat, wide, flat)
    rows = P(("dp", "zero"), None)

    def local(nodes, cotangent, lengths, *params):
        out, gx, *fins = make_fused(n_dp, n_zero, params)(lengths, nodes, cotangent, *params)
        fins = [f.reshape(-1, D) for f in fins]
        return tuple(make_finish(n_dp, n_zero, params)(out, gx, *fins))

    return jax.shard_map(
        local,
        mesh=mesh,
        in_specs=(rows, rows, P(("dp", "zero"))) + params,
        out_specs=(rows, rows) + params,
        check_vma=False,
    )
```

```python
import jax
import jax.numpy as jnp
from jax import lax
from jax.experimental import pallas as pl
from jax.experimental.pallas import tpu as pltpu
from jax.sharding import PartitionSpec as P

D=128; FF=256; SEGS=4; BLK=512; TOK=2048; HD=32
F32=jnp.float32; BF=jnp.bfloat16
VM=pltpu.VMEM

def split(x):
    hi=x.astype(BF); lo=(x-hi.astype(F32)).astype(BF)
    return hi,lo
def cat0(*x): return jnp.concatenate(x,axis=0)
def cat1(*x): return jnp.concatenate(x,axis=1)
def pack(x):
    return cat1(*split(x))
def quad(x):
    p=pack(x)
    return cat0(p,p)
def quad_t(x):
    h,l=split(x)
    return cat0(cat1(h,h),cat1(l,l))
def mm(a,b):
    return jnp.dot(a,b,preferred_element_type=F32)
def tn(a,b):
    return lax.dot_general(a,b,(((0,),(0,)),((),())),preferred_element_type=F32)
def nt(a,b):
    return lax.dot_general(a,b,(((1,),(1,)),((),())),preferred_element_type=F32)
def halves(r):
    n=r.shape[1]//2
    return r[:,:n]+r[:,n:]
def quads(r):
    m=r.shape[0]//2
    return halves(r[:m]+r[m:])
def part(x):
    return jnp.sum(x.reshape(x.shape[0]//8,8,x.shape[1]),axis=0)
def one(x):
    return jnp.sum(x,axis=0,keepdims=True)
def group_mask():
    r=lax.broadcasted_iota(jnp.int32,(D,D),0)//HD
    c=lax.broadcasted_iota(jnp.int32,(D,D),1)//HD
    return r==c
def center(x,a1):
    h=x.astype(BF); r=x-h.astype(F32); m=r.astype(BF); lo=(r-m.astype(F32)).astype(BF)
    return x-(mm(h,a1)+mm(m,a1)+mm(lo,a1))

BQ,BK,BV,BO,GK,SK,GV,SV,BD,BU0,BU1=range(11)
AUG=D+16

LAYER_SCRATCH=dict(
    X=((TOK,2*D),BF), H=((TOK,D),F32), NK=((TOK,D),F32), NV=((TOK,D),F32), RK=((TOK,D),F32), RV=((TOK,D),F32),
    KN=((TOK,2*D),BF), VN=((TOK,2*D),BF), MD=((TOK,2*D),BF), ACT=((TOK,2*FF),BF), DG=((TOK,FF),F32),
    WKV=((2*D,4*D),BF), WUP=((2*D,2*FF),BF), WDN=((2*FF,2*D),BF), WDNT=((2*FF,2*D),BF), WUPT=((2*D,2*FF),BF),
    WKVT=((2*D,4*D),BF), WO2=((2*D,2*D),BF), WOT2=((2*D,2*D),BF), WQA=((AUG,2*D),BF),
    SP=((SEGS*D,2*D),BF), TP=((2*D,SEGS*D),BF), UT2=((SEGS,2*D,2*D),BF), U2=((SEGS,2*D,2*D),BF), UB=((SEGS,8,D),F32),
    CB=((8,D),F32),
)
TMP_SCRATCH=dict(
    E=((TOK,D),F32), ED=((TOK,2*D),BF), EP=((TOK,2*FF),BF), EM=((TOK,D),F32), EO=((TOK,2*D),BF), FKV=((TOK,4*D),BF),
    A2=((2*D,D),BF),
)

def prep_kv(L,w,vec,A2):
    a1=A2[0:D,:]
    b8=cat0(vec[BK:BV+1,:],jnp.zeros((6,D),F32))
    L['CB'][...]=center(b8,a1)
    wk=center(w['k'][...],a1); wv=center(w['v'][...],a1)
    kh,kl=split(wk); vh,vl=split(wv)
    kv=cat1(kh,vh,kl,vl)
    L['WKV'][0:D,:]=kv; L['WKV'][D:,:]=kv
    L['WKVT'][0:D,:]=cat1(kh,kh,vh,vh); L['WKVT'][D:,:]=cat1(kl,kl,vl,vl)

def prep_qo(L,w,vec):
    wo=w['o'][...]
    L['WO2'][...]=quad(wo); L['WOT2'][...]=quad_t(wo)
    L['WQA'][0:D,:]=pack(w['q'][...])
    L['WQA'][D:,:]=pack(cat0(vec[BQ:BQ+1,:],jnp.zeros((15,D),F32)))

def prep_ff(L,w):
    up=w['up'][...]
    L['WUP'][...]=quad(up)
    dn=w['dn'][...]
    L['WDN'][...]=quad(dn)

def prep_back(L,w):
    L['WUPT'][...]=quad_t(w['up'][...])
    L['WDNT'][...]=quad_t(w['dn'][...])

def fwd_a(L,vec,A2,live,r0,n,fresh):
    rows=pl.ds(r0,n)
    if fresh:
        x=pack(L['H'][rows,:])
        L['X'][rows,:]=x
    else:
        x=L['X'][rows,:]
    r=mm(x,L['WKV'][...])
    a2=A2[...]
    lv=live(r0,n)
    for i,(N,R,O,g,s) in enumerate((('NK','RK','KN',GK,SK),('NV','RV','VN',GV,SV))):
        c=r[:,i*D:(i+1)*D]+r[:,(i+2)*D:(i+3)*D]+L['CB'][i:i+1,:]
        rs=lax.rsqrt(mm(pack(c*c),a2)+1e-5)
        nn=c*rs
        L[R][rows,:]=rs; L[N][rows,:]=nn
        y=jnp.where(lv,nn*vec[g:g+1,:]+vec[s:s+1,:],0.0)
        L[O][rows,:]=pack(y)

def fwd_s(L,vec,gm,inv):
    for s in range(SEGS):
        rows=pl.ds(s*BLK,BLK)
        S=jnp.where(gm,quads(tn(L['KN'][rows,:],L['VN'][rows,:]))*inv[s],0.0)
        L['SP'][s*D:(s+1)*D,:]=pack(S)
    T=halves(mm(L['SP'][...],L['WO2'][...]))
    ts=[T[s*D:(s+1)*D] for s in range(SEGS)]
    sp=[split(t) for t in ts]
    for s in range(SEGS):
        L['TP'][0:D,s*D:(s+1)*D]=sp[s][0]; L['TP'][D:,s*D:(s+1)*D]=sp[s][1]
    row=cat1(*[x for hl in sp for x in hl])
    u=mm(L['WQA'][...],cat0(row,row))
    for s in range(SEGS):
        us=halves(u[:,s*2*D:(s+1)*2*D])
        L['UB'][s]=us[D:D+8]+vec[BO:BO+1,:]
        h,l=split(us[:D])
        p=cat1(h,l)
        L['U2'][s,0:D,:]=p; L['U2'][s,D:,:]=p
        L['UT2'][s,0:D,:]=cat1(h,h); L['UT2'][s,D:,:]=cat1(l,l)

def fwd_c1(L,s,r0,n):
    rows=pl.ds(r0,n)
    mid=L['H'][rows,:]+halves(mm(L['X'][rows,:],L['U2'][s]))+L['UB'][s,0:1,:]
    L['MD'][rows,:]=pack(mid)
    return mid

def fwd_c2(L,vec,r0,n):
    rows=pl.ds(r0,n)
    bu=cat1(vec[BU0:BU0+1,:],vec[BU1:BU1+1,:])
    z=halves(mm(L['MD'][rows,:],L['WUP'][...]))+bu
    z2=z*z
    c0=0.7978845608028654
    t=jnp.tanh(z*(c0+(c0*0.044715)*z2))
    p=0.5*t+0.5
    act=z*p
    L['DG'][rows,:]=p+act*(1.0-p)*((2*c0)+(6*c0*0.044715)*z2)
    L['ACT'][rows,:]=pack(act)

def fwd_c3(L,vec,OUT,mid,r0,n):
    rows=pl.ds(r0,n)
    OUT[rows,:]=mid+halves(mm(L['ACT'][rows,:],L['WDN'][...]))+vec[BD:BD+1,:]

def bwd_a1(L,Tm,r0,n,fresh):
    rows=pl.ds(r0,n)
    if fresh:
        e=Tm['E'][rows,:]
        ed=pack(e); Tm['ED'][rows,:]=ed
        se=part(e)
    else:
        ed=Tm['ED'][rows,:]; se=None
    ep=halves(nt(ed,L['WDNT'][...]))*L['DG'][rows,:]
    Tm['EP'][rows,:]=pack(ep)
    return se,part(ep)

def bwd_a2(L,Tm,r0,n):
    rows=pl.ds(r0,n)
    em=Tm['E'][rows,:]+halves(nt(Tm['EP'][rows,:],L['WUPT'][...]))
    Tm['EM'][rows,:]=em
    Tm['EO'][rows,:]=pack(em)
    return part(em)

def bwd_s1(L,Tm,c):
    hs=[]
    for s in range(SEGS):
        rows=pl.ds(s*BLK,BLK)
        H=quads(tn(L['X'][rows,:],Tm['EO'][rows,:]))
        hs.append(split(cat0(H,one(c[s]),jnp.zeros((15,D),F32))))
    return hs

def bwd_s2(L,hs):
    P=tn(L['WQA'][...],cat1(*[x for hl in hs for x in hl]))
    P=P[:D]+P[D:]
    pp=cat0(*[pack(halves(P[:,s*2*D:(s+1)*2*D])) for s in range(SEGS)])
    return pp

def bwd_s3(L,gm,inv,pp):
    es=halves(nt(pp,L['WOT2'][...]))
    out=[]
    for s in range(SEGS):
        e=jnp.where(gm,es[s*D:(s+1)*D]*inv[s],0.0)
        h,l=split(e); p=cat1(h,l)
        out.append((cat0(cat1(h,h),cat1(l,l)),cat0(p,p)))
    return out

def bwd_s4(L,hs,pp):
    go=quads(tn(L['SP'][...],pp))
    gq=halves(nt(cat0(cat1(*[h for h,l in hs]),cat1(*[l for h,l in hs])),L['TP'][...]))
    gq=gq[:AUG]+gq[AUG:]
    return gq[:D],gq[D:D+1],go

def bwd_b(L,vec,Tm,A2,es,r0,n,i):
    rows=pl.ds(r0,n)
    N,R,O,g,dot=(('NK','RK','VN',GK,nt),('NV','RV','KN',GV,mm))[i]
    en=halves(dot(L[O][rows,:],es))
    nn=L[N][rows,:]
    m=en*vec[g:g+1,:]
    mn=m*nn
    av=mm(pack(mn),A2[...])
    f=L[R][rows,:]*(m-nn*av)
    Tm['FKV'][rows,i*2*D:(i+1)*2*D]=pack(f)
    return part(en),part(en*nn),part(f)

def bwd_x(L,Tm,DX,s,r0,n):
    rows=pl.ds(r0,n)
    DX[rows,:]=Tm['EM'][rows,:]+halves(nt(Tm['FKV'][rows,:],L['WKVT'][...])+nt(Tm['EO'][rows,:],L['UT2'][s]))


MESH = pl.DeviceIdType.MESH
NAMES = ("k", "v", "q", "o", "up", "dn")
ARG = dict(q=0, k=1, v=2, o=3, up=12, dn=14)
VECS = ((4, BQ), (5, BK), (6, BV), (7, BO), (8, GK), (9, SK), (10, GV), (11, SV), (15, BD), (13, BU0))
SMALL = 16
GROUPS = (
    (((1, "up"), (1, "dn")), True),
    (((1, "q"), (1, "o")), True),
    (((1, "k"), (1, "v"), (1, "small")), True),
    (((0, "up"), (0, "dn")), True),
    (((0, "q"), (0, "o")), True),
    (((0, "k"),), False),
    (((0, "small"),), True),
    (((0, "v"),), False),
)
PAIR = 2
NG = len(GROUPS)


def shard(name, n_zero):
    if name == "dn":
        return FF // n_zero, D
    return D // n_zero, FF if name == "up" else D


def group_layout(n_zero):
    places, sizes, pieces = {}, [], []
    for g, (members, halved) in enumerate(GROUPS):
        at = 0
        for item in members:
            places[item] = (g, at)
            if item[1] == "small":
                at += SMALL
            else:
                rows, cols = shard(item[1], n_zero)
                at += rows * cols // D
        at = -(-at // 16) * 16
        sizes.append(at)
        pieces.append(at // PAIR if halved else at)
    return places, sizes, pieces


class Names:
    pass


def fused_kernel(n_dp, n_zero, order, *refs):
    R = Names()
    for name, ref in zip(order, refs):
        setattr(R, name, ref)
    places, sizes, pieces = group_layout(n_zero)
    dp, zero = lax.axis_index("dp"), lax.axis_index("zero")
    zpeer = [None] + [lax.rem(zero + k, n_zero) for k in range(1, n_zero)]
    fast, slow, n_slow = lax.rem(dp, PAIR), dp // PAIR, n_dp // PAIR
    n_plane = PAIR * n_zero
    me = fast * n_zero + zero
    ppeer = [None] + [lax.rem(me + k, n_plane) for k in range(1, n_plane)]
    speer = [None] + [lax.rem(slow + k, n_slow) for k in range(1, n_slow)]
    sfrom = [None] + [lax.rem(slow + n_slow - k, n_slow) for k in range(1, n_slow)]
    pfrom = [None] + [lax.rem(me + n_plane - k, n_plane) for k in range(1, n_plane)]
    other = PAIR - 1 - fast

    def in_plane(k):
        return (slow * PAIR + ppeer[k] // n_zero, lax.rem(ppeer[k], n_zero))

    def along(k):
        return (speer[k] * PAIR + fast, zero)

    barrier = pltpu.get_barrier_semaphore()
    for k in range(1, n_slow):
        pl.semaphore_signal(barrier, inc=1, device_id=along(k), device_id_type=MESH)
    for k in range(1, n_plane):
        pl.semaphore_signal(barrier, inc=1, device_id=in_plane(k), device_id_type=MESH)

    len_in = pltpu.make_async_copy(R.lengths_in, R.lengths, R.io_sem.at[2])
    len_in.start()
    small_in = []
    for i, (arg, _) in enumerate(VECS):
        c = pltpu.make_async_copy(R.params[arg], R.stage[i], R.stage_sem.at[i])
        c.start()
        small_in.append(c)
    nodes_in = pltpu.make_async_copy(R.nodes, R.nodes_v, R.io_sem.at[0])
    nodes_in.start()

    def rows_of(name, who):
        n = shard(name, n_zero)[0]
        return pl.ds(pl.multiple_of(who * n, n), n)

    own = {}
    for level in range(2):
        for i, name in enumerate(NAMES):
            own[level, name] = pltpu.make_async_copy(
                R.params[ARG[name]].at[level],
                R.weights[name].at[level, rows_of(name, zero), :],
                R.own_sem.at[level, i],
            )
    for level in range(2):
        for name in NAMES:
            own[level, name].start()
    cot_in = pltpu.make_async_copy(R.cotangent, R.cot_v, R.io_sem.at[1])
    cot_in.start()

    pl.semaphore_wait(barrier, n_slow - 1 + n_plane - 1)

    n_x = n_zero // 2
    mate = zero + 1 - 2 * lax.rem(zero, 2)
    xpeer = [None] + [lax.rem(zero + 2 * k, n_zero) for k in range(1, n_x)]
    xfrom = [None] + [lax.rem(zero + n_zero - 2 * k, n_zero) for k in range(1, n_x)]
    mate_from = [None] + [lax.rem(mate + n_zero - 2 * k, n_zero) for k in range(1, n_x)]

    def part_of(level, name, who):
        if name == "vec":
            return R.vec_in.at[who]
        return R.weights[name].at[level, rows_of(name, who), :]

    def own_part(level, name):
        return R.vec_own if name == "vec" else R.params[ARG[name]].at[level]

    def place(level, name):
        return 12 if name == "vec" else level * 6 + NAMES.index(name)

    def x_copy(level, name, k, who):
        i = place(level, name)
        return pltpu.make_async_remote_copy(
            src_ref=own_part(level, name),
            dst_ref=part_of(level, name, who),
            send_sem=R.x_send.at[i, k - 1],
            recv_sem=R.x_recv.at[i, k - 1],
            device_id=(dp, xpeer[k]),
            device_id_type=MESH,
        )

    def mate_copy(level, name, k, who):
        i = place(level, name)
        return pltpu.make_async_remote_copy(
            src_ref=own_part(level, name) if k == 0 else part_of(level, name, xfrom[k]),
            dst_ref=part_of(level, name, who),
            send_sem=R.m_send.at[i, k],
            recv_sem=R.m_recv.at[i, k],
            device_id=(dp, mate),
            device_id_type=MESH,
        )

    def send_weights(level, names):
        for name in names:
            for k in range(1, n_x):
                x_copy(level, name, k, zero).start()
        for name in names:
            mate_copy(level, name, 0, zero).start()

    def relay_weights(level, names):
        for name in names:
            for k in range(1, n_x):
                x_copy(level, name, k, xfrom[k]).wait_recv()
                mate_copy(level, name, k, xfrom[k]).start()

    def take_weights(level, names):
        for name in names:
            if name != "vec":
                own[level, name].wait()
            mate_copy(level, name, 0, mate).wait_recv()
            for k in range(1, n_x):
                mate_copy(level, name, k, mate_from[k]).wait_recv()

    send_weights(0, ("k", "v"))

    for c in small_in:
        c.wait()
    lane = lax.broadcasted_iota(jnp.int32, (2, D), 1)
    R.vec_own[...] = jnp.zeros((2, SMALL, D), F32)
    for i, (arg, row) in enumerate(VECS):
        x = R.stage[i][...]
        n = x.shape[1]
        x = jnp.concatenate([x, jnp.zeros((2, D - n), F32)], axis=1)
        x = pltpu.roll(x, lax.rem(zero * n, D), axis=1)
        if row != BU0:
            R.vec_own[:, row, :] = x
        else:
            first = zero * n < D
            R.vec_own[:, row, :] = jnp.where(first, x, 0.0)
            R.vec_own[:, row + 1, :] = jnp.where(first, 0.0, x)

    send_weights(0, ("vec",))

    len_in.wait()
    gm = group_mask()
    a = jnp.where(gm, 1.0 / HD, 0.0).astype(BF)
    R.A2[0:D, :] = a
    R.A2[D:, :] = a
    ln = [R.lengths[i] for i in range(SEGS)]
    st = [0]
    for i in range(SEGS):
        st.append(st[-1] + ln[i])
    inv = [1.0 / (jnp.full((1, D), ln[s], jnp.int32).astype(F32)) for s in range(SEGS)]

    def live(r0, n):
        s = r0 // BLK
        return lax.broadcasted_iota(jnp.int32, (n, D), 0) + (r0 - s * BLK) < ln[s]

    Ls, Tm = R.layers, R.temps
    Tm["A2"] = R.A2
    for y in (R.Y, R.Y2):
        y[TOK:, :] = jnp.zeros((y.shape[0] - TOK, D), F32)
    nodes_in.wait()
    for s in range(SEGS):
        x = R.nodes_v[pl.ds(st[s], BLK), :]
        Ls[0]["H"][s * BLK : (s + 1) * BLK, :] = x
        Ls[0]["X"][s * BLK : (s + 1) * BLK, :] = pack(x)
    cot_in.wait()
    sum_e = zero8 = jnp.zeros((8, D), F32)
    for s in range(SEGS):
        x = jnp.where(live(s * BLK, BLK), R.cot_v[pl.ds(st[s], BLK), :], 0.0)
        Tm["E"][s * BLK : (s + 1) * BLK, :] = x
        Tm["ED"][s * BLK : (s + 1) * BLK, :] = pack(x)
        sum_e = sum_e + part(x)

    send_weights(0, ("q", "o", "up", "dn"))
    relay_weights(0, ("k", "v", "vec"))
    send_weights(1, NAMES)
    take_weights(0, ("vec",))
    vecs = []
    for level in range(2):
        x = R.vec_own[level]
        for k in range(1, n_zero):
            x = x + R.vec_in[zpeer[k], level]
        R.vec[level] = x
        vecs.append(R.vec.at[level])

    tiles = [(s, s * BLK) for s in range(SEGS)]

    def pipe(stages, hook=None):
        kept = [None] * len(tiles)
        for t in range(len(tiles) + len(stages) - 1):
            for j, stage in enumerate(stages):
                if 0 <= t - j < len(tiles):
                    kept[t - j] = stage(tiles[t - j], kept[t - j])
            if hook is not None and t == 2:
                hook()
        return kept

    for level in range(2):
        L, vec = Ls[level], vecs[level]
        dst = Ls[1]["H"] if level == 0 else R.Y
        w = {n: R.weights[n].at[level] for n in NAMES}
        take_weights(level, ("k", "v"))
        prep_kv(L, w, vec, R.A2)
        for s, r in tiles:
            fwd_a(L, vec, R.A2, live, r, BLK, level == 1)
            if level == 0 and s == 0:
                relay_weights(0, ("q", "o", "up", "dn"))
        take_weights(level, ("q", "o"))
        prep_qo(L, w, vec)
        fwd_s(L, vec, gm, inv)
        take_weights(level, ("up", "dn"))
        prep_ff(L, w)
        def middle(tile, _):
            return fwd_c1(L, *tile, BLK)

        def hidden(tile, mid):
            fwd_c2(L, vec, tile[1], BLK)
            return mid

        def close(tile, mid):
            fwd_c3(L, vec, dst, mid, tile[1], BLK)

        pipe([middle, hidden, close], (lambda: relay_weights(1, NAMES)) if level == 0 else None)

    def put(level, name, g):
        grp, at = places[level, name]
        n = shard(name, n_zero)[0]
        for p in range(n_zero):
            part_p = g[p * n : (p + 1) * n]
            if name == "up":
                R.gsend[grp][p, at : at + n, :] = part_p[:, :D]
                R.gsend[grp][p, at + n : at + 2 * n, :] = part_p[:, D:]
            else:
                R.gsend[grp][p, at : at + n, :] = part_p

    def plane_copy(grp, k, who):
        rows, src = pieces[grp], R.gsend[grp].at[lax.rem(ppeer[k], n_zero)]
        if GROUPS[grp][1]:
            src = src.at[pl.ds(pl.multiple_of(ppeer[k] // n_zero * rows, 8), rows), :]
        return pltpu.make_async_remote_copy(
            src_ref=src,
            dst_ref=R.gplane[grp].at[who],
            send_sem=R.p_send.at[grp, k - 1],
            recv_sem=R.p_recv.at[grp, k - 1],
            device_id=in_plane(k),
            device_id_type=MESH,
        )

    def slow_copy(grp, k, who):
        return pltpu.make_async_remote_copy(
            src_ref=R.gslow[grp].at[slow],
            dst_ref=R.gslow[grp].at[who],
            send_sem=R.s_send.at[grp, k - 1],
            recv_sem=R.s_recv.at[grp, k - 1],
            device_id=along(k),
            device_id_type=MESH,
        )

    def half_of(grp, who):
        rows = pieces[grp]
        return R.fin_out[grp].at[pl.ds(pl.multiple_of(who * rows, 8), rows), :]

    def pair_copy(grp, who):
        return pltpu.make_async_remote_copy(
            src_ref=half_of(grp, fast),
            dst_ref=half_of(grp, who),
            send_sem=R.f_send.at[grp],
            recv_sem=R.f_recv.at[grp],
            device_id=(slow * PAIR + other, zero),
            device_id_type=MESH,
        )

    def start_plane(grp):
        for k in range(1, n_plane):
            plane_copy(grp, k, me).start()

    def start_slow(grp):
        rows = pieces[grp]
        at = pl.multiple_of(fast * rows, 8) if GROUPS[grp][1] else 0
        R.gplane[grp][me] = R.gsend[grp][zero, pl.ds(at, rows), :]
        for k in range(1, n_plane):
            plane_copy(grp, k, pfrom[k]).wait_recv()
        x = R.gplane[grp][0]
        for j in range(1, n_plane):
            x = x + R.gplane[grp][j]
        R.gslow[grp][slow] = x
        for k in range(1, n_slow):
            slow_copy(grp, k, slow).start()

    def start_pair(grp):
        for k in range(1, n_slow):
            slow_copy(grp, k, sfrom[k]).wait_recv()
        x = R.gslow[grp][0]
        for j in range(1, n_slow):
            x = x + R.gslow[grp][j]
        if GROUPS[grp][1]:
            R.fin_out[grp][pl.ds(pl.multiple_of(fast * pieces[grp], 8), pieces[grp]), :] = x
            pair_copy(grp, fast).start()
        else:
            R.fin_out[grp][...] = x

    def end_pair(grp):
        if GROUPS[grp][1]:
            pair_copy(grp, other).wait_recv()

    shift = [jnp.minimum(BLK * s - st[s], (BLK - 256) * s) for s in range(SEGS)]

    def unpack(Y, base):
        lo, hi = (0, 256, 512, 768), (512, 1024, 1536, 2048)
        step = 256
        for t0 in range(0, TOK, step):
            it = lax.broadcasted_iota(jnp.int32, (step, D), 0) + t0
            x = base[t0 : t0 + step, :]
            for s in range(SEGS):
                if t0 < hi[s] and t0 + step > lo[s]:
                    y = Y[pl.ds(t0 + shift[s], step), :]
                    x = jnp.where((it >= st[s]) & (it < st[s + 1]), y, x)
            base[t0 : t0 + step, :] = x

    for level in (1, 0):
        L, vec = Ls[level], vecs[level]
        w = {n: R.weights[n].at[level] for n in NAMES}
        prep_back(L, w)

        def feed(tile, _):
            return bwd_a1(L, Tm, tile[1], BLK, level == 0)

        def after(tile, sums):
            return (*sums, bwd_a2(L, Tm, tile[1], BLK))

        sums = pipe([feed, after])
        sb = sum_e if level == 1 else sum((x[0] for x in sums), zero8)
        su = sum((x[1] for x in sums), jnp.zeros((8, FF), F32))
        sc = [x[2] for x in sums]
        put(level, "dn", quads(tn(L["ACT"][...], Tm["ED"][...])))
        put(level, "up", quads(tn(L["MD"][...], Tm["EP"][...])))
        start_plane(0 if level == 1 else 3)
        if level == 0:
            start_slow(0)
        hs = bwd_s1(L, Tm, sc)
        pp = bwd_s2(L, hs)
        es = bwd_s3(L, gm, inv, pp)
        gq, gbq, go = bwd_s4(L, hs, pp)
        put(level, "q", gq)
        put(level, "o", go)
        start_plane(1 if level == 1 else 4)
        if level == 0:
            start_slow(1)
        a1 = R.A2[0:D, :]
        ss = [zero8] * 6

        def key_value(i):
            for s, r in tiles:
                o = bwd_b(L, vec, Tm, R.A2, es[s][i], r, BLK, i)
                for j in range(3):
                    ss[3 * i + j] = ss[3 * i + j] + o[j]

        key_value(0)
        if level == 0:
            put(level, "k", center(quads(tn(L["X"][...], Tm["FKV"][:, : 2 * D])), a1))
            start_plane(5)
            start_slow(2)
        key_value(1)
        rows = [jnp.zeros((1, D), F32)] * SMALL
        rows[BQ], rows[BK], rows[BV] = gbq, one(center(ss[2], a1)), one(center(ss[5], a1))
        rows[BO] = one(sc[0] + sc[1] + sc[2] + sc[3])
        rows[SK], rows[GK], rows[SV], rows[GV] = one(ss[0]), one(ss[1]), one(ss[3]), one(ss[4])
        rows[BD] = one(sb)
        u = one(su)
        rows[BU0], rows[BU1] = u[:, :D], u[:, D:]
        small = jnp.concatenate(rows, axis=0)
        grp, at = places[level, "small"]
        for p in range(n_zero):
            R.gsend[grp][p, at : at + SMALL, :] = small
        if level == 1:
            gkv = tn(L["X"][...], Tm["FKV"][...])
            gkv = gkv[0:D] + gkv[D:]
            put(level, "k", center(halves(gkv[:, : 2 * D]), a1))
            put(level, "v", center(halves(gkv[:, 2 * D :]), a1))
            start_plane(2)
        else:
            start_plane(6)
            put(level, "v", center(quads(tn(L["X"][...], Tm["FKV"][:, 2 * D :])), a1))
            start_plane(7)
            start_slow(3)
            start_pair(0)
            start_pair(1)
        dst = Tm["E"] if level == 1 else R.Y2
        for s, r in tiles:
            bwd_x(L, Tm, dst, s, r, BLK)

    start_slow(4)
    start_pair(2)
    unpack(R.Y, R.nodes_v)
    store_out = pltpu.make_async_copy(R.nodes_v, R.out, R.io_sem.at[3])
    store_out.start()
    start_slow(5)
    start_slow(6)
    unpack(R.Y2, R.cot_v)
    store_gx = pltpu.make_async_copy(R.cot_v, R.gx, R.io_sem.at[4])
    store_gx.start()
    start_slow(7)
    for g in (3, 4, 6, 5, 7):
        start_pair(g)
    for g in range(NG):
        end_pair(g)

    for level, names in ((0, NAMES + ("vec",)), (1, NAMES)):
        for name in names:
            mate_copy(level, name, 0, zero).wait_send()
            for k in range(1, n_x):
                x_copy(level, name, k, zero).wait_send()
                mate_copy(level, name, k, xfrom[k]).wait_send()
    for g in range(NG):
        for k in range(1, n_plane):
            plane_copy(g, k, me).wait_send()
        for k in range(1, n_slow):
            slow_copy(g, k, slow).wait_send()
        if GROUPS[g][1]:
            pair_copy(g, fast).wait_send()
    store_out.wait()
    store_gx.wait()


def finish_kernel(n_dp, n_zero, order, *refs):
    R = Names()
    for name, ref in zip(order, refs):
        setattr(R, name, ref)
    places, sizes, pieces = group_layout(n_zero)
    copies = []

    def copy(src, dst):
        c = pltpu.make_async_copy(src, dst, R.sem.at[len(copies)])
        c.start()
        copies.append(c)

    smalls = []
    for level in range(2):
        g, at = places[level, "small"]
        c = pltpu.make_async_copy(R.fin[g].at[pl.ds(at, SMALL), :], R.small.at[level], R.small_sem.at[level])
        c.start()
        smalls.append(c)
    half = TOK // 2
    for i in range(2):
        copy(R.out.at[pl.ds(i * half, half), :], R.outs[0].at[pl.ds(i * half, half), :])
        copy(R.gx.at[pl.ds(i * half, half), :], R.outs[1].at[pl.ds(i * half, half), :])
    for name, arg in ARG.items():
        for level in range(2):
            g, at = places[level, name]
            n = shard(name, n_zero)[0]
            if name == "up":
                for h in range(2):
                    copy(
                        R.fin[g].at[pl.ds(at + h * n, n), :],
                        R.outs[2 + arg].at[level, :, pl.ds(h * D, D)],
                    )
            else:
                copy(R.fin[g].at[pl.ds(at, n), :], R.outs[2 + arg].at[level])
    zero = lax.axis_index("zero")
    for c in smalls:
        c.wait()
    small = [R.small[level] for level in range(2)]
    for arg, row in VECS:
        n = R.outs[2 + arg].shape[1]
        x = jnp.concatenate([s[row : row + 1, :] for s in small], axis=0)
        if row == BU0:
            x1 = jnp.concatenate([s[row + 1 : row + 2, :] for s in small], axis=0)
            x = jnp.where(zero * n < D, x, x1)
        x = pltpu.roll(x, lax.rem(D - lax.rem(zero * n, D), D), axis=1)
        R.outs[2 + arg][...] = x[:, :n]
    for c in copies:
        c.wait()


def make_fused(n_dp, n_zero, params):
    places, sizes, pieces = group_layout(n_zero)
    dma = pltpu.SemaphoreType.DMA
    any_ = pl.BlockSpec(memory_space=pl.ANY)
    order, scratch = [], []

    def add(name, shape):
        order.append(name)
        scratch.append(shape)

    n_params = len(params)
    out_shape = [VM((TOK, D), F32)] * 2 + [VM((p, D), F32) for p in sizes]
    ls, ts = list(LAYER_SCRATCH), [n for n in TMP_SCRATCH if n != "A2"]
    for level in range(2):
        for n in ls:
            add(("layer", level, n), VM(*LAYER_SCRATCH[n]))
    for n in ts:
        add(("temp", n), VM(*TMP_SCRATCH[n]))
    add("lengths", pltpu.SMEM((SEGS,), jnp.int32))
    add("A2", VM(*TMP_SCRATCH["A2"]))
    add("Y", VM((TOK + 768, D), F32))
    add("Y2", VM((TOK + 768, D), F32))
    add("nodes_v", VM((TOK, D), F32))
    add("cot_v", VM((TOK, D), F32))
    for i, (arg, _) in enumerate(VECS):
        add(("stage", i), VM(params[arg].shape, F32))
    for n in NAMES:
        rows, cols = shard(n, n_zero)
        add(("weights", n), VM((2, rows * n_zero, cols), F32))
    add("vec_own", VM((2, SMALL, D), F32))
    add("vec_in", VM((n_zero, 2, SMALL, D), F32))
    add("vec", VM((2, SMALL, D), F32))
    for g in range(NG):
        add(("gsend", g), VM((n_zero, sizes[g], D), F32))
        add(("gplane", g), VM((PAIR * n_zero, pieces[g], D), F32))
        add(("gslow", g), VM((n_dp // PAIR, pieces[g], D), F32))
    add("stage_sem", dma((len(VECS),)))
    add("io_sem", dma((5,)))
    add("own_sem", dma((2, 6)))
    for n, m in (("x", n_zero // 2 - 1), ("m", n_zero // 2)):
        add(n + "_send", dma((13, m)))
        add(n + "_recv", dma((13, m)))
    for n, m in (("p", PAIR * n_zero), ("s", n_dp // PAIR)):
        add(n + "_send", dma((NG, m - 1)))
        add(n + "_recv", dma((NG, m - 1)))
    add("f_send", dma((NG,)))
    add("f_recv", dma((NG,)))

    def body(*refs):
        lengths_in, nodes, cot = refs[:3]
        pr = refs[3 : 3 + n_params]
        outs = refs[3 + n_params : 5 + NG + n_params]
        rest = refs[5 + NG + n_params :]
        simple = dict(lengths_in=lengths_in, nodes=nodes, cotangent=cot, params=pr, out=outs[0], gx=outs[1], fin_out=outs[2:])
        layers, temps = [{}, {}], {}
        simple.update(layers=layers, temps=temps, stage=[None] * len(VECS), weights={})
        for n in ("gsend", "gplane", "gslow"):
            simple[n] = [None] * NG
        for key, ref in zip(order, rest):
            if isinstance(key, str):
                simple[key] = ref
            elif key[0] == "layer":
                layers[key[1]][key[2]] = ref
            elif key[0] == "temp":
                temps[key[1]] = ref
            else:
                simple[key[0]][key[1]] = ref
        fused_kernel(n_dp, n_zero, list(simple), *simple.values())

    call = pl.pallas_call(
        body,
        out_shape=out_shape,
        in_specs=[any_] * (3 + n_params),
        out_specs=[any_] * 2 + [pl.BlockSpec(memory_space=pltpu.VMEM)] * NG,
        scratch_shapes=scratch,
        compiler_params=pltpu.CompilerParams(
            collective_id=0, has_side_effects=True, vmem_limit_bytes=56 * 1024 * 1024
        ),
    )
    return call


def make_finish(n_dp, n_zero, params):
    places, sizes, pieces = group_layout(n_zero)
    any_ = pl.BlockSpec(memory_space=pl.ANY)
    vmem = pl.BlockSpec(memory_space=pltpu.VMEM)
    out_shape = [jax.ShapeDtypeStruct((TOK, D), F32)] * 2
    out_shape += [jax.ShapeDtypeStruct(p.shape, F32) for p in params]
    weights = set(ARG.values())
    out_specs = [any_] * 2 + [any_ if i in weights else vmem for i in range(len(params))]

    def body(*refs):
        out, gx = refs[:2]
        fin = refs[2 : 2 + NG]
        outs = refs[2 + NG : 4 + NG + len(params)]
        rest = refs[4 + NG + len(params) :]
        simple = dict(out=out, gx=gx, fin=fin, outs=outs, small=rest[0], sem=rest[1], small_sem=rest[2])
        finish_kernel(n_dp, n_zero, list(simple), *simple.values())

    call = pl.pallas_call(
        body,
        out_shape=out_shape,
        in_specs=[any_] * (2 + NG),
        out_specs=out_specs,
        scratch_shapes=[
            VM((2, SMALL, D), F32),
            pltpu.SemaphoreType.DMA((18,)),
            pltpu.SemaphoreType.DMA((2,)),
        ],
        compiler_params=pltpu.CompilerParams(vmem_limit_bytes=16 * 1024 * 1024),
    )
    return lambda *xs: call(*[pltpu.with_memory_space_constraint(x, pltpu.VMEM) for x in xs])


def solution(mesh):
    n_dp, n_zero = mesh.shape["dp"], mesh.shape["zero"]
    wide, flat = P(None, "zero", None), P(None, "zero")
    params = (wide,) * 4 + (flat,) * 8 + (wide, flat, wide, flat)
    rows = P(("dp", "zero"), None)

    def local(nodes, cotangent, lengths, *params):
        out, gx, *fins = make_fused(n_dp, n_zero, params)(lengths, nodes, cotangent, *params)
        return tuple(make_finish(n_dp, n_zero, params)(out, gx, *fins))

    return jax.shard_map(
        local,
        mesh=mesh,
        in_specs=(rows, rows, P(("dp", "zero"))) + params,
        out_specs=(rows, rows) + params,
        check_vma=False,
    )
```

```python
import jax
import jax.numpy as jnp
from jax import lax
from jax.experimental import pallas as pl
from jax.experimental.pallas import tpu as pltpu
from jax.sharding import PartitionSpec as P

D=128; FF=256; SEGS=4; BLK=512; TOK=2048; HD=32
F32=jnp.float32; BF=jnp.bfloat16
VM=pltpu.VMEM

def split(x):
    hi=x.astype(BF); lo=(x-hi.astype(F32)).astype(BF)
    return hi,lo
def cat0(*x): return jnp.concatenate(x,axis=0)
def cat1(*x): return jnp.concatenate(x,axis=1)
def pack(x):
    return cat1(*split(x))
def quad(x):
    p=pack(x)
    return cat0(p,p)
def quad_t(x):
    h,l=split(x)
    return cat0(cat1(h,h),cat1(l,l))
def mm(a,b):
    return jnp.dot(a,b,preferred_element_type=F32)
def tn(a,b):
    return lax.dot_general(a,b,(((0,),(0,)),((),())),preferred_element_type=F32)
def nt(a,b):
    return lax.dot_general(a,b,(((1,),(1,)),((),())),preferred_element_type=F32)
def halves(r):
    n=r.shape[1]//2
    return r[:,:n]+r[:,n:]
def quads(r):
    m=r.shape[0]//2
    return halves(r[:m]+r[m:])
def part(x):
    return jnp.sum(x.reshape(x.shape[0]//8,8,x.shape[1]),axis=0)
def one(x):
    return jnp.sum(x,axis=0,keepdims=True)
def group_mask():
    r=lax.broadcasted_iota(jnp.int32,(D,D),0)//HD
    c=lax.broadcasted_iota(jnp.int32,(D,D),1)//HD
    return r==c
def center(x,a1):
    h=x.astype(BF); r=x-h.astype(F32); m=r.astype(BF); lo=(r-m.astype(F32)).astype(BF)
    return x-(mm(h,a1)+mm(m,a1)+mm(lo,a1))

BQ,BK,BV,BO,GK,SK,GV,SV,BD,BU0,BU1=range(11)
AUG=D+16

LAYER_SCRATCH=dict(
    X=((TOK,2*D),BF), H=((TOK,D),F32), NK=((TOK,D),F32), NV=((TOK,D),F32), RK=((TOK,D),F32), RV=((TOK,D),F32),
    KN=((TOK,2*D),BF), VN=((TOK,2*D),BF), MD=((TOK,2*D),BF), ACT=((TOK,2*FF),BF), DG=((TOK,FF),F32),
    WKV=((2*D,4*D),BF), WUP=((2*D,2*FF),BF), WDN=((2*FF,2*D),BF), WDNT=((2*FF,2*D),BF), WUPT=((2*D,2*FF),BF),
    WKVT=((2*D,4*D),BF), WO2=((2*D,2*D),BF), WOT2=((2*D,2*D),BF), WQA=((AUG,2*D),BF),
    SP=((SEGS*D,2*D),BF), TP=((2*D,SEGS*D),BF), UT2=((SEGS,2*D,2*D),BF), U2=((SEGS,2*D,2*D),BF), UB=((SEGS,8,D),F32),
    CB=((8,D),F32),
)
TMP_SCRATCH=dict(
    E=((TOK,D),F32), ED=((TOK,2*D),BF), EP=((TOK,2*FF),BF), EM=((TOK,D),F32), EO=((TOK,2*D),BF), FKV=((TOK,4*D),BF),
    HT=((2*AUG,SEGS*D),BF), PP=((SEGS*D,2*D),BF), ES=((2,SEGS,2*D,2*D),BF),
    A2=((2*D,D),BF),
)

def prep_kv(L,w,vec,A2):
    a1=A2[0:D,:]
    b8=cat0(vec[BK:BV+1,:],jnp.zeros((6,D),F32))
    L['CB'][...]=center(b8,a1)
    wk=center(w['k'][...],a1); wv=center(w['v'][...],a1)
    kh,kl=split(wk); vh,vl=split(wv)
    kv=cat1(kh,vh,kl,vl)
    L['WKV'][0:D,:]=kv; L['WKV'][D:,:]=kv
    L['WKVT'][0:D,:]=cat1(kh,kh,vh,vh); L['WKVT'][D:,:]=cat1(kl,kl,vl,vl)

def prep_qo(L,w,vec):
    wo=w['o'][...]
    L['WO2'][...]=quad(wo); L['WOT2'][...]=quad_t(wo)
    L['WQA'][0:D,:]=pack(w['q'][...])
    L['WQA'][D:,:]=pack(cat0(vec[BQ:BQ+1,:],jnp.zeros((15,D),F32)))

def prep_ff(L,w):
    L['WUP'][...]=quad(w['up'][...])
    L['WDN'][...]=quad(w['dn'][...])

def prep_back(L,w):
    L['WUPT'][...]=quad_t(w['up'][...])
    L['WDNT'][...]=quad_t(w['dn'][...])

def fwd_a(L,vec,A2,live,r0,n,fresh):
    rows=pl.ds(r0,n)
    if fresh:
        x=pack(L['H'][rows,:])
        L['X'][rows,:]=x
    else:
        x=L['X'][rows,:]
    r=mm(x,L['WKV'][...])
    a2=A2[...]
    lv=live(r0,n)
    for i,(N,R,O,g,s) in enumerate((('NK','RK','KN',GK,SK),('NV','RV','VN',GV,SV))):
        c=r[:,i*D:(i+1)*D]+r[:,(i+2)*D:(i+3)*D]+L['CB'][i:i+1,:]
        rs=lax.rsqrt(mm(pack(c*c),a2)+1e-5)
        nn=c*rs
        L[R][rows,:]=rs; L[N][rows,:]=nn
        y=jnp.where(lv,nn*vec[g:g+1,:]+vec[s:s+1,:],0.0)
        L[O][rows,:]=pack(y)

def fwd_s1(L,gm,inv,s):
    rows=pl.ds(s*BLK,BLK)
    S=jnp.where(gm,quads(tn(L['KN'][rows,:],L['VN'][rows,:]))*inv[s],0.0)
    L['SP'][s*D:(s+1)*D,:]=pack(S)

def fwd_s2(L,s):
    h,l=split(halves(mm(L['SP'][s*D:(s+1)*D,:],L['WO2'][...])))
    L['TP'][0:D,s*D:(s+1)*D]=h; L['TP'][D:,s*D:(s+1)*D]=l
    row=cat1(h,l)
    return cat0(row,row)

def fwd_s3(L,vec,s,t2):
    us=halves(mm(L['WQA'][...],t2))
    L['UB'][s]=us[D:D+8]+vec[BO:BO+1,:]
    h,l=split(us[:D])
    p=cat1(h,l)
    L['U2'][s,0:D,:]=p; L['U2'][s,D:,:]=p
    L['UT2'][s,0:D,:]=cat1(h,h); L['UT2'][s,D:,:]=cat1(l,l)

def fwd_c1(L,s,r0,n):
    rows=pl.ds(r0,n)
    mid=L['H'][rows,:]+halves(mm(L['X'][rows,:],L['U2'][s]))+L['UB'][s,0:1,:]
    L['MD'][rows,:]=pack(mid)
    return mid

def fwd_c2(L,vec,r0,n):
    rows=pl.ds(r0,n)
    bu=cat1(vec[BU0:BU0+1,:],vec[BU1:BU1+1,:])
    z=halves(mm(L['MD'][rows,:],L['WUP'][...]))+bu
    z2=z*z
    c0=0.7978845608028654
    t=jnp.tanh(z*(c0+(c0*0.044715)*z2))
    p=0.5*t+0.5
    act=z*p
    L['DG'][rows,:]=p+act*(1.0-p)*((2*c0)+(6*c0*0.044715)*z2)
    L['ACT'][rows,:]=pack(act)

def fwd_c3(L,vec,OUT,mid,r0,n):
    rows=pl.ds(r0,n)
    OUT[rows,:]=mid+halves(mm(L['ACT'][rows,:],L['WDN'][...]))+vec[BD:BD+1,:]

def bwd_a1(L,Tm,r0,n):
    rows=pl.ds(r0,n)
    ep=halves(nt(Tm['ED'][rows,:],L['WDNT'][...]))*L['DG'][rows,:]
    Tm['EP'][rows,:]=pack(ep)
    return part(ep)

def bwd_a2(L,Tm,r0,n):
    rows=pl.ds(r0,n)
    em=Tm['E'][rows,:]+halves(nt(Tm['EP'][rows,:],L['WUPT'][...]))
    Tm['EM'][rows,:]=em
    Tm['EO'][rows,:]=pack(em)
    return part(em)

def bwd_s1(L,Tm,s,c):
    rows=pl.ds(s*BLK,BLK)
    if 'XT' in L:
        H=quads(mm(L['XT'][:,s*BLK:(s+1)*BLK],Tm['EO'][rows,:]))
    else:
        H=quads(tn(L['X'][rows,:],Tm['EO'][rows,:]))
    h,l=split(cat0(H,one(c),jnp.zeros((15,D),F32)))
    Tm['HT'][0:AUG,s*D:(s+1)*D]=h; Tm['HT'][AUG:,s*D:(s+1)*D]=l
    return cat1(h,l)

def bwd_s2(L,Tm,s,hp):
    Tm['PP'][s*D:(s+1)*D,:]=pack(quads(tn(L['WQA'][...],hp)))

def bwd_s3(L,Tm,gm,inv,s):
    e=jnp.where(gm,halves(nt(Tm['PP'][s*D:(s+1)*D,:],L['WOT2'][...]))*inv[s],0.0)
    h,l=split(e); p=cat1(h,l)
    Tm['ES'][0,s,0:D,:]=cat1(h,h); Tm['ES'][0,s,D:,:]=cat1(l,l)
    Tm['ES'][1,s,0:D,:]=p; Tm['ES'][1,s,D:,:]=p

def bwd_s4(L,Tm):
    go=quads(tn(L['SP'][...],Tm['PP'][...]))
    gq=halves(nt(Tm['HT'][...],L['TP'][...]))
    gq=gq[:AUG]+gq[AUG:]
    return gq[:D],gq[D:D+1],go

def bwd_b(L,vec,Tm,A2,s,r0,n,i):
    rows=pl.ds(r0,n)
    N,R,O,g,dot=(('NK','RK','VN',GK,nt),('NV','RV','KN',GV,mm))[i]
    en=halves(dot(L[O][rows,:],Tm['ES'][i,s]))
    nn=L[N][rows,:]
    m=en*vec[g:g+1,:]
    mn=m*nn
    av=mm(pack(mn),A2[...])
    f=L[R][rows,:]*(m-nn*av)
    Tm['FKV'][rows,i*2*D:(i+1)*2*D]=pack(f)
    return part(en),part(en*nn),part(f)

def bwd_x(L,Tm,DX,s,r0,n):
    rows=pl.ds(r0,n)
    dx=Tm['EM'][rows,:]+halves(nt(Tm['FKV'][rows,:],L['WKVT'][...])+nt(Tm['EO'][rows,:],L['UT2'][s]))
    DX[rows,:]=dx
    return dx

def bwd_x_next(L,Tm,s,r0,n):
    dx=bwd_x(L,Tm,Tm['E'],s,r0,n)
    Tm['ED'][pl.ds(r0,n),:]=pack(dx)
    return part(dx)

def grad_up(L,Tm):
    return quads(tn(L['MD'][...],Tm['EP'][...]))

def grad_down(L,Tm):
    return quads(tn(L['ACT'][...],Tm['ED'][...]))

def grad_both(L,Tm):
    g=tn(L['X'][...],Tm['FKV'][...])
    g=g[:D]+g[D:]
    return halves(g[:,:2*D]),halves(g[:,2*D:])

def grad_one(L,Tm,i):
    return quads(mm(L['XT'][...],Tm['FKV'][:,i*2*D:(i+1)*2*D]))


MESH = pl.DeviceIdType.MESH
NAMES = ("k", "v", "q", "o", "up", "dn")
ARG = dict(q=0, k=1, v=2, o=3, up=12, dn=14)
VECS = ((4, BQ), (5, BK), (6, BV), (7, BO), (8, GK), (9, SK), (10, GV), (11, SV), (15, BD), (13, BU0))
SMALL = 16
GROUPS = (
    (((1, "up"), (1, "dn"), (1, "q"), (1, "o")), True),
    (((1, "k"), (1, "v"), (1, "small")), True),
    (((0, "dn"),), True),
    (((0, "up"),), True),
    (((0, "q"), (0, "o")), True),
    (((0, "k"),), True),
    (((0, "small"),), False),
    (((0, "v"),), False),
)
PAIR = 2
NG = len(GROUPS)


def shard(name, n_zero):
    if name == "dn":
        return FF // n_zero, D
    return D // n_zero, FF if name == "up" else D


def group_layout(n_zero):
    places, sizes, pieces = {}, [], []
    for g, (members, halved) in enumerate(GROUPS):
        at = 0
        for item in members:
            places[item] = (g, at)
            if item[1] == "small":
                at += SMALL
            else:
                rows, cols = shard(item[1], n_zero)
                at += rows * cols // D
        at = -(-at // 16) * 16
        sizes.append(at)
        pieces.append(at // PAIR if halved else at)
    return places, sizes, pieces


class Names:
    pass


def fused_kernel(n_dp, n_zero, order, *refs):
    R = Names()
    for name, ref in zip(order, refs):
        setattr(R, name, ref)
    places, sizes, pieces = group_layout(n_zero)
    dp, zero = lax.axis_index("dp"), lax.axis_index("zero")
    zpeer = [None] + [lax.rem(zero + k, n_zero) for k in range(1, n_zero)]
    zfrom = [None] + [lax.rem(zero + n_zero - k, n_zero) for k in range(1, n_zero)]
    fast, slow, n_slow = lax.rem(dp, PAIR), dp // PAIR, n_dp // PAIR
    n_plane = PAIR * n_zero
    me = fast * n_zero + zero
    ppeer = [None] + [lax.rem(me + k, n_plane) for k in range(1, n_plane)]
    speer = [None] + [lax.rem(slow + k, n_slow) for k in range(1, n_slow)]
    sfrom = [None] + [lax.rem(slow + n_slow - k, n_slow) for k in range(1, n_slow)]
    pfrom = [None] + [lax.rem(me + n_plane - k, n_plane) for k in range(1, n_plane)]
    other = PAIR - 1 - fast

    def in_plane(k):
        return (slow * PAIR + ppeer[k] // n_zero, lax.rem(ppeer[k], n_zero))

    def along(k):
        return (speer[k] * PAIR + fast, zero)

    barrier = pltpu.get_barrier_semaphore()
    for k in range(1, n_slow):
        pl.semaphore_signal(barrier, inc=1, device_id=along(k), device_id_type=MESH)
    for k in range(1, n_plane):
        pl.semaphore_signal(barrier, inc=1, device_id=in_plane(k), device_id_type=MESH)

    len_in = pltpu.make_async_copy(R.lengths_in, R.lengths, R.io_sem.at[2])
    len_in.start()
    small_in = []
    for i, (arg, _) in enumerate(VECS):
        c = pltpu.make_async_copy(R.params[arg], R.stage[i], R.stage_sem.at[i])
        c.start()
        small_in.append(c)
    nodes_in = pltpu.make_async_copy(R.nodes, R.nodes_v, R.io_sem.at[0])
    nodes_in.start()

    def rows_of(name, who):
        n = shard(name, n_zero)[0]
        return pl.ds(pl.multiple_of(who * n, n), n)

    own = {}
    for level in range(2):
        for i, name in enumerate(NAMES):
            own[level, name] = pltpu.make_async_copy(
                R.params[ARG[name]].at[level],
                R.weights[name].at[level, rows_of(name, zero), :],
                R.own_sem.at[level, i],
            )
    for level in range(2):
        for name in NAMES:
            own[level, name].start()
    cot_in = pltpu.make_async_copy(R.cotangent, R.cot_v, R.io_sem.at[1])
    cot_in.start()

    pl.semaphore_wait(barrier, n_slow - 1 + n_plane - 1)

    def place(level, name):
        return level * 7 + (6 if name == "vec" else NAMES.index(name))

    def weight_copy(level, name, k, who):
        i = place(level, name)
        if name == "vec":
            src, dst = R.vec_own.at[level], R.vec_in.at[level, who]
        else:
            src, dst = R.params[ARG[name]].at[level], R.weights[name].at[level, rows_of(name, who), :]
        return pltpu.make_async_remote_copy(
            src_ref=src,
            dst_ref=dst,
            send_sem=R.w_send.at[i, k - 1],
            recv_sem=R.w_recv.at[i, k - 1],
            device_id=(dp, zpeer[k]),
            device_id_type=MESH,
        )

    n_x = n_zero // 2
    mate = zero + 1 - 2 * lax.rem(zero, 2)
    xpeer = [None] + [lax.rem(zero + 2 * k, n_zero) for k in range(1, n_x)]
    xfrom = [None] + [lax.rem(zero + n_zero - 2 * k, n_zero) for k in range(1, n_x)]
    mate_from = [None] + [lax.rem(mate + n_zero - 2 * k, n_zero) for k in range(1, n_x)]

    def part_of(name, who):
        if name == "vec":
            return R.vec_in.at[0, who]
        return R.weights[name].at[0, rows_of(name, who), :]

    def own_part(name):
        return R.vec_own.at[0] if name == "vec" else R.params[ARG[name]].at[0]

    def x_copy(name, k, who):
        i = place(0, name)
        return pltpu.make_async_remote_copy(
            src_ref=own_part(name),
            dst_ref=part_of(name, who),
            send_sem=R.x_send.at[i, k - 1],
            recv_sem=R.x_recv.at[i, k - 1],
            device_id=(dp, xpeer[k]),
            device_id_type=MESH,
        )

    def mate_copy(name, k, who):
        i = place(0, name)
        return pltpu.make_async_remote_copy(
            src_ref=own_part(name) if k == 0 else part_of(name, xfrom[k]),
            dst_ref=part_of(name, who),
            send_sem=R.m_send.at[i, k],
            recv_sem=R.m_recv.at[i, k],
            device_id=(dp, mate),
            device_id_type=MESH,
        )

    def send_first(*names):
        for name in names:
            for k in range(1, n_x):
                x_copy(name, k, zero).start()
        for name in names:
            mate_copy(name, 0, zero).start()

    def relay_first(*names):
        for name in names:
            for k in range(1, n_x):
                x_copy(name, k, xfrom[k]).wait_recv()
                mate_copy(name, k, xfrom[k]).start()

    def take_first(*names):
        for name in names:
            if name != "vec":
                own[0, name].wait()
            mate_copy(name, 0, mate).wait_recv()
            for k in range(1, n_x):
                mate_copy(name, k, mate_from[k]).wait_recv()

    far_first = sorted(range(1, n_zero), key=lambda k: k in (1, n_zero - 1))

    def send_weights(level, *names):
        for name in names:
            for k in far_first:
                weight_copy(level, name, k, zero).start()

    def take_weights(level, *names):
        for name in names:
            if name != "vec":
                own[level, name].wait()
            for k in range(1, n_zero):
                weight_copy(level, name, k, zfrom[k]).wait_recv()

    send_first("k", "v", "q", "o")

    for c in small_in:
        c.wait()
    lane = lax.broadcasted_iota(jnp.int32, (2, D), 1)
    R.vec_own[...] = jnp.zeros((2, SMALL, D), F32)
    for i, (arg, row) in enumerate(VECS):
        x = R.stage[i][...]
        n = x.shape[1]
        x = jnp.concatenate([x, jnp.zeros((2, D - n), F32)], axis=1)
        x = pltpu.roll(x, lax.rem(zero * n, D), axis=1)
        if row != BU0:
            R.vec_own[:, row, :] = x
        else:
            first = zero * n < D
            R.vec_own[:, row, :] = jnp.where(first, x, 0.0)
            R.vec_own[:, row + 1, :] = jnp.where(first, 0.0, x)

    send_first("vec", "up", "dn")

    len_in.wait()
    gm = group_mask()
    a = jnp.where(gm, 1.0 / HD, 0.0).astype(BF)
    R.A2[0:D, :] = a
    R.A2[D:, :] = a
    ln = [R.lengths[i] for i in range(SEGS)]
    st = [0]
    for i in range(SEGS):
        st.append(st[-1] + ln[i])
    inv = [1.0 / (jnp.full((1, D), ln[s], jnp.int32).astype(F32)) for s in range(SEGS)]

    def live(r0, n):
        s = r0 // BLK
        return lax.broadcasted_iota(jnp.int32, (n, D), 0) + (r0 - s * BLK) < ln[s]

    Ls, Tm = R.layers, R.temps
    Tm["A2"] = R.A2
    Ls[0]["XT"] = R.XT
    for y in (R.Y, R.Y2):
        y[TOK:, :] = jnp.zeros((y.shape[0] - TOK, D), F32)
    nodes_in.wait()
    for s in range(SEGS):
        x = R.nodes_v[pl.ds(st[s], BLK), :]
        Ls[0]["H"][s * BLK : (s + 1) * BLK, :] = x
        x = pack(x)
        Ls[0]["X"][s * BLK : (s + 1) * BLK, :] = x
        R.XT[:, s * BLK : (s + 1) * BLK] = x.T
    cot_in.wait()
    sum_e = zero8 = jnp.zeros((8, D), F32)
    for s in range(SEGS):
        x = jnp.where(live(s * BLK, BLK), R.cot_v[pl.ds(st[s], BLK), :], 0.0)
        Tm["E"][s * BLK : (s + 1) * BLK, :] = x
        Tm["ED"][s * BLK : (s + 1) * BLK, :] = pack(x)
        sum_e = sum_e + part(x)

    relay_first("k", "v", "q", "o", "vec", "up", "dn")
    send_weights(1, "k", "v", "vec", "q", "o", "up", "dn")
    vecs = [None, None]

    def take_vecs(level):
        x = R.vec_own[level]
        for k in range(1, n_zero):
            x = x + R.vec_in[level, zpeer[k]]
        R.vec[level] = x
        vecs[level] = R.vec.at[level]

    tiles = [(s, s * BLK) for s in range(SEGS)]

    def pipe(stages):
        kept = [None] * len(tiles)
        for t in range(len(tiles) + len(stages) - 1):
            for j, stage in enumerate(stages):
                if 0 <= t - j < len(tiles):
                    kept[t - j] = stage(tiles[t - j], kept[t - j])
        return kept

    for level in range(2):
        L = Ls[level]
        dst = Ls[1]["H"] if level == 0 else R.Y
        w = {n: R.weights[n].at[level] for n in NAMES}
        if level == 0:
            take_first("k", "v", "vec")
        else:
            take_weights(1, "k", "v", "vec", "q", "o")
        take_vecs(level)
        vec = vecs[level]
        prep_kv(L, w, vec, R.A2)
        if level == 0:
            take_first("q", "o")
        prep_qo(L, w, vec)
        if level == 0:
            take_first("up", "dn")
            prep_ff(L, w)
        for s, r in tiles:
            fwd_a(L, vec, R.A2, live, r, BLK, level == 1)
        for s in range(SEGS):
            fwd_s1(L, gm, inv, s)
        t2 = [fwd_s2(L, s) for s in range(SEGS)]
        for s in range(SEGS):
            fwd_s3(L, vec, s, t2[s])
        if level == 1:
            take_weights(1, "up", "dn")
            prep_ff(L, w)

        def middle(tile, _):
            return fwd_c1(L, *tile, BLK)

        def hidden(tile, mid):
            fwd_c2(L, vec, tile[1], BLK)
            return mid

        def close(tile, mid):
            fwd_c3(L, vec, dst, mid, tile[1], BLK)

        pipe([middle, hidden, close])

    def put(level, name, g):
        grp, at = places[level, name]
        n = shard(name, n_zero)[0]
        for p in range(n_zero):
            part_p = g[p * n : (p + 1) * n]
            if name == "up":
                R.gsend[grp][p, at : at + n, :] = part_p[:, :D]
                R.gsend[grp][p, at + n : at + 2 * n, :] = part_p[:, D:]
            else:
                R.gsend[grp][p, at : at + n, :] = part_p

    def plane_copy(grp, k, who):
        rows, src = pieces[grp], R.gsend[grp].at[lax.rem(ppeer[k], n_zero)]
        if GROUPS[grp][1]:
            src = src.at[pl.ds(pl.multiple_of(ppeer[k] // n_zero * rows, 8), rows), :]
        return pltpu.make_async_remote_copy(
            src_ref=src,
            dst_ref=R.gplane[grp].at[who],
            send_sem=R.p_send.at[grp, k - 1],
            recv_sem=R.p_recv.at[grp, k - 1],
            device_id=in_plane(k),
            device_id_type=MESH,
        )

    def slow_copy(grp, k, who):
        return pltpu.make_async_remote_copy(
            src_ref=R.gslow[grp].at[slow],
            dst_ref=R.gslow[grp].at[who],
            send_sem=R.s_send.at[grp, k - 1],
            recv_sem=R.s_recv.at[grp, k - 1],
            device_id=along(k),
            device_id_type=MESH,
        )

    def half_of(grp, who):
        rows = pieces[grp]
        return R.fin_out[grp].at[pl.ds(pl.multiple_of(who * rows, 8), rows), :]

    def pair_copy(grp, who):
        return pltpu.make_async_remote_copy(
            src_ref=half_of(grp, fast),
            dst_ref=half_of(grp, who),
            send_sem=R.f_send.at[grp],
            recv_sem=R.f_recv.at[grp],
            device_id=(slow * PAIR + other, zero),
            device_id_type=MESH,
        )

    def start_plane(grp):
        for k in range(1, n_plane):
            plane_copy(grp, k, me).start()

    def start_slow(grp):
        rows = pieces[grp]
        at = pl.multiple_of(fast * rows, 8) if GROUPS[grp][1] else 0
        R.gplane[grp][me] = R.gsend[grp][zero, pl.ds(at, rows), :]
        for k in range(1, n_plane):
            plane_copy(grp, k, pfrom[k]).wait_recv()
        x = R.gplane[grp][0]
        for j in range(1, n_plane):
            x = x + R.gplane[grp][j]
        R.gslow[grp][slow] = x
        for k in range(1, n_slow):
            slow_copy(grp, k, slow).start()

    def start_pair(grp):
        for k in range(1, n_slow):
            slow_copy(grp, k, sfrom[k]).wait_recv()
        x = R.gslow[grp][0]
        for j in range(1, n_slow):
            x = x + R.gslow[grp][j]
        if GROUPS[grp][1]:
            R.fin_out[grp][pl.ds(pl.multiple_of(fast * pieces[grp], 8), pieces[grp]), :] = x
            pair_copy(grp, fast).start()
        else:
            R.fin_out[grp][...] = x

    def end_pair(grp):
        if GROUPS[grp][1]:
            pair_copy(grp, other).wait_recv()

    def hand_out_vectors():
        small = []
        for level in range(2):
            g, at = places[level, "small"]
            small.append(R.fin_out[g][at : at + SMALL, :])
        for (_, row), out in zip(VECS, R.vec_out):
            n = out.shape[1]
            x = jnp.concatenate([s[row : row + 1, :] for s in small], axis=0)
            if row == BU0:
                x1 = jnp.concatenate([s[row + 1 : row + 2, :] for s in small], axis=0)
                x = jnp.where(zero * n < D, x, x1)
            x = pltpu.roll(x, lax.rem(D - lax.rem(zero * n, D), D), axis=1)
            out[...] = x[:, :n]

    shift = [jnp.minimum(BLK * s - st[s], (BLK - 256) * s) for s in range(SEGS)]

    def unpack(Y, base):
        lo, hi = (0, 256, 512, 768), (512, 1024, 1536, 2048)
        step = 256
        for t0 in range(0, TOK, step):
            it = lax.broadcasted_iota(jnp.int32, (step, D), 0) + t0
            x = base[t0 : t0 + step, :]
            for s in range(SEGS):
                if t0 < hi[s] and t0 + step > lo[s]:
                    y = Y[pl.ds(t0 + shift[s], step), :]
                    x = jnp.where((it >= st[s]) & (it < st[s + 1]), y, x)
            base[t0 : t0 + step, :] = x

    for level in (1, 0):
        L, vec = Ls[level], vecs[level]
        w = {n: R.weights[n].at[level] for n in NAMES}
        prep_back(L, w)
        put(level, "dn", grad_down(L, Tm))
        if level == 0:
            start_plane(2)

        def feed(tile, _):
            return bwd_a1(L, Tm, tile[1], BLK)

        def after(tile, su):
            return su, bwd_a2(L, Tm, tile[1], BLK)

        sums = pipe([feed, after])
        su = sum((x[0] for x in sums), jnp.zeros((8, FF), F32))
        sc = [x[1] for x in sums]
        put(level, "up", grad_up(L, Tm))
        if level == 0:
            start_plane(3)
            start_slow(0)
        hp = [bwd_s1(L, Tm, s, sc[s]) for s in range(SEGS)]
        for s in range(SEGS):
            bwd_s2(L, Tm, s, hp[s])
        for s in range(SEGS):
            bwd_s3(L, Tm, gm, inv, s)
        gq, gbq, go = bwd_s4(L, Tm)
        put(level, "q", gq)
        put(level, "o", go)
        start_plane(0 if level == 1 else 4)
        a1 = R.A2[0:D, :]
        ss = [zero8] * 6

        def key_value(i):
            for s, r in tiles:
                o = bwd_b(L, vec, Tm, R.A2, s, r, BLK, i)
                for j in range(3):
                    ss[3 * i + j] = ss[3 * i + j] + o[j]

        key_value(0)
        if level == 0:
            put(level, "k", center(grad_one(L, Tm, 0), a1))
            start_plane(5)
            start_slow(1)
        key_value(1)
        rows = [jnp.zeros((1, D), F32)] * SMALL
        rows[BQ], rows[BK], rows[BV] = gbq, one(center(ss[2], a1)), one(center(ss[5], a1))
        rows[BO] = one(sc[0] + sc[1] + sc[2] + sc[3])
        rows[SK], rows[GK], rows[SV], rows[GV] = one(ss[0]), one(ss[1]), one(ss[3]), one(ss[4])
        rows[BD] = one(sum_e)
        u = one(su)
        rows[BU0], rows[BU1] = u[:, :D], u[:, D:]
        small = jnp.concatenate(rows, axis=0)
        grp, at = places[level, "small"]
        for p in range(n_zero):
            R.gsend[grp][p, at : at + SMALL, :] = small
        if level == 1:
            gk, gv = grad_both(L, Tm)
            put(level, "k", center(gk, a1))
            put(level, "v", center(gv, a1))
            start_plane(1)
        else:
            put(level, "v", center(grad_one(L, Tm, 1), a1))
            start_plane(7)
            start_plane(6)
            start_slow(2)
        if level == 1:
            sum_e = zero8
            for s, r in tiles:
                sum_e = sum_e + bwd_x_next(L, Tm, s, r, BLK)
        else:
            for s, r in tiles:
                bwd_x(L, Tm, R.Y2, s, r, BLK)

    start_slow(3)
    start_slow(4)
    start_pair(0)
    unpack(R.Y, R.nodes_v)
    store_out = pltpu.make_async_copy(R.nodes_v, R.out, R.io_sem.at[3])
    store_out.start()
    start_pair(1)
    start_slow(5)
    unpack(R.Y2, R.cot_v)
    store_gx = pltpu.make_async_copy(R.cot_v, R.gx, R.io_sem.at[4])
    store_gx.start()
    start_slow(7)
    start_slow(6)
    for g in (2, 3, 4, 5):
        start_pair(g)
    start_pair(6)
    end_pair(1)
    hand_out_vectors()
    start_pair(7)
    for g in range(NG):
        if g != 1:
            end_pair(g)

    for name in NAMES + ("vec",):
        mate_copy(name, 0, zero).wait_send()
        for k in range(1, n_x):
            x_copy(name, k, zero).wait_send()
            mate_copy(name, k, xfrom[k]).wait_send()
        for k in range(1, n_zero):
            weight_copy(1, name, k, zero).wait_send()
    for g in range(NG):
        for k in range(1, n_plane):
            plane_copy(g, k, me).wait_send()
        for k in range(1, n_slow):
            slow_copy(g, k, slow).wait_send()
        if GROUPS[g][1]:
            pair_copy(g, fast).wait_send()
    store_out.wait()
    store_gx.wait()


def finish_kernel(n_zero, out, gx, fin, vec, outs, sem):
    places, _, _ = group_layout(n_zero)
    copies = []

    def copy(src, dst):
        c = pltpu.make_async_copy(src, dst, sem.at[len(copies)])
        c.start()
        copies.append(c)

    half = TOK // 2
    for i in range(2):
        copy(out.at[pl.ds(i * half, half), :], outs[0].at[pl.ds(i * half, half), :])
        copy(gx.at[pl.ds(i * half, half), :], outs[1].at[pl.ds(i * half, half), :])
    for name, arg in ARG.items():
        for level in range(2):
            g, at = places[level, name]
            n = shard(name, n_zero)[0]
            if name == "up":
                for h in range(2):
                    copy(
                        fin[g].at[pl.ds(at + h * n, n), :],
                        outs[2 + arg].at[level, :, pl.ds(h * D, D)],
                    )
            else:
                copy(fin[g].at[pl.ds(at, n), :], outs[2 + arg].at[level])
    for (arg, _), v in zip(VECS, vec):
        copy(v, outs[2 + arg])
    for c in copies:
        c.wait()


def make_fused(n_dp, n_zero, params):
    places, sizes, pieces = group_layout(n_zero)
    dma = pltpu.SemaphoreType.DMA
    any_ = pl.BlockSpec(memory_space=pl.ANY)
    order, scratch = [], []

    def add(name, shape):
        order.append(name)
        scratch.append(shape)

    n_params = len(params)
    out_shape = [VM((TOK, D), F32)] * 2 + [VM((p, D), F32) for p in sizes]
    out_shape += [VM(params[arg].shape, F32) for arg, _ in VECS]
    ls, ts = list(LAYER_SCRATCH), [n for n in TMP_SCRATCH if n != "A2"]
    for level in range(2):
        for n in ls:
            add(("layer", level, n), VM(*LAYER_SCRATCH[n]))
    for n in ts:
        add(("temp", n), VM(*TMP_SCRATCH[n]))
    add("lengths", pltpu.SMEM((SEGS,), jnp.int32))
    add("A2", VM(*TMP_SCRATCH["A2"]))
    add("Y", VM((TOK + 768, D), F32))
    add("XT", VM((2 * D, TOK), BF))
    add("Y2", VM((TOK + 768, D), F32))
    add("nodes_v", VM((TOK, D), F32))
    add("cot_v", VM((TOK, D), F32))
    for i, (arg, _) in enumerate(VECS):
        add(("stage", i), VM(params[arg].shape, F32))
    for n in NAMES:
        rows, cols = shard(n, n_zero)
        add(("weights", n), VM((2, rows * n_zero, cols), F32))
    add("vec_own", VM((2, SMALL, D), F32))
    add("vec_in", VM((2, n_zero, SMALL, D), F32))
    add("vec", VM((2, SMALL, D), F32))
    for g in range(NG):
        add(("gsend", g), VM((n_zero, sizes[g], D), F32))
        add(("gplane", g), VM((PAIR * n_zero, pieces[g], D), F32))
        add(("gslow", g), VM((n_dp // PAIR, pieces[g], D), F32))
    add("stage_sem", dma((len(VECS),)))
    add("io_sem", dma((5,)))
    add("own_sem", dma((2, 6)))
    add("w_send", dma((14, n_zero - 1)))
    add("w_recv", dma((14, n_zero - 1)))
    for n, m in (("x", n_zero // 2 - 1), ("m", n_zero // 2)):
        add(n + "_send", dma((7, m)))
        add(n + "_recv", dma((7, m)))
    for n, m in (("p", PAIR * n_zero), ("s", n_dp // PAIR)):
        add(n + "_send", dma((NG, m - 1)))
        add(n + "_recv", dma((NG, m - 1)))
    add("f_send", dma((NG,)))
    add("f_recv", dma((NG,)))

    def body(*refs):
        lengths_in, nodes, cot = refs[:3]
        pr = refs[3 : 3 + n_params]
        n_outs = 2 + NG + len(VECS)
        outs = refs[3 + n_params : 3 + n_outs + n_params]
        rest = refs[3 + n_outs + n_params :]
        simple = dict(lengths_in=lengths_in, nodes=nodes, cotangent=cot, params=pr, out=outs[0], gx=outs[1], fin_out=outs[2 : 2 + NG], vec_out=outs[2 + NG :])
        layers, temps = [{}, {}], {}
        simple.update(layers=layers, temps=temps, stage=[None] * len(VECS), weights={})
        for n in ("gsend", "gplane", "gslow"):
            simple[n] = [None] * NG
        for key, ref in zip(order, rest):
            if isinstance(key, str):
                simple[key] = ref
            elif key[0] == "layer":
                layers[key[1]][key[2]] = ref
            elif key[0] == "temp":
                temps[key[1]] = ref
            else:
                simple[key[0]][key[1]] = ref
        fused_kernel(n_dp, n_zero, list(simple), *simple.values())

    call = pl.pallas_call(
        body,
        out_shape=out_shape,
        in_specs=[any_] * (3 + n_params),
        out_specs=[any_] * 2 + [pl.BlockSpec(memory_space=pltpu.VMEM)] * (NG + len(VECS)),
        scratch_shapes=scratch,
        compiler_params=pltpu.CompilerParams(
            collective_id=0, has_side_effects=True, vmem_limit_bytes=56 * 1024 * 1024
        ),
    )
    return call


def make_finish(n_zero, params):
    any_ = pl.BlockSpec(memory_space=pl.ANY)
    out_shape = [jax.ShapeDtypeStruct((TOK, D), F32)] * 2
    out_shape += [jax.ShapeDtypeStruct(p.shape, F32) for p in params]
    n_ins = 2 + NG + len(VECS)

    def body(*refs):
        out, gx = refs[:2]
        fin, vec = refs[2 : 2 + NG], refs[2 + NG : n_ins]
        finish_kernel(n_zero, out, gx, fin, vec, refs[n_ins:-1], refs[-1])

    call = pl.pallas_call(
        body,
        out_shape=out_shape,
        in_specs=[any_] * n_ins,
        out_specs=[any_] * len(out_shape),
        scratch_shapes=[pltpu.SemaphoreType.DMA((28,))],
    )
    return lambda *xs: call(*[pltpu.with_memory_space_constraint(x, pltpu.VMEM) for x in xs])


def solution(mesh):
    n_dp, n_zero = mesh.shape["dp"], mesh.shape["zero"]
    wide, flat = P(None, "zero", None), P(None, "zero")
    params = (wide,) * 4 + (flat,) * 8 + (wide, flat, wide, flat)
    rows = P(("dp", "zero"), None)

    def local(nodes, cotangent, lengths, *params):
        results = make_fused(n_dp, n_zero, params)(lengths, nodes, cotangent, *params)
        return tuple(make_finish(n_zero, params)(*results))

    return jax.shard_map(
        local,
        mesh=mesh,
        in_specs=(rows, rows, P(("dp", "zero"))) + params,
        out_specs=(rows, rows) + params,
        check_vma=False,
    )
```

```python
import jax
import jax.numpy as jnp
from jax import lax
from jax.experimental import pallas as pl
from jax.experimental.pallas import tpu as pltpu
from jax.sharding import PartitionSpec as P

D=128; FF=256; SEGS=4; BLK=512; TOK=2048; HD=32
F32=jnp.float32; BF=jnp.bfloat16
VM=pltpu.VMEM

def split(x):
    hi=x.astype(BF); lo=(x-hi.astype(F32)).astype(BF)
    return hi,lo
def cat0(*x): return jnp.concatenate(x,axis=0)
def cat1(*x): return jnp.concatenate(x,axis=1)
def pack(x):
    return cat1(*split(x))
def quad(x):
    p=pack(x)
    return cat0(p,p)
def quad_t(x):
    h,l=split(x)
    return cat0(cat1(h,h),cat1(l,l))
def mm(a,b):
    return jnp.dot(a,b,preferred_element_type=F32)
def tn(a,b):
    return lax.dot_general(a,b,(((0,),(0,)),((),())),preferred_element_type=F32)
def nt(a,b):
    return lax.dot_general(a,b,(((1,),(1,)),((),())),preferred_element_type=F32)
def halves(r):
    n=r.shape[1]//2
    return r[:,:n]+r[:,n:]
def quads(r):
    m=r.shape[0]//2
    return halves(r[:m]+r[m:])
def part(x):
    return jnp.sum(x.reshape(x.shape[0]//8,8,x.shape[1]),axis=0)
def one(x):
    return jnp.sum(x,axis=0,keepdims=True)
def group_mask():
    r=lax.broadcasted_iota(jnp.int32,(D,D),0)//HD
    c=lax.broadcasted_iota(jnp.int32,(D,D),1)//HD
    return r==c
def center(x,a1):
    h=x.astype(BF); r=x-h.astype(F32); m=r.astype(BF); lo=(r-m.astype(F32)).astype(BF)
    return x-(mm(h,a1)+mm(m,a1)+mm(lo,a1))

BQ,BK,BV,BO,GK,SK,GV,SV,BD,BU0,BU1=range(11)
AUG=D+16

LAYER_SCRATCH=dict(
    X=((TOK,2*D),BF), H=((TOK,D),F32), NK=((TOK,D),F32), NV=((TOK,D),F32), RK=((TOK,D),F32), RV=((TOK,D),F32),
    KN=((TOK,2*D),BF), VN=((TOK,2*D),BF), MD=((TOK,2*D),BF), ACT=((TOK,2*FF),BF), DG=((TOK,FF),F32),
    WKV=((2*D,4*D),BF), WUP=((2*D,2*FF),BF), WDN=((2*FF,2*D),BF), WDNT=((2*FF,2*D),BF), WUPT=((2*D,2*FF),BF),
    WKVT=((2*D,4*D),BF), WO2=((2*D,2*D),BF), WOT2=((2*D,2*D),BF), WQA=((AUG,2*D),BF),
    SP=((SEGS*D,2*D),BF), TP=((2*D,SEGS*D),BF), UT2=((SEGS,2*D,2*D),BF), U2=((SEGS,2*D,2*D),BF), UB=((SEGS,8,D),F32),
    CB=((8,D),F32),
)
TMP_SCRATCH=dict(
    E=((TOK,D),F32), ED=((TOK,2*D),BF), EP=((TOK,2*FF),BF), EM=((TOK,D),F32), EO=((TOK,2*D),BF), FKV=((TOK,4*D),BF),
    HT=((2*AUG,SEGS*D),BF), PP=((SEGS*D,2*D),BF), ES=((2,SEGS,2*D,2*D),BF),
    A2=((2*D,D),BF),
)

def prep_kv(L,w,vec,A2):
    a1=A2[0:D,:]
    b8=cat0(vec[BK:BV+1,:],jnp.zeros((6,D),F32))
    L['CB'][...]=center(b8,a1)
    wk=center(w['k'][...],a1); wv=center(w['v'][...],a1)
    kh,kl=split(wk); vh,vl=split(wv)
    kv=cat1(kh,vh,kl,vl)
    L['WKV'][0:D,:]=kv; L['WKV'][D:,:]=kv
    L['WKVT'][0:D,:]=cat1(kh,kh,vh,vh); L['WKVT'][D:,:]=cat1(kl,kl,vl,vl)

def prep_qo(L,w,vec):
    wo=w['o'][...]
    L['WO2'][...]=quad(wo); L['WOT2'][...]=quad_t(wo)
    L['WQA'][0:D,:]=pack(w['q'][...])
    L['WQA'][D:,:]=pack(cat0(vec[BQ:BQ+1,:],jnp.zeros((15,D),F32)))

def prep_ff(L,w):
    L['WUP'][...]=quad(w['up'][...])
    L['WDN'][...]=quad(w['dn'][...])

def prep_back(L,w):
    L['WUPT'][...]=quad_t(w['up'][...])
    L['WDNT'][...]=quad_t(w['dn'][...])

def fwd_a(L,vec,A2,live,r0,n,fresh):
    rows=pl.ds(r0,n)
    if fresh:
        x=pack(L['H'][rows,:])
        L['X'][rows,:]=x
    else:
        x=L['X'][rows,:]
    r=mm(x,L['WKV'][...])
    a2=A2[...]
    lv=live(r0,n)
    for i,(N,R,O,g,s) in enumerate((('NK','RK','KN',GK,SK),('NV','RV','VN',GV,SV))):
        c=r[:,i*D:(i+1)*D]+r[:,(i+2)*D:(i+3)*D]+L['CB'][i:i+1,:]
        rs=lax.rsqrt(mm(pack(c*c),a2)+1e-5)
        nn=c*rs
        L[R][rows,:]=rs; L[N][rows,:]=nn
        y=jnp.where(lv,nn*vec[g:g+1,:]+vec[s:s+1,:],0.0)
        L[O][rows,:]=pack(y)

def fwd_s1(L,gm,inv,s):
    rows=pl.ds(s*BLK,BLK)
    S=jnp.where(gm,quads(tn(L['KN'][rows,:],L['VN'][rows,:]))*inv[s],0.0)
    L['SP'][s*D:(s+1)*D,:]=pack(S)

def fwd_s2(L,s):
    h,l=split(halves(mm(L['SP'][s*D:(s+1)*D,:],L['WO2'][...])))
    L['TP'][0:D,s*D:(s+1)*D]=h; L['TP'][D:,s*D:(s+1)*D]=l
    row=cat1(h,l)
    return cat0(row,row)

def fwd_s3(L,vec,s,t2):
    us=halves(mm(L['WQA'][...],t2))
    L['UB'][s]=us[D:D+8]+vec[BO:BO+1,:]
    h,l=split(us[:D])
    p=cat1(h,l)
    L['U2'][s,0:D,:]=p; L['U2'][s,D:,:]=p
    L['UT2'][s,0:D,:]=cat1(h,h); L['UT2'][s,D:,:]=cat1(l,l)

def fwd_c1(L,s,r0,n):
    rows=pl.ds(r0,n)
    mid=L['H'][rows,:]+halves(mm(L['X'][rows,:],L['U2'][s]))+L['UB'][s,0:1,:]
    L['MD'][rows,:]=pack(mid)
    return mid

def fwd_c2(L,vec,r0,n):
    rows=pl.ds(r0,n)
    bu=cat1(vec[BU0:BU0+1,:],vec[BU1:BU1+1,:])
    z=halves(mm(L['MD'][rows,:],L['WUP'][...]))+bu
    z2=z*z
    c0=0.7978845608028654
    t=jnp.tanh(z*(c0+(c0*0.044715)*z2))
    p=0.5*t+0.5
    act=z*p
    L['DG'][rows,:]=p+act*(1.0-p)*((2*c0)+(6*c0*0.044715)*z2)
    L['ACT'][rows,:]=pack(act)

def fwd_c3(L,vec,OUT,mid,r0,n):
    rows=pl.ds(r0,n)
    OUT[rows,:]=mid+halves(mm(L['ACT'][rows,:],L['WDN'][...]))+vec[BD:BD+1,:]

def bwd_a1(L,Tm,r0,n):
    rows=pl.ds(r0,n)
    ep=halves(nt(Tm['ED'][rows,:],L['WDNT'][...]))*L['DG'][rows,:]
    Tm['EP'][rows,:]=pack(ep)
    return part(ep)

def bwd_a2(L,Tm,r0,n):
    rows=pl.ds(r0,n)
    em=Tm['E'][rows,:]+halves(nt(Tm['EP'][rows,:],L['WUPT'][...]))
    Tm['EM'][rows,:]=em
    Tm['EO'][rows,:]=pack(em)
    return part(em)

def bwd_s1(L,Tm,s,c):
    rows=pl.ds(s*BLK,BLK)
    if 'XT' in L:
        H=quads(mm(L['XT'][:,s*BLK:(s+1)*BLK],Tm['EO'][rows,:]))
    else:
        H=quads(tn(L['X'][rows,:],Tm['EO'][rows,:]))
    h,l=split(cat0(H,one(c),jnp.zeros((15,D),F32)))
    Tm['HT'][0:AUG,s*D:(s+1)*D]=h; Tm['HT'][AUG:,s*D:(s+1)*D]=l
    return cat1(h,l)

def bwd_s2(L,Tm,s,hp):
    Tm['PP'][s*D:(s+1)*D,:]=pack(quads(tn(L['WQA'][...],hp)))

def bwd_s3(L,Tm,gm,inv,s):
    e=jnp.where(gm,halves(nt(Tm['PP'][s*D:(s+1)*D,:],L['WOT2'][...]))*inv[s],0.0)
    h,l=split(e); p=cat1(h,l)
    Tm['ES'][0,s,0:D,:]=cat1(h,h); Tm['ES'][0,s,D:,:]=cat1(l,l)
    Tm['ES'][1,s,0:D,:]=p; Tm['ES'][1,s,D:,:]=p

def bwd_s4(L,Tm):
    go=quads(tn(L['SP'][...],Tm['PP'][...]))
    gq=halves(nt(Tm['HT'][...],L['TP'][...]))
    gq=gq[:AUG]+gq[AUG:]
    return gq[:D],gq[D:D+1],go

def bwd_b(L,vec,Tm,A2,s,r0,n,i):
    rows=pl.ds(r0,n)
    N,R,O,g,dot=(('NK','RK','VN',GK,nt),('NV','RV','KN',GV,mm))[i]
    en=halves(dot(L[O][rows,:],Tm['ES'][i,s]))
    nn=L[N][rows,:]
    m=en*vec[g:g+1,:]
    mn=m*nn
    av=mm(pack(mn),A2[...])
    f=L[R][rows,:]*(m-nn*av)
    Tm['FKV'][rows,i*2*D:(i+1)*2*D]=pack(f)
    return part(en),part(en*nn),part(f)

def bwd_x(L,Tm,DX,s,r0,n):
    rows=pl.ds(r0,n)
    dx=Tm['EM'][rows,:]+halves(nt(Tm['FKV'][rows,:],L['WKVT'][...])+nt(Tm['EO'][rows,:],L['UT2'][s]))
    DX[rows,:]=dx
    return dx

def bwd_x_next(L,Tm,s,r0,n):
    dx=bwd_x(L,Tm,Tm['E'],s,r0,n)
    Tm['ED'][pl.ds(r0,n),:]=pack(dx)
    return part(dx)

def grad_up(L,Tm):
    return quads(tn(L['MD'][...],Tm['EP'][...]))

def grad_down(L,Tm):
    return quads(tn(L['ACT'][...],Tm['ED'][...]))

def grad_both(L,Tm):
    g=tn(L['X'][...],Tm['FKV'][...])
    g=g[:D]+g[D:]
    return halves(g[:,:2*D]),halves(g[:,2*D:])

def grad_one(L,Tm,i):
    return quads(mm(L['XT'][...],Tm['FKV'][:,i*2*D:(i+1)*2*D]))


MESH = pl.DeviceIdType.MESH
NAMES = ("k", "v", "q", "o", "up", "dn")
ARG = dict(q=0, k=1, v=2, o=3, up=12, dn=14)
VECS = ((4, BQ), (5, BK), (6, BV), (7, BO), (8, GK), (9, SK), (10, GV), (11, SV), (15, BD), (13, BU0))
SMALL = 16
GROUPS = (
    (((1, "up"), (1, "dn"), (1, "q"), (1, "o")), True),
    (((1, "k"), (1, "v"), (1, "small")), True),
    (((0, "dn"), (0, "up")), True),
    (((0, "q"), (0, "o")), True),
    (((0, "k"), (0, "v"), (0, "small")), 2),
)
PAIR = 2
NG = len(GROUPS)


def shard(name, n_zero):
    if name == "dn":
        return FF // n_zero, D
    return D // n_zero, FF if name == "up" else D


def group_layout(n_zero):
    places, sizes, pieces = {}, [], []
    for g, (members, halved) in enumerate(GROUPS):
        at = 0
        for item in members:
            places[item] = (g, at)
            if item[1] == "small":
                at += SMALL
            else:
                rows, cols = shard(item[1], n_zero)
                at += rows * cols // D
        at = -(-at // 16) * 16
        sizes.append(at)
        pieces.append(at // PAIR if halved else at)
    return places, sizes, pieces


class Names:
    pass


def fused_kernel(n_dp, n_zero, order, *refs):
    R = Names()
    for name, ref in zip(order, refs):
        setattr(R, name, ref)
    places, sizes, pieces = group_layout(n_zero)
    dp, zero = lax.axis_index("dp"), lax.axis_index("zero")
    zpeer = [None] + [lax.rem(zero + k, n_zero) for k in range(1, n_zero)]
    zfrom = [None] + [lax.rem(zero + n_zero - k, n_zero) for k in range(1, n_zero)]
    fast, slow, n_slow = lax.rem(dp, PAIR), dp // PAIR, n_dp // PAIR
    n_plane = PAIR * n_zero
    me = fast * n_zero + zero
    ppeer = [None] + [lax.rem(me + k, n_plane) for k in range(1, n_plane)]
    speer = [None] + [lax.rem(slow + k, n_slow) for k in range(1, n_slow)]
    sfrom = [None] + [lax.rem(slow + n_slow - k, n_slow) for k in range(1, n_slow)]
    pfrom = [None] + [lax.rem(me + n_plane - k, n_plane) for k in range(1, n_plane)]
    other = PAIR - 1 - fast

    def in_plane(k):
        return (slow * PAIR + ppeer[k] // n_zero, lax.rem(ppeer[k], n_zero))

    def along(k):
        return (speer[k] * PAIR + fast, zero)

    barrier = pltpu.get_barrier_semaphore()
    for k in range(1, n_slow):
        for f in range(PAIR):
            pl.semaphore_signal(barrier, inc=1, device_id=(speer[k] * PAIR + f, zero), device_id_type=MESH)
    for k in range(1, n_plane):
        pl.semaphore_signal(barrier, inc=1, device_id=in_plane(k), device_id_type=MESH)

    len_in = pltpu.make_async_copy(R.lengths_in, R.lengths, R.io_sem.at[2])
    len_in.start()
    small_in = []
    for i, (arg, _) in enumerate(VECS):
        c = pltpu.make_async_copy(R.params[arg], R.stage[i], R.stage_sem.at[i])
        c.start()
        small_in.append(c)
    nodes_in = pltpu.make_async_copy(R.nodes, R.nodes_v, R.io_sem.at[0])
    nodes_in.start()

    def rows_of(name, who):
        n = shard(name, n_zero)[0]
        return pl.ds(pl.multiple_of(who * n, n), n)

    own = {}
    for level in range(2):
        for i, name in enumerate(NAMES):
            own[level, name] = pltpu.make_async_copy(
                R.params[ARG[name]].at[level],
                R.weights[name].at[level, rows_of(name, zero), :],
                R.own_sem.at[level, i],
            )
    for level in range(2):
        for name in NAMES:
            own[level, name].start()
    cot_in = pltpu.make_async_copy(R.cotangent, R.cot_v, R.io_sem.at[1])
    cot_in.start()

    pl.semaphore_wait(barrier, PAIR * (n_slow - 1) + n_plane - 1)

    def place(level, name):
        return level * 7 + (6 if name == "vec" else NAMES.index(name))

    def weight_copy(level, name, k, who):
        i = place(level, name)
        if name == "vec":
            src, dst = R.vec_own.at[level], R.vec_in.at[level, who]
        else:
            src, dst = R.params[ARG[name]].at[level], R.weights[name].at[level, rows_of(name, who), :]
        return pltpu.make_async_remote_copy(
            src_ref=src,
            dst_ref=dst,
            send_sem=R.w_send.at[i, k - 1],
            recv_sem=R.w_recv.at[i, k - 1],
            device_id=(dp, zpeer[k]),
            device_id_type=MESH,
        )

    n_x = n_zero // 2
    mate = zero + 1 - 2 * lax.rem(zero, 2)
    xpeer = [None] + [lax.rem(zero + 2 * k, n_zero) for k in range(1, n_x)]
    xfrom = [None] + [lax.rem(zero + n_zero - 2 * k, n_zero) for k in range(1, n_x)]
    mate_from = [None] + [lax.rem(mate + n_zero - 2 * k, n_zero) for k in range(1, n_x)]

    def part_of(name, who):
        if name == "vec":
            return R.vec_in.at[0, who]
        return R.weights[name].at[0, rows_of(name, who), :]

    def own_part(name):
        return R.vec_own.at[0] if name == "vec" else R.params[ARG[name]].at[0]

    def x_copy(name, k, who):
        i = place(0, name)
        return pltpu.make_async_remote_copy(
            src_ref=own_part(name),
            dst_ref=part_of(name, who),
            send_sem=R.x_send.at[i, k - 1],
            recv_sem=R.x_recv.at[i, k - 1],
            device_id=(dp, xpeer[k]),
            device_id_type=MESH,
        )

    def mate_copy(name, k, who):
        i = place(0, name)
        return pltpu.make_async_remote_copy(
            src_ref=own_part(name) if k == 0 else part_of(name, xfrom[k]),
            dst_ref=part_of(name, who),
            send_sem=R.m_send.at[i, k],
            recv_sem=R.m_recv.at[i, k],
            device_id=(dp, mate),
            device_id_type=MESH,
        )

    def send_first(*names):
        for name in names:
            for k in range(1, n_x):
                x_copy(name, k, zero).start()
        for name in names:
            mate_copy(name, 0, zero).start()

    def relay_first(*names):
        for name in names:
            for k in range(1, n_x):
                x_copy(name, k, xfrom[k]).wait_recv()
                mate_copy(name, k, xfrom[k]).start()

    def take_first(*names):
        for name in names:
            if name != "vec":
                own[0, name].wait()
            mate_copy(name, 0, mate).wait_recv()
            for k in range(1, n_x):
                mate_copy(name, k, mate_from[k]).wait_recv()

    far_first = sorted(range(1, n_zero), key=lambda k: k in (1, n_zero - 1))

    def send_weights(level, *names):
        for name in names:
            for k in far_first:
                weight_copy(level, name, k, zero).start()

    def take_weights(level, *names):
        for name in names:
            if name != "vec":
                own[level, name].wait()
            for k in range(1, n_zero):
                weight_copy(level, name, k, zfrom[k]).wait_recv()

    send_first("k", "v", "q", "o")

    for c in small_in:
        c.wait()
    lane = lax.broadcasted_iota(jnp.int32, (2, D), 1)
    R.vec_own[...] = jnp.zeros((2, SMALL, D), F32)
    for i, (arg, row) in enumerate(VECS):
        x = R.stage[i][...]
        n = x.shape[1]
        x = jnp.concatenate([x, jnp.zeros((2, D - n), F32)], axis=1)
        x = pltpu.roll(x, lax.rem(zero * n, D), axis=1)
        if row != BU0:
            R.vec_own[:, row, :] = x
        else:
            first = zero * n < D
            R.vec_own[:, row, :] = jnp.where(first, x, 0.0)
            R.vec_own[:, row + 1, :] = jnp.where(first, 0.0, x)

    send_first("vec")

    len_in.wait()
    gm = group_mask()
    a = jnp.where(gm, 1.0 / HD, 0.0).astype(BF)
    R.A2[0:D, :] = a
    R.A2[D:, :] = a
    ln = [R.lengths[i] for i in range(SEGS)]
    st = [0]
    for i in range(SEGS):
        st.append(st[-1] + ln[i])
    inv = [1.0 / (jnp.full((1, D), ln[s], jnp.int32).astype(F32)) for s in range(SEGS)]

    def live(r0, n):
        s = r0 // BLK
        return lax.broadcasted_iota(jnp.int32, (n, D), 0) + (r0 - s * BLK) < ln[s]

    Ls, Tm = R.layers, R.temps
    Tm["A2"] = R.A2
    Ls[0]["XT"] = R.XT
    for y in (R.Y, R.Y2):
        y[TOK:, :] = jnp.zeros((y.shape[0] - TOK, D), F32)
    nodes_in.wait()
    for s in range(SEGS):
        x = R.nodes_v[pl.ds(st[s], BLK), :]
        Ls[0]["H"][s * BLK : (s + 1) * BLK, :] = x
        x = pack(x)
        Ls[0]["X"][s * BLK : (s + 1) * BLK, :] = x
        R.XT[:, s * BLK : (s + 1) * BLK] = x.T
    cot_in.wait()
    sum_e = zero8 = jnp.zeros((8, D), F32)
    for s in range(SEGS):
        x = jnp.where(live(s * BLK, BLK), R.cot_v[pl.ds(st[s], BLK), :], 0.0)
        Tm["E"][s * BLK : (s + 1) * BLK, :] = x
        Tm["ED"][s * BLK : (s + 1) * BLK, :] = pack(x)
        sum_e = sum_e + part(x)

    send_weights(0, "up", "dn")
    relay_first("k", "v", "vec", "q", "o")
    send_weights(1, "k", "v", "vec", "q", "o")
    vecs = [None, None]

    def take_vecs(level):
        x = R.vec_own[level]
        for k in range(1, n_zero):
            x = x + R.vec_in[level, zpeer[k]]
        R.vec[level] = x
        vecs[level] = R.vec.at[level]

    tiles = [(s, s * BLK) for s in range(SEGS)]

    def pipe(stages):
        kept = [None] * len(tiles)
        for t in range(len(tiles) + len(stages) - 1):
            for j, stage in enumerate(stages):
                if 0 <= t - j < len(tiles):
                    kept[t - j] = stage(tiles[t - j], kept[t - j])
        return kept

    for level in range(2):
        L = Ls[level]
        w = {n: R.weights[n].at[level] for n in NAMES}
        if level == 0:
            take_first("k", "v", "vec")
        else:
            take_weights(1, "k", "v", "vec", "q", "o")
        take_vecs(level)
        vec = vecs[level]
        prep_kv(L, w, vec, R.A2)
        if level == 0:
            take_first("q", "o")
        prep_qo(L, w, vec)
        for s, r in tiles:
            fwd_a(L, vec, R.A2, live, r, BLK, level == 1)
        for s in range(SEGS):
            fwd_s1(L, gm, inv, s)
        t2 = [fwd_s2(L, s) for s in range(SEGS)]
        for s in range(SEGS):
            fwd_s3(L, vec, s, t2[s])
        take_weights(level, "up", "dn")
        if level == 0:
            send_weights(1, "up", "dn")
        prep_ff(L, w)

        def middle(tile, _):
            return fwd_c1(L, *tile, BLK)

        def hidden(tile, mid):
            fwd_c2(L, vec, tile[1], BLK)
            return mid

        def close(tile, mid):
            if level == 0:
                fwd_c3(L, vec, Ls[1]["H"], mid, tile[1], BLK)
            else:
                R.Y[pl.ds(tile[1], BLK), :] = mid

        pipe([middle, hidden, close])

    def put(level, name, g):
        grp, at = places[level, name]
        n = shard(name, n_zero)[0]
        for p in range(n_zero):
            part_p = g[p * n : (p + 1) * n]
            if name == "up":
                R.gsend[grp][p, at : at + n, :] = part_p[:, :D]
                R.gsend[grp][p, at + n : at + 2 * n, :] = part_p[:, D:]
            else:
                R.gsend[grp][p, at : at + n, :] = part_p

    def plane_copy(grp, k, who):
        rows, src = pieces[grp], R.gsend[grp].at[lax.rem(ppeer[k], n_zero)]
        if GROUPS[grp][1]:
            src = src.at[pl.ds(pl.multiple_of(ppeer[k] // n_zero * rows, 8), rows), :]
        return pltpu.make_async_remote_copy(
            src_ref=src,
            dst_ref=R.gplane[grp].at[who],
            send_sem=R.p_send.at[grp, k - 1],
            recv_sem=R.p_recv.at[grp, k - 1],
            device_id=in_plane(k),
            device_id_type=MESH,
        )

    def slow_copy(grp, k, who):
        return pltpu.make_async_remote_copy(
            src_ref=R.gslow[grp].at[slow],
            dst_ref=R.gslow[grp].at[who],
            send_sem=R.s_send.at[grp, k - 1],
            recv_sem=R.s_recv.at[grp, k - 1],
            device_id=along(k),
            device_id_type=MESH,
        )

    dpeer = [None] + [lax.rem(dp + k, n_dp) for k in range(1, n_dp)]
    dfrom = [None] + [lax.rem(dp + n_dp - k, n_dp) for k in range(1, n_dp)]

    def dp_copy(grp, k, who):
        return pltpu.make_async_remote_copy(
            src_ref=R.gslow[grp].at[dp],
            dst_ref=R.gslow[grp].at[who],
            send_sem=R.s_send.at[grp, k - 1],
            recv_sem=R.s_recv.at[grp, k - 1],
            device_id=(dpeer[k], zero),
            device_id_type=MESH,
        )

    def half_of(grp, who):
        rows = pieces[grp]
        return R.fin_out[grp].at[pl.ds(pl.multiple_of(who * rows, 8), rows), :]

    def pair_copy(grp, who):
        return pltpu.make_async_remote_copy(
            src_ref=half_of(grp, fast),
            dst_ref=half_of(grp, who),
            send_sem=R.f_send.at[grp],
            recv_sem=R.f_recv.at[grp],
            device_id=(slow * PAIR + other, zero),
            device_id_type=MESH,
        )

    def start_plane(grp):
        for k in range(1, n_plane):
            plane_copy(grp, k, me).start()

    def start_slow(grp):
        rows = pieces[grp]
        at = pl.multiple_of(fast * rows, 8) if GROUPS[grp][1] else 0
        R.gplane[grp][me] = R.gsend[grp][zero, pl.ds(at, rows), :]
        for k in range(1, n_plane):
            plane_copy(grp, k, pfrom[k]).wait_recv()
        x = R.gplane[grp][0]
        for j in range(1, n_plane):
            x = x + R.gplane[grp][j]
        if GROUPS[grp][1] == 2:
            R.gslow[grp][dp] = x
            for k in range(1, n_dp):
                dp_copy(grp, k, dp).start()
        else:
            R.gslow[grp][slow] = x
            for k in range(1, n_slow):
                slow_copy(grp, k, slow).start()

    def start_pair(grp):
        if GROUPS[grp][1] == 2:
            for k in range(1, n_dp):
                dp_copy(grp, k, dfrom[k]).wait_recv()
            rows = pieces[grp]
            for f in range(PAIR):
                x = R.gslow[grp][f]
                for j in range(1, n_slow):
                    x = x + R.gslow[grp][j * PAIR + f]
                R.fin_out[grp][f * rows : (f + 1) * rows, :] = x
            return
        for k in range(1, n_slow):
            slow_copy(grp, k, sfrom[k]).wait_recv()
        x = R.gslow[grp][0]
        for j in range(1, n_slow):
            x = x + R.gslow[grp][j]
        if GROUPS[grp][1]:
            R.fin_out[grp][pl.ds(pl.multiple_of(fast * pieces[grp], 8), pieces[grp]), :] = x
            pair_copy(grp, fast).start()
        else:
            R.fin_out[grp][...] = x

    def end_pair(grp):
        if GROUPS[grp][1] == 1:
            pair_copy(grp, other).wait_recv()

    def hand_out_vectors():
        small = []
        for level in range(2):
            g, at = places[level, "small"]
            small.append(R.fin_out[g][at : at + SMALL, :])
        for (_, row), out in zip(VECS, R.vec_out):
            n = out.shape[1]
            x = jnp.concatenate([s[row : row + 1, :] for s in small], axis=0)
            if row == BU0:
                x1 = jnp.concatenate([s[row + 1 : row + 2, :] for s in small], axis=0)
                x = jnp.where(zero * n < D, x, x1)
            x = pltpu.roll(x, lax.rem(D - lax.rem(zero * n, D), D), axis=1)
            out[...] = x[:, :n]

    shift = [jnp.minimum(BLK * s - st[s], (BLK - 256) * s) for s in range(SEGS)]

    def unpack(Y, base):
        lo, hi = (0, 256, 512, 768), (512, 1024, 1536, 2048)
        step = 256
        for t0 in range(0, TOK, step):
            it = lax.broadcasted_iota(jnp.int32, (step, D), 0) + t0
            x = base[t0 : t0 + step, :]
            for s in range(SEGS):
                if t0 < hi[s] and t0 + step > lo[s]:
                    y = Y[pl.ds(t0 + shift[s], step), :]
                    x = jnp.where((it >= st[s]) & (it < st[s + 1]), y, x)
            base[t0 : t0 + step, :] = x

    for level in (1, 0):
        L, vec = Ls[level], vecs[level]
        w = {n: R.weights[n].at[level] for n in NAMES}
        prep_back(L, w)
        put(level, "dn", grad_down(L, Tm))

        def feed(tile, _):
            return bwd_a1(L, Tm, tile[1], BLK)

        def after(tile, su):
            return su, bwd_a2(L, Tm, tile[1], BLK)

        sums = pipe([feed, after])
        su = sum((x[0] for x in sums), jnp.zeros((8, FF), F32))
        sc = [x[1] for x in sums]
        put(level, "up", grad_up(L, Tm))
        if level == 0:
            start_plane(2)
            start_slow(0)
        hp = [bwd_s1(L, Tm, s, sc[s]) for s in range(SEGS)]
        for s in range(SEGS):
            bwd_s2(L, Tm, s, hp[s])
        gq, gbq, go = bwd_s4(L, Tm)
        put(level, "q", gq)
        put(level, "o", go)
        for s in range(SEGS):
            bwd_s3(L, Tm, gm, inv, s)
        start_plane(0 if level == 1 else 3)
        a1 = R.A2[0:D, :]
        ss = [zero8] * 6

        def key_value(i):
            for s, r in tiles:
                o = bwd_b(L, vec, Tm, R.A2, s, r, BLK, i)
                for j in range(3):
                    ss[3 * i + j] = ss[3 * i + j] + o[j]

        key_value(0)
        key_value(1)
        rows = [jnp.zeros((1, D), F32)] * SMALL
        rows[BQ], rows[BK], rows[BV] = gbq, one(center(ss[2], a1)), one(center(ss[5], a1))
        rows[BO] = one(sc[0] + sc[1] + sc[2] + sc[3])
        rows[SK], rows[GK], rows[SV], rows[GV] = one(ss[0]), one(ss[1]), one(ss[3]), one(ss[4])
        rows[BD] = one(sum_e)
        u = one(su)
        rows[BU0], rows[BU1] = u[:, :D], u[:, D:]
        small = jnp.concatenate(rows, axis=0)
        grp, at = places[level, "small"]
        for p in range(n_zero):
            R.gsend[grp][p, at : at + SMALL, :] = small
        if level == 1:
            gk, gv = grad_both(L, Tm)
            put(level, "k", center(gk, a1))
            put(level, "v", center(gv, a1))
            start_plane(1)
        else:
            put(level, "k", center(grad_one(L, Tm, 0), a1))
            put(level, "v", center(grad_one(L, Tm, 1), a1))
            start_plane(4)
            start_slow(1)
        if level == 1:
            sum_e = zero8
            for s, r in tiles:
                sum_e = sum_e + bwd_x_next(L, Tm, s, r, BLK)
        else:
            for s, r in tiles:
                bwd_x(L, Tm, R.Y2, s, r, BLK)

    start_slow(2)
    start_slow(3)
    start_pair(0)
    start_pair(1)
    for s, r in tiles:
        fwd_c3(Ls[1], vecs[1], R.Y, R.Y[pl.ds(r, BLK), :], r, BLK)
    unpack(R.Y, R.nodes_v)
    store_out = pltpu.make_async_copy(R.nodes_v, R.out, R.io_sem.at[3])
    store_out.start()
    start_slow(4)
    start_pair(2)
    start_pair(3)
    unpack(R.Y2, R.cot_v)
    store_gx = pltpu.make_async_copy(R.cot_v, R.gx, R.io_sem.at[4])
    store_gx.start()
    start_pair(4)
    end_pair(0)
    end_pair(1)
    end_pair(2)
    end_pair(3)
    end_pair(4)
    hand_out_vectors()
    for name in NAMES + ("vec",):
        if name in ("up", "dn"):
            for k in range(1, n_zero):
                weight_copy(0, name, k, zero).wait_send()
        else:
            mate_copy(name, 0, zero).wait_send()
            for k in range(1, n_x):
                x_copy(name, k, zero).wait_send()
                mate_copy(name, k, xfrom[k]).wait_send()
        for k in range(1, n_zero):
            weight_copy(1, name, k, zero).wait_send()
    for g in range(NG):
        for k in range(1, n_plane):
            plane_copy(g, k, me).wait_send()
        if GROUPS[g][1] == 2:
            for k in range(1, n_dp):
                dp_copy(g, k, dp).wait_send()
            continue
        for k in range(1, n_slow):
            slow_copy(g, k, slow).wait_send()
        if GROUPS[g][1]:
            pair_copy(g, fast).wait_send()
    store_out.wait()
    store_gx.wait()


def finish_kernel(n_zero, out, gx, fin, vec, outs, sem):
    places, _, _ = group_layout(n_zero)
    copies = []

    def copy(src, dst):
        c = pltpu.make_async_copy(src, dst, sem.at[len(copies)])
        c.start()
        copies.append(c)

    half = TOK // 2
    for i in range(2):
        copy(out.at[pl.ds(i * half, half), :], outs[0].at[pl.ds(i * half, half), :])
        copy(gx.at[pl.ds(i * half, half), :], outs[1].at[pl.ds(i * half, half), :])
    for name, arg in ARG.items():
        for level in range(2):
            g, at = places[level, name]
            n = shard(name, n_zero)[0]
            if name == "up":
                for h in range(2):
                    copy(
                        fin[g].at[pl.ds(at + h * n, n), :],
                        outs[2 + arg].at[level, :, pl.ds(h * D, D)],
                    )
            else:
                copy(fin[g].at[pl.ds(at, n), :], outs[2 + arg].at[level])
    for (arg, _), v in zip(VECS, vec):
        copy(v, outs[2 + arg])
    for c in copies:
        c.wait()


def make_fused(n_dp, n_zero, params):
    places, sizes, pieces = group_layout(n_zero)
    dma = pltpu.SemaphoreType.DMA
    any_ = pl.BlockSpec(memory_space=pl.ANY)
    order, scratch = [], []

    def add(name, shape):
        order.append(name)
        scratch.append(shape)

    n_params = len(params)
    out_shape = [VM((TOK, D), F32)] * 2 + [VM((p, D), F32) for p in sizes]
    out_shape += [VM(params[arg].shape, F32) for arg, _ in VECS]
    ls, ts = list(LAYER_SCRATCH), [n for n in TMP_SCRATCH if n != "A2"]
    for level in range(2):
        for n in ls:
            add(("layer", level, n), VM(*LAYER_SCRATCH[n]))
    for n in ts:
        add(("temp", n), VM(*TMP_SCRATCH[n]))
    add("lengths", pltpu.SMEM((SEGS,), jnp.int32))
    add("A2", VM(*TMP_SCRATCH["A2"]))
    add("Y", VM((TOK + 768, D), F32))
    add("XT", VM((2 * D, TOK), BF))
    add("Y2", VM((TOK + 768, D), F32))
    add("nodes_v", VM((TOK, D), F32))
    add("cot_v", VM((TOK, D), F32))
    for i, (arg, _) in enumerate(VECS):
        add(("stage", i), VM(params[arg].shape, F32))
    for n in NAMES:
        rows, cols = shard(n, n_zero)
        add(("weights", n), VM((2, rows * n_zero, cols), F32))
    add("vec_own", VM((2, SMALL, D), F32))
    add("vec_in", VM((2, n_zero, SMALL, D), F32))
    add("vec", VM((2, SMALL, D), F32))
    for g in range(NG):
        add(("gsend", g), VM((n_zero, sizes[g], D), F32))
        add(("gplane", g), VM((PAIR * n_zero, pieces[g], D), F32))
        add(("gslow", g), VM((n_dp, pieces[g], D), F32))
    add("stage_sem", dma((len(VECS),)))
    add("io_sem", dma((5,)))
    add("own_sem", dma((2, 6)))
    add("w_send", dma((14, n_zero - 1)))
    add("w_recv", dma((14, n_zero - 1)))
    for n, m in (("x", n_zero // 2 - 1), ("m", n_zero // 2)):
        add(n + "_send", dma((7, m)))
        add(n + "_recv", dma((7, m)))
    for n, m in (("p", PAIR * n_zero), ("s", n_dp)):
        add(n + "_send", dma((NG, m - 1)))
        add(n + "_recv", dma((NG, m - 1)))
    add("f_send", dma((NG,)))
    add("f_recv", dma((NG,)))

    def body(*refs):
        lengths_in, nodes, cot = refs[:3]
        pr = refs[3 : 3 + n_params]
        n_outs = 2 + NG + len(VECS)
        outs = refs[3 + n_params : 3 + n_outs + n_params]
        rest = refs[3 + n_outs + n_params :]
        simple = dict(lengths_in=lengths_in, nodes=nodes, cotangent=cot, params=pr, out=outs[0], gx=outs[1], fin_out=outs[2 : 2 + NG], vec_out=outs[2 + NG :])
        layers, temps = [{}, {}], {}
        simple.update(layers=layers, temps=temps, stage=[None] * len(VECS), weights={})
        for n in ("gsend", "gplane", "gslow"):
            simple[n] = [None] * NG
        for key, ref in zip(order, rest):
            if isinstance(key, str):
                simple[key] = ref
            elif key[0] == "layer":
                layers[key[1]][key[2]] = ref
            elif key[0] == "temp":
                temps[key[1]] = ref
            else:
                simple[key[0]][key[1]] = ref
        fused_kernel(n_dp, n_zero, list(simple), *simple.values())

    call = pl.pallas_call(
        body,
        out_shape=out_shape,
        in_specs=[any_] * (3 + n_params),
        out_specs=[any_] * 2 + [pl.BlockSpec(memory_space=pltpu.VMEM)] * (NG + len(VECS)),
        scratch_shapes=scratch,
        compiler_params=pltpu.CompilerParams(
            collective_id=0, has_side_effects=True, vmem_limit_bytes=56 * 1024 * 1024
        ),
    )
    return call


def make_finish(n_zero, params):
    any_ = pl.BlockSpec(memory_space=pl.ANY)
    out_shape = [jax.ShapeDtypeStruct((TOK, D), F32)] * 2
    out_shape += [jax.ShapeDtypeStruct(p.shape, F32) for p in params]
    n_ins = 2 + NG + len(VECS)

    def body(*refs):
        out, gx = refs[:2]
        fin, vec = refs[2 : 2 + NG], refs[2 + NG : n_ins]
        finish_kernel(n_zero, out, gx, fin, vec, refs[n_ins:-1], refs[-1])

    call = pl.pallas_call(
        body,
        out_shape=out_shape,
        in_specs=[any_] * n_ins,
        out_specs=[any_] * len(out_shape),
        scratch_shapes=[pltpu.SemaphoreType.DMA((28,))],
    )
    return lambda *xs: call(*[pltpu.with_memory_space_constraint(x, pltpu.VMEM) for x in xs])


def solution(mesh):
    n_dp, n_zero = mesh.shape["dp"], mesh.shape["zero"]
    wide, flat = P(None, "zero", None), P(None, "zero")
    params = (wide,) * 4 + (flat,) * 8 + (wide, flat, wide, flat)
    rows = P(("dp", "zero"), None)

    def local(nodes, cotangent, lengths, *params):
        results = make_fused(n_dp, n_zero, params)(lengths, nodes, cotangent, *params)
        return tuple(make_finish(n_zero, params)(*results))

    return jax.shard_map(
        local,
        mesh=mesh,
        in_specs=(rows, rows, P(("dp", "zero"))) + params,
        out_specs=(rows, rows) + params,
        check_vma=False,
    )
```

```python
import jax
import jax.numpy as jnp
from jax import lax
from jax.experimental import pallas as pl
from jax.experimental.pallas import tpu as pltpu
from jax.sharding import PartitionSpec as P

D=128; FF=256; SEGS=4; BLK=512; TOK=2048; HD=32
F32=jnp.float32; BF=jnp.bfloat16
VM=pltpu.VMEM

def split(x):
    hi=x.astype(BF); lo=(x-hi.astype(F32)).astype(BF)
    return hi,lo
def cat0(*x): return jnp.concatenate(x,axis=0)
def cat1(*x): return jnp.concatenate(x,axis=1)
def pack(x):
    return cat1(*split(x))
def quad(x):
    p=pack(x)
    return cat0(p,p)
def quad_t(x):
    h,l=split(x)
    return cat0(cat1(h,h),cat1(l,l))
def mm(a,b):
    return jnp.dot(a,b,preferred_element_type=F32)
def tn(a,b):
    return lax.dot_general(a,b,(((0,),(0,)),((),())),preferred_element_type=F32)
def nt(a,b):
    return lax.dot_general(a,b,(((1,),(1,)),((),())),preferred_element_type=F32)
def halves(r):
    n=r.shape[1]//2
    return r[:,:n]+r[:,n:]
def quads(r):
    m=r.shape[0]//2
    return halves(r[:m]+r[m:])
def part(x):
    return jnp.sum(x.reshape(x.shape[0]//8,8,x.shape[1]),axis=0)
def one(x):
    return jnp.sum(x,axis=0,keepdims=True)
def group_mask():
    r=lax.broadcasted_iota(jnp.int32,(D,D),0)//HD
    c=lax.broadcasted_iota(jnp.int32,(D,D),1)//HD
    return r==c
def center(x,a1):
    h=x.astype(BF); r=x-h.astype(F32); m=r.astype(BF); lo=(r-m.astype(F32)).astype(BF)
    return x-(mm(h,a1)+mm(m,a1)+mm(lo,a1))

BQ,BK,BV,BO,GK,SK,GV,SV,BD,BU0,BU1=range(11)
AUG=D+16

LAYER_SCRATCH=dict(
    X=((TOK,2*D),BF), H=((TOK,D),F32), NK=((TOK,D),F32), NV=((TOK,D),F32), RK=((TOK,D),F32), RV=((TOK,D),F32),
    KN=((TOK,2*D),BF), VN=((TOK,2*D),BF), MD=((TOK,2*D),BF), ACT=((TOK,2*FF),BF), DG=((TOK,FF),F32),
    WKV=((2*D,4*D),BF), WUP=((2*D,2*FF),BF), WDN=((2*FF,2*D),BF), WDNT=((2*FF,2*D),BF), WUPT=((2*D,2*FF),BF),
    WKVT=((2*D,4*D),BF), WO2=((2*D,2*D),BF), WOT2=((2*D,2*D),BF), WQA=((AUG,2*D),BF),
    SP=((SEGS*D,2*D),BF), TP=((2*D,SEGS*D),BF), UT2=((SEGS,2*D,2*D),BF), U2=((SEGS,2*D,2*D),BF), UB=((SEGS,8,D),F32),
    CB=((8,D),F32),
)
TMP_SCRATCH=dict(
    E=((TOK,D),F32), ED=((TOK,2*D),BF), EP=((TOK,2*FF),BF), EM=((TOK,D),F32), EO=((TOK,2*D),BF), FKV=((TOK,4*D),BF),
    HT=((2*AUG,SEGS*D),BF), PP=((SEGS*D,2*D),BF), ES=((2,SEGS,2*D,2*D),BF),
    A2=((2*D,D),BF),
)

def prep_kv(L,w,vec,A2):
    a1=A2[0:D,:]
    b8=cat0(vec[BK:BV+1,:],jnp.zeros((6,D),F32))
    L['CB'][...]=center(b8,a1)
    wk=center(w['k'][...],a1); wv=center(w['v'][...],a1)
    kh,kl=split(wk); vh,vl=split(wv)
    kv=cat1(kh,vh,kl,vl)
    L['WKV'][0:D,:]=kv; L['WKV'][D:,:]=kv
    L['WKVT'][0:D,:]=cat1(kh,kh,vh,vh); L['WKVT'][D:,:]=cat1(kl,kl,vl,vl)

def prep_qo(L,w,vec):
    wo=w['o'][...]
    L['WO2'][...]=quad(wo); L['WOT2'][...]=quad_t(wo)
    L['WQA'][0:D,:]=pack(w['q'][...])
    L['WQA'][D:,:]=pack(cat0(vec[BQ:BQ+1,:],jnp.zeros((15,D),F32)))

def prep_ff(L,w):
    L['WUP'][...]=quad(w['up'][...])
    L['WDN'][...]=quad(w['dn'][...])

def prep_back(L,w):
    L['WUPT'][...]=quad_t(w['up'][...])
    L['WDNT'][...]=quad_t(w['dn'][...])

def fwd_a(L,vec,A2,live,r0,n,fresh):
    rows=pl.ds(r0,n)
    if fresh:
        x=pack(L['H'][rows,:])
        L['X'][rows,:]=x
    else:
        x=L['X'][rows,:]
    r=mm(x,L['WKV'][...])
    a2=A2[...]
    lv=live(r0,n)
    for i,(N,R,O,g,s) in enumerate((('NK','RK','KN',GK,SK),('NV','RV','VN',GV,SV))):
        c=r[:,i*D:(i+1)*D]+r[:,(i+2)*D:(i+3)*D]+L['CB'][i:i+1,:]
        rs=lax.rsqrt(mm(pack(c*c),a2)+1e-5)
        nn=c*rs
        L[R][rows,:]=rs; L[N][rows,:]=nn
        y=jnp.where(lv,nn*vec[g:g+1,:]+vec[s:s+1,:],0.0)
        L[O][rows,:]=pack(y)

def fwd_s1(L,gm,inv,s):
    rows=pl.ds(s*BLK,BLK)
    S=jnp.where(gm,quads(tn(L['KN'][rows,:],L['VN'][rows,:]))*inv[s],0.0)
    L['SP'][s*D:(s+1)*D,:]=pack(S)

def fwd_s2(L,s):
    h,l=split(halves(mm(L['SP'][s*D:(s+1)*D,:],L['WO2'][...])))
    L['TP'][0:D,s*D:(s+1)*D]=h; L['TP'][D:,s*D:(s+1)*D]=l
    row=cat1(h,l)
    return cat0(row,row)

def fwd_s3(L,vec,s,t2):
    us=halves(mm(L['WQA'][...],t2))
    L['UB'][s]=us[D:D+8]+vec[BO:BO+1,:]
    h,l=split(us[:D])
    p=cat1(h,l)
    L['U2'][s,0:D,:]=p; L['U2'][s,D:,:]=p
    L['UT2'][s,0:D,:]=cat1(h,h); L['UT2'][s,D:,:]=cat1(l,l)

def fwd_c1(L,s,r0,n):
    rows=pl.ds(r0,n)
    mid=L['H'][rows,:]+halves(mm(L['X'][rows,:],L['U2'][s]))+L['UB'][s,0:1,:]
    L['MD'][rows,:]=pack(mid)
    return mid

def fwd_c2(L,vec,r0,n):
    rows=pl.ds(r0,n)
    bu=cat1(vec[BU0:BU0+1,:],vec[BU1:BU1+1,:])
    z=halves(mm(L['MD'][rows,:],L['WUP'][...]))+bu
    z2=z*z
    c0=0.7978845608028654
    t=jnp.tanh(z*(c0+(c0*0.044715)*z2))
    p=0.5*t+0.5
    act=z*p
    L['DG'][rows,:]=p+act*(1.0-p)*((2*c0)+(6*c0*0.044715)*z2)
    L['ACT'][rows,:]=pack(act)

def fwd_c3(L,vec,OUT,mid,r0,n):
    rows=pl.ds(r0,n)
    OUT[rows,:]=mid+halves(mm(L['ACT'][rows,:],L['WDN'][...]))+vec[BD:BD+1,:]

def bwd_a1(L,Tm,r0,n):
    rows=pl.ds(r0,n)
    ep=halves(nt(Tm['ED'][rows,:],L['WDNT'][...]))*L['DG'][rows,:]
    Tm['EP'][rows,:]=pack(ep)
    return part(ep)

def bwd_a2(L,Tm,r0,n):
    rows=pl.ds(r0,n)
    em=Tm['E'][rows,:]+halves(nt(Tm['EP'][rows,:],L['WUPT'][...]))
    Tm['EM'][rows,:]=em
    Tm['EO'][rows,:]=pack(em)
    return part(em)

def bwd_s1(L,Tm,s,c):
    rows=pl.ds(s*BLK,BLK)
    if 'XT' in L:
        H=quads(mm(L['XT'][:,s*BLK:(s+1)*BLK],Tm['EO'][rows,:]))
    else:
        H=quads(tn(L['X'][rows,:],Tm['EO'][rows,:]))
    h,l=split(cat0(H,one(c),jnp.zeros((15,D),F32)))
    Tm['HT'][0:AUG,s*D:(s+1)*D]=h; Tm['HT'][AUG:,s*D:(s+1)*D]=l
    return cat1(h,l)

def bwd_s2(L,Tm,s,hp):
    Tm['PP'][s*D:(s+1)*D,:]=pack(quads(tn(L['WQA'][...],hp)))

def bwd_s3(L,Tm,gm,inv,s):
    e=jnp.where(gm,halves(nt(Tm['PP'][s*D:(s+1)*D,:],L['WOT2'][...]))*inv[s],0.0)
    h,l=split(e); p=cat1(h,l)
    Tm['ES'][0,s,0:D,:]=cat1(h,h); Tm['ES'][0,s,D:,:]=cat1(l,l)
    Tm['ES'][1,s,0:D,:]=p; Tm['ES'][1,s,D:,:]=p

def bwd_s4(L,Tm):
    go=quads(tn(L['SP'][...],Tm['PP'][...]))
    gq=halves(nt(Tm['HT'][...],L['TP'][...]))
    gq=gq[:AUG]+gq[AUG:]
    return gq[:D],gq[D:D+1],go

def bwd_b(L,vec,Tm,A2,s,r0,n,i):
    rows=pl.ds(r0,n)
    N,R,O,g,dot=(('NK','RK','VN',GK,nt),('NV','RV','KN',GV,mm))[i]
    en=halves(dot(L[O][rows,:],Tm['ES'][i,s]))
    nn=L[N][rows,:]
    m=en*vec[g:g+1,:]
    mn=m*nn
    av=mm(pack(mn),A2[...])
    f=L[R][rows,:]*(m-nn*av)
    Tm['FKV'][rows,i*2*D:(i+1)*2*D]=pack(f)
    return part(en),part(en*nn),part(f)

def bwd_x(L,Tm,DX,s,r0,n):
    rows=pl.ds(r0,n)
    dx=Tm['EM'][rows,:]+halves(nt(Tm['FKV'][rows,:],L['WKVT'][...])+nt(Tm['EO'][rows,:],L['UT2'][s]))
    DX[rows,:]=dx
    return dx

def bwd_x_next(L,Tm,s,r0,n):
    dx=bwd_x(L,Tm,Tm['E'],s,r0,n)
    Tm['ED'][pl.ds(r0,n),:]=pack(dx)
    return part(dx)

def grad_up(L,Tm):
    return quads(tn(L['MD'][...],Tm['EP'][...]))

def grad_down(L,Tm):
    return quads(tn(L['ACT'][...],Tm['ED'][...]))

def grad_both(L,Tm):
    g=mm(L['XT'][...],Tm['FKV'][...]) if 'XT' in L else tn(L['X'][...],Tm['FKV'][...])
    g=g[:D]+g[D:]
    return halves(g[:,:2*D]),halves(g[:,2*D:])

def grad_one(L,Tm,i):
    return quads(mm(L['XT'][...],Tm['FKV'][:,i*2*D:(i+1)*2*D]))


MESH = pl.DeviceIdType.MESH
NAMES = ("k", "v", "q", "o", "up", "dn")
ARG = dict(q=0, k=1, v=2, o=3, up=12, dn=14)
VECS = ((4, BQ), (5, BK), (6, BV), (7, BO), (8, GK), (9, SK), (10, GV), (11, SV), (15, BD), (13, BU0))
SMALL = 16
GROUPS = (
    (((1, "up"), (1, "dn"), (1, "q"), (1, "o")), True),
    (((1, "k"), (1, "v"), (1, "small")), True),
    (((0, "dn"), (0, "up")), True),
    (((0, "q"), (0, "o")), True),
    (((0, "k"), (0, "v"), (0, "small")), 2),
)
PAIR = 2
NG = len(GROUPS)


def shard(name, n_zero):
    if name == "dn":
        return FF // n_zero, D
    return D // n_zero, FF if name == "up" else D


def group_layout(n_zero):
    places, sizes, pieces = {}, [], []
    for g, (members, halved) in enumerate(GROUPS):
        at = 0
        for item in members:
            places[item] = (g, at)
            if item[1] == "small":
                at += SMALL
            else:
                rows, cols = shard(item[1], n_zero)
                at += rows * cols // D
        at = -(-at // 16) * 16
        sizes.append(at)
        pieces.append(at // PAIR if halved else at)
    return places, sizes, pieces


class Names:
    pass


def fused_kernel(n_dp, n_zero, order, *refs):
    R = Names()
    for name, ref in zip(order, refs):
        setattr(R, name, ref)
    places, sizes, pieces = group_layout(n_zero)
    dp, zero = lax.axis_index("dp"), lax.axis_index("zero")
    zpeer = [None] + [lax.rem(zero + k, n_zero) for k in range(1, n_zero)]
    zfrom = [None] + [lax.rem(zero + n_zero - k, n_zero) for k in range(1, n_zero)]
    fast, slow, n_slow = lax.rem(dp, PAIR), dp // PAIR, n_dp // PAIR
    n_plane = PAIR * n_zero
    me = fast * n_zero + zero
    ppeer = [None] + [lax.rem(me + k, n_plane) for k in range(1, n_plane)]
    speer = [None] + [lax.rem(slow + k, n_slow) for k in range(1, n_slow)]
    sfrom = [None] + [lax.rem(slow + n_slow - k, n_slow) for k in range(1, n_slow)]
    pfrom = [None] + [lax.rem(me + n_plane - k, n_plane) for k in range(1, n_plane)]
    other = PAIR - 1 - fast

    def in_plane(k):
        return (slow * PAIR + ppeer[k] // n_zero, lax.rem(ppeer[k], n_zero))

    def along(k):
        return (speer[k] * PAIR + fast, zero)

    barrier = pltpu.get_barrier_semaphore()
    for k in range(1, n_slow):
        for f in range(PAIR):
            pl.semaphore_signal(barrier, inc=1, device_id=(speer[k] * PAIR + f, zero), device_id_type=MESH)
    for k in range(1, n_plane):
        pl.semaphore_signal(barrier, inc=1, device_id=in_plane(k), device_id_type=MESH)

    len_in = pltpu.make_async_copy(R.lengths_in, R.lengths, R.io_sem.at[2])
    len_in.start()
    small_in = []
    for i, (arg, _) in enumerate(VECS):
        c = pltpu.make_async_copy(R.params[arg], R.stage[i], R.stage_sem.at[i])
        c.start()
        small_in.append(c)
    nodes_in = pltpu.make_async_copy(R.nodes, R.nodes_v, R.io_sem.at[0])
    nodes_in.start()

    def rows_of(name, who):
        n = shard(name, n_zero)[0]
        return pl.ds(pl.multiple_of(who * n, n), n)

    own = {}
    for level in range(2):
        for i, name in enumerate(NAMES):
            own[level, name] = pltpu.make_async_copy(
                R.params[ARG[name]].at[level],
                R.weights[name].at[level, rows_of(name, zero), :],
                R.own_sem.at[level, i],
            )
    for level in range(2):
        for name in NAMES:
            own[level, name].start()
    cot_in = pltpu.make_async_copy(R.cotangent, R.cot_v, R.io_sem.at[1])
    cot_in.start()

    pl.semaphore_wait(barrier, PAIR * (n_slow - 1) + n_plane - 1)

    def place(level, name):
        return level * 7 + (6 if name == "vec" else NAMES.index(name))

    def weight_copy(level, name, k, who):
        i = place(level, name)
        if name == "vec":
            src, dst = R.vec_own.at[level], R.vec_in.at[level, who]
        else:
            src, dst = R.params[ARG[name]].at[level], R.weights[name].at[level, rows_of(name, who), :]
        return pltpu.make_async_remote_copy(
            src_ref=src,
            dst_ref=dst,
            send_sem=R.w_send.at[i, k - 1],
            recv_sem=R.w_recv.at[i, k - 1],
            device_id=(dp, zpeer[k]),
            device_id_type=MESH,
        )

    n_x = n_zero // 2
    mate = zero + 1 - 2 * lax.rem(zero, 2)
    xpeer = [None] + [lax.rem(zero + 2 * k, n_zero) for k in range(1, n_x)]
    xfrom = [None] + [lax.rem(zero + n_zero - 2 * k, n_zero) for k in range(1, n_x)]
    mate_from = [None] + [lax.rem(mate + n_zero - 2 * k, n_zero) for k in range(1, n_x)]

    def part_of(name, who):
        if name == "vec":
            return R.vec_in.at[0, who]
        return R.weights[name].at[0, rows_of(name, who), :]

    def own_part(name):
        return R.vec_own.at[0] if name == "vec" else R.params[ARG[name]].at[0]

    def x_copy(name, k, who):
        i = place(0, name)
        return pltpu.make_async_remote_copy(
            src_ref=own_part(name),
            dst_ref=part_of(name, who),
            send_sem=R.x_send.at[i, k - 1],
            recv_sem=R.x_recv.at[i, k - 1],
            device_id=(dp, xpeer[k]),
            device_id_type=MESH,
        )

    def mate_copy(name, k, who):
        i = place(0, name)
        return pltpu.make_async_remote_copy(
            src_ref=own_part(name) if k == 0 else part_of(name, xfrom[k]),
            dst_ref=part_of(name, who),
            send_sem=R.m_send.at[i, k],
            recv_sem=R.m_recv.at[i, k],
            device_id=(dp, mate),
            device_id_type=MESH,
        )

    def send_first(*names):
        for name in names:
            for k in range(1, n_x):
                x_copy(name, k, zero).start()
        for name in names:
            mate_copy(name, 0, zero).start()

    def relay_first(*names):
        for name in names:
            for k in range(1, n_x):
                x_copy(name, k, xfrom[k]).wait_recv()
                mate_copy(name, k, xfrom[k]).start()

    def take_first(*names):
        for name in names:
            if name != "vec":
                own[0, name].wait()
            mate_copy(name, 0, mate).wait_recv()
            for k in range(1, n_x):
                mate_copy(name, k, mate_from[k]).wait_recv()

    far_first = sorted(range(1, n_zero), key=lambda k: k in (1, n_zero - 1))

    def send_weights(level, *names):
        for name in names:
            for k in far_first:
                weight_copy(level, name, k, zero).start()

    def take_weights(level, *names):
        for name in names:
            if name != "vec":
                own[level, name].wait()
            for k in range(1, n_zero):
                weight_copy(level, name, k, zfrom[k]).wait_recv()

    send_first("k", "v", "q", "o")

    for c in small_in:
        c.wait()
    lane = lax.broadcasted_iota(jnp.int32, (2, D), 1)
    R.vec_own[...] = jnp.zeros((2, SMALL, D), F32)
    for i, (arg, row) in enumerate(VECS):
        x = R.stage[i][...]
        n = x.shape[1]
        x = jnp.concatenate([x, jnp.zeros((2, D - n), F32)], axis=1)
        x = pltpu.roll(x, lax.rem(zero * n, D), axis=1)
        if row != BU0:
            R.vec_own[:, row, :] = x
        else:
            first = zero * n < D
            R.vec_own[:, row, :] = jnp.where(first, x, 0.0)
            R.vec_own[:, row + 1, :] = jnp.where(first, 0.0, x)

    send_first("vec")

    len_in.wait()
    gm = group_mask()
    a = jnp.where(gm, 1.0 / HD, 0.0).astype(BF)
    R.A2[0:D, :] = a
    R.A2[D:, :] = a
    ln = [R.lengths[i] for i in range(SEGS)]
    st = [0]
    for i in range(SEGS):
        st.append(st[-1] + ln[i])
    inv = [1.0 / (jnp.full((1, D), ln[s], jnp.int32).astype(F32)) for s in range(SEGS)]

    def live(r0, n):
        s = r0 // BLK
        return lax.broadcasted_iota(jnp.int32, (n, D), 0) + (r0 - s * BLK) < ln[s]

    Ls, Tm = R.layers, R.temps
    Tm["A2"] = R.A2
    Ls[0]["XT"] = R.XT
    for y in (R.Y, R.Y2):
        y[TOK:, :] = jnp.zeros((y.shape[0] - TOK, D), F32)
    nodes_in.wait()
    for s in range(SEGS):
        x = R.nodes_v[pl.ds(st[s], BLK), :]
        Ls[0]["H"][s * BLK : (s + 1) * BLK, :] = x
        x = pack(x)
        Ls[0]["X"][s * BLK : (s + 1) * BLK, :] = x
        R.XT[:, s * BLK : (s + 1) * BLK] = x.T
    cot_in.wait()
    sum_e = zero8 = jnp.zeros((8, D), F32)
    for s in range(SEGS):
        x = jnp.where(live(s * BLK, BLK), R.cot_v[pl.ds(st[s], BLK), :], 0.0)
        Tm["E"][s * BLK : (s + 1) * BLK, :] = x
        Tm["ED"][s * BLK : (s + 1) * BLK, :] = pack(x)
        sum_e = sum_e + part(x)

    send_weights(0, "up", "dn")
    relay_first("k", "v")
    send_weights(1, "k", "v", "vec")
    relay_first("vec", "q", "o")
    send_weights(1, "q", "o")
    vecs = [None, None]

    def take_vecs(level):
        x = R.vec_own[level]
        for k in range(1, n_zero):
            x = x + R.vec_in[level, zpeer[k]]
        R.vec[level] = x
        vecs[level] = R.vec.at[level]

    tiles = [(s, s * BLK) for s in range(SEGS)]

    def pipe(stages):
        kept = [None] * len(tiles)
        for t in range(len(tiles) + len(stages) - 1):
            for j, stage in enumerate(stages):
                if 0 <= t - j < len(tiles):
                    kept[t - j] = stage(tiles[t - j], kept[t - j])
        return kept

    for level in range(2):
        L = Ls[level]
        w = {n: R.weights[n].at[level] for n in NAMES}
        if level == 0:
            take_first("k", "v", "vec")
        else:
            take_weights(1, "k", "v", "vec", "q", "o")
        take_vecs(level)
        vec = vecs[level]
        prep_kv(L, w, vec, R.A2)
        if level == 0:
            take_first("q", "o")
        prep_qo(L, w, vec)
        for s, r in tiles:
            fwd_a(L, vec, R.A2, live, r, BLK, level == 1)
        for s in range(SEGS):
            fwd_s1(L, gm, inv, s)
        t2 = [fwd_s2(L, s) for s in range(SEGS)]
        for s in range(SEGS):
            fwd_s3(L, vec, s, t2[s])
        take_weights(level, "up", "dn")
        if level == 0:
            send_weights(1, "up", "dn")
        prep_ff(L, w)

        def middle(tile, _):
            return fwd_c1(L, *tile, BLK)

        def hidden(tile, mid):
            fwd_c2(L, vec, tile[1], BLK)
            return mid

        def close(tile, mid):
            if level == 0:
                fwd_c3(L, vec, Ls[1]["H"], mid, tile[1], BLK)
            else:
                R.Y[pl.ds(tile[1], BLK), :] = mid

        pipe([middle, hidden, close])

    def put(level, name, g):
        grp, at = places[level, name]
        n = shard(name, n_zero)[0]
        for p in range(n_zero):
            part_p = g[p * n : (p + 1) * n]
            if name == "up":
                R.gsend[grp][p, at : at + n, :] = part_p[:, :D]
                R.gsend[grp][p, at + n : at + 2 * n, :] = part_p[:, D:]
            else:
                R.gsend[grp][p, at : at + n, :] = part_p

    def plane_copy(grp, k, who):
        rows, src = pieces[grp], R.gsend[grp].at[lax.rem(ppeer[k], n_zero)]
        if GROUPS[grp][1]:
            src = src.at[pl.ds(pl.multiple_of(ppeer[k] // n_zero * rows, 8), rows), :]
        return pltpu.make_async_remote_copy(
            src_ref=src,
            dst_ref=R.gplane[grp].at[who],
            send_sem=R.p_send.at[grp, k - 1],
            recv_sem=R.p_recv.at[grp, k - 1],
            device_id=in_plane(k),
            device_id_type=MESH,
        )

    def slow_copy(grp, k, who):
        return pltpu.make_async_remote_copy(
            src_ref=R.gslow[grp].at[slow],
            dst_ref=R.gslow[grp].at[who],
            send_sem=R.s_send.at[grp, k - 1],
            recv_sem=R.s_recv.at[grp, k - 1],
            device_id=along(k),
            device_id_type=MESH,
        )

    dpeer = [None] + [lax.rem(dp + k, n_dp) for k in range(1, n_dp)]
    dfrom = [None] + [lax.rem(dp + n_dp - k, n_dp) for k in range(1, n_dp)]

    def dp_copy(grp, k, who):
        return pltpu.make_async_remote_copy(
            src_ref=R.gslow[grp].at[dp],
            dst_ref=R.gslow[grp].at[who],
            send_sem=R.s_send.at[grp, k - 1],
            recv_sem=R.s_recv.at[grp, k - 1],
            device_id=(dpeer[k], zero),
            device_id_type=MESH,
        )

    def half_of(grp, who):
        rows = pieces[grp]
        return R.fin_out[grp].at[pl.ds(pl.multiple_of(who * rows, 8), rows), :]

    def pair_copy(grp, who):
        return pltpu.make_async_remote_copy(
            src_ref=half_of(grp, fast),
            dst_ref=half_of(grp, who),
            send_sem=R.f_send.at[grp],
            recv_sem=R.f_recv.at[grp],
            device_id=(slow * PAIR + other, zero),
            device_id_type=MESH,
        )

    def start_plane(grp):
        for k in range(1, n_plane):
            plane_copy(grp, k, me).start()

    def start_slow(grp):
        rows = pieces[grp]
        at = pl.multiple_of(fast * rows, 8) if GROUPS[grp][1] else 0
        R.gplane[grp][me] = R.gsend[grp][zero, pl.ds(at, rows), :]
        for k in range(1, n_plane):
            plane_copy(grp, k, pfrom[k]).wait_recv()
        x = R.gplane[grp][0]
        for j in range(1, n_plane):
            x = x + R.gplane[grp][j]
        if GROUPS[grp][1] == 2:
            R.gslow[grp][dp] = x
            for k in range(1, n_dp):
                dp_copy(grp, k, dp).start()
        else:
            R.gslow[grp][slow] = x
            for k in range(1, n_slow):
                slow_copy(grp, k, slow).start()

    def start_pair(grp):
        if GROUPS[grp][1] == 2:
            for k in range(1, n_dp):
                dp_copy(grp, k, dfrom[k]).wait_recv()
            rows = pieces[grp]
            for f in range(PAIR):
                x = R.gslow[grp][f]
                for j in range(1, n_slow):
                    x = x + R.gslow[grp][j * PAIR + f]
                R.fin_out[grp][f * rows : (f + 1) * rows, :] = x
            return
        for k in range(1, n_slow):
            slow_copy(grp, k, sfrom[k]).wait_recv()
        x = R.gslow[grp][0]
        for j in range(1, n_slow):
            x = x + R.gslow[grp][j]
        if GROUPS[grp][1]:
            R.fin_out[grp][pl.ds(pl.multiple_of(fast * pieces[grp], 8), pieces[grp]), :] = x
            pair_copy(grp, fast).start()
        else:
            R.fin_out[grp][...] = x

    def end_pair(grp):
        if GROUPS[grp][1] == 1:
            pair_copy(grp, other).wait_recv()

    def hand_out_vectors():
        small = []
        for level in range(2):
            g, at = places[level, "small"]
            small.append(R.fin_out[g][at : at + SMALL, :])
        for (_, row), out in zip(VECS, R.vec_out):
            n = out.shape[1]
            x = jnp.concatenate([s[row : row + 1, :] for s in small], axis=0)
            if row == BU0:
                x1 = jnp.concatenate([s[row + 1 : row + 2, :] for s in small], axis=0)
                x = jnp.where(zero * n < D, x, x1)
            x = pltpu.roll(x, lax.rem(D - lax.rem(zero * n, D), D), axis=1)
            out[...] = x[:, :n]

    shift = [jnp.minimum(BLK * s - st[s], (BLK - 256) * s) for s in range(SEGS)]

    def unpack(Y, base):
        lo, hi = (0, 256, 512, 768), (512, 1024, 1536, 2048)
        step = 256
        for t0 in range(0, TOK, step):
            it = lax.broadcasted_iota(jnp.int32, (step, D), 0) + t0
            x = base[t0 : t0 + step, :]
            for s in range(SEGS):
                if t0 < hi[s] and t0 + step > lo[s]:
                    y = Y[pl.ds(t0 + shift[s], step), :]
                    x = jnp.where((it >= st[s]) & (it < st[s + 1]), y, x)
            base[t0 : t0 + step, :] = x

    for level in (1, 0):
        L, vec = Ls[level], vecs[level]
        w = {n: R.weights[n].at[level] for n in NAMES}
        prep_back(L, w)

        def feed(tile, _):
            return bwd_a1(L, Tm, tile[1], BLK)

        def after(tile, su):
            return su, bwd_a2(L, Tm, tile[1], BLK)

        sums = pipe([feed, after])
        su = sum((x[0] for x in sums), jnp.zeros((8, FF), F32))
        sc = [x[1] for x in sums]
        put(level, "dn", grad_down(L, Tm))
        put(level, "up", grad_up(L, Tm))
        if level == 0:
            start_plane(2)
            start_slow(0)
        hp = [bwd_s1(L, Tm, s, sc[s]) for s in range(SEGS)]
        for s in range(SEGS):
            bwd_s2(L, Tm, s, hp[s])
        gq, gbq, go = bwd_s4(L, Tm)
        put(level, "q", gq)
        put(level, "o", go)
        for s in range(SEGS):
            bwd_s3(L, Tm, gm, inv, s)
        start_plane(0 if level == 1 else 3)
        a1 = R.A2[0:D, :]
        ss = [zero8] * 6

        def key_value(i):
            for s, r in tiles:
                o = bwd_b(L, vec, Tm, R.A2, s, r, BLK, i)
                for j in range(3):
                    ss[3 * i + j] = ss[3 * i + j] + o[j]

        key_value(0)
        key_value(1)
        rows = [jnp.zeros((1, D), F32)] * SMALL
        rows[BQ], rows[BK], rows[BV] = gbq, one(center(ss[2], a1)), one(center(ss[5], a1))
        rows[BO] = one(sc[0] + sc[1] + sc[2] + sc[3])
        rows[SK], rows[GK], rows[SV], rows[GV] = one(ss[0]), one(ss[1]), one(ss[3]), one(ss[4])
        rows[BD] = one(sum_e)
        u = one(su)
        rows[BU0], rows[BU1] = u[:, :D], u[:, D:]
        small = jnp.concatenate(rows, axis=0)
        grp, at = places[level, "small"]
        for p in range(n_zero):
            R.gsend[grp][p, at : at + SMALL, :] = small
        if level == 1:
            gk, gv = grad_both(L, Tm)
            put(level, "k", center(gk, a1))
            put(level, "v", center(gv, a1))
            start_plane(1)
        else:
            gk, gv = grad_both(L, Tm)
            put(level, "k", center(gk, a1))
            put(level, "v", center(gv, a1))
            start_plane(4)
            start_slow(1)
        if level == 1:
            sum_e = zero8
            for s, r in tiles:
                sum_e = sum_e + bwd_x_next(L, Tm, s, r, BLK)
        else:
            for s, r in tiles:
                bwd_x(L, Tm, R.Y2, s, r, BLK)

    start_slow(2)
    start_slow(3)
    start_pair(0)
    start_pair(1)
    for s, r in tiles:
        fwd_c3(Ls[1], vecs[1], R.Y, R.Y[pl.ds(r, BLK), :], r, BLK)
    unpack(R.Y, R.nodes_v)
    store_out = pltpu.make_async_copy(R.nodes_v, R.out, R.io_sem.at[3])
    store_out.start()
    start_slow(4)
    start_pair(2)
    start_pair(3)
    unpack(R.Y2, R.cot_v)
    store_gx = pltpu.make_async_copy(R.cot_v, R.gx, R.io_sem.at[4])
    store_gx.start()
    start_pair(4)
    end_pair(0)
    end_pair(1)
    end_pair(2)
    end_pair(3)
    end_pair(4)
    hand_out_vectors()
    for name in NAMES + ("vec",):
        if name in ("up", "dn"):
            for k in range(1, n_zero):
                weight_copy(0, name, k, zero).wait_send()
        else:
            mate_copy(name, 0, zero).wait_send()
            for k in range(1, n_x):
                x_copy(name, k, zero).wait_send()
                mate_copy(name, k, xfrom[k]).wait_send()
        for k in range(1, n_zero):
            weight_copy(1, name, k, zero).wait_send()
    for g in range(NG):
        for k in range(1, n_plane):
            plane_copy(g, k, me).wait_send()
        if GROUPS[g][1] == 2:
            for k in range(1, n_dp):
                dp_copy(g, k, dp).wait_send()
            continue
        for k in range(1, n_slow):
            slow_copy(g, k, slow).wait_send()
        if GROUPS[g][1]:
            pair_copy(g, fast).wait_send()
    store_out.wait()
    store_gx.wait()


def finish_kernel(n_zero, out, gx, fin, vec, outs, sem):
    places, _, _ = group_layout(n_zero)
    copies = []

    def copy(src, dst):
        c = pltpu.make_async_copy(src, dst, sem.at[len(copies)])
        c.start()
        copies.append(c)

    half = TOK // 2
    for i in range(2):
        copy(out.at[pl.ds(i * half, half), :], outs[0].at[pl.ds(i * half, half), :])
        copy(gx.at[pl.ds(i * half, half), :], outs[1].at[pl.ds(i * half, half), :])
    for name, arg in ARG.items():
        for level in range(2):
            g, at = places[level, name]
            n = shard(name, n_zero)[0]
            if name == "up":
                for h in range(2):
                    copy(
                        fin[g].at[pl.ds(at + h * n, n), :],
                        outs[2 + arg].at[level, :, pl.ds(h * D, D)],
                    )
            else:
                copy(fin[g].at[pl.ds(at, n), :], outs[2 + arg].at[level])
    for (arg, _), v in zip(VECS, vec):
        copy(v, outs[2 + arg])
    for c in copies:
        c.wait()


def make_fused(n_dp, n_zero, params):
    places, sizes, pieces = group_layout(n_zero)
    dma = pltpu.SemaphoreType.DMA
    any_ = pl.BlockSpec(memory_space=pl.ANY)
    order, scratch = [], []

    def add(name, shape):
        order.append(name)
        scratch.append(shape)

    n_params = len(params)
    out_shape = [VM((TOK, D), F32)] * 2 + [VM((p, D), F32) for p in sizes]
    out_shape += [VM(params[arg].shape, F32) for arg, _ in VECS]
    ls, ts = list(LAYER_SCRATCH), [n for n in TMP_SCRATCH if n != "A2"]
    for level in range(2):
        for n in ls:
            add(("layer", level, n), VM(*LAYER_SCRATCH[n]))
    for n in ts:
        add(("temp", n), VM(*TMP_SCRATCH[n]))
    add("lengths", pltpu.SMEM((SEGS,), jnp.int32))
    add("A2", VM(*TMP_SCRATCH["A2"]))
    add("Y", VM((TOK + 768, D), F32))
    add("XT", VM((2 * D, TOK), BF))
    add("Y2", VM((TOK + 768, D), F32))
    add("nodes_v", VM((TOK, D), F32))
    add("cot_v", VM((TOK, D), F32))
    for i, (arg, _) in enumerate(VECS):
        add(("stage", i), VM(params[arg].shape, F32))
    for n in NAMES:
        rows, cols = shard(n, n_zero)
        add(("weights", n), VM((2, rows * n_zero, cols), F32))
    add("vec_own", VM((2, SMALL, D), F32))
    add("vec_in", VM((2, n_zero, SMALL, D), F32))
    add("vec", VM((2, SMALL, D), F32))
    for g in range(NG):
        add(("gsend", g), VM((n_zero, sizes[g], D), F32))
        add(("gplane", g), VM((PAIR * n_zero, pieces[g], D), F32))
        add(("gslow", g), VM((n_dp, pieces[g], D), F32))
    add("stage_sem", dma((len(VECS),)))
    add("io_sem", dma((5,)))
    add("own_sem", dma((2, 6)))
    add("w_send", dma((14, n_zero - 1)))
    add("w_recv", dma((14, n_zero - 1)))
    for n, m in (("x", n_zero // 2 - 1), ("m", n_zero // 2)):
        add(n + "_send", dma((7, m)))
        add(n + "_recv", dma((7, m)))
    for n, m in (("p", PAIR * n_zero), ("s", n_dp)):
        add(n + "_send", dma((NG, m - 1)))
        add(n + "_recv", dma((NG, m - 1)))
    add("f_send", dma((NG,)))
    add("f_recv", dma((NG,)))

    def body(*refs):
        lengths_in, nodes, cot = refs[:3]
        pr = refs[3 : 3 + n_params]
        n_outs = 2 + NG + len(VECS)
        outs = refs[3 + n_params : 3 + n_outs + n_params]
        rest = refs[3 + n_outs + n_params :]
        simple = dict(lengths_in=lengths_in, nodes=nodes, cotangent=cot, params=pr, out=outs[0], gx=outs[1], fin_out=outs[2 : 2 + NG], vec_out=outs[2 + NG :])
        layers, temps = [{}, {}], {}
        simple.update(layers=layers, temps=temps, stage=[None] * len(VECS), weights={})
        for n in ("gsend", "gplane", "gslow"):
            simple[n] = [None] * NG
        for key, ref in zip(order, rest):
            if isinstance(key, str):
                simple[key] = ref
            elif key[0] == "layer":
                layers[key[1]][key[2]] = ref
            elif key[0] == "temp":
                temps[key[1]] = ref
            else:
                simple[key[0]][key[1]] = ref
        fused_kernel(n_dp, n_zero, list(simple), *simple.values())

    call = pl.pallas_call(
        body,
        out_shape=out_shape,
        in_specs=[any_] * (3 + n_params),
        out_specs=[any_] * 2 + [pl.BlockSpec(memory_space=pltpu.VMEM)] * (NG + len(VECS)),
        scratch_shapes=scratch,
        compiler_params=pltpu.CompilerParams(
            collective_id=0, has_side_effects=True, vmem_limit_bytes=56 * 1024 * 1024
        ),
    )
    return call


def make_finish(n_zero, params):
    any_ = pl.BlockSpec(memory_space=pl.ANY)
    out_shape = [jax.ShapeDtypeStruct((TOK, D), F32)] * 2
    out_shape += [jax.ShapeDtypeStruct(p.shape, F32) for p in params]
    n_ins = 2 + NG + len(VECS)

    def body(*refs):
        out, gx = refs[:2]
        fin, vec = refs[2 : 2 + NG], refs[2 + NG : n_ins]
        finish_kernel(n_zero, out, gx, fin, vec, refs[n_ins:-1], refs[-1])

    call = pl.pallas_call(
        body,
        out_shape=out_shape,
        in_specs=[any_] * n_ins,
        out_specs=[any_] * len(out_shape),
        scratch_shapes=[pltpu.SemaphoreType.DMA((28,))],
    )
    return lambda *xs: call(*[pltpu.with_memory_space_constraint(x, pltpu.VMEM) for x in xs])


def solution(mesh):
    n_dp, n_zero = mesh.shape["dp"], mesh.shape["zero"]
    wide, flat = P(None, "zero", None), P(None, "zero")
    params = (wide,) * 4 + (flat,) * 8 + (wide, flat, wide, flat)
    rows = P(("dp", "zero"), None)

    def local(nodes, cotangent, lengths, *params):
        results = make_fused(n_dp, n_zero, params)(lengths, nodes, cotangent, *params)
        return tuple(make_finish(n_zero, params)(*results))

    return jax.shard_map(
        local,
        mesh=mesh,
        in_specs=(rows, rows, P(("dp", "zero"))) + params,
        out_specs=(rows, rows) + params,
        check_vma=False,
    )
```
